32 devices in a mesh: shots: 2 (over y), bfly: 4 (over z), sub: 2 (over x), tr: 2 (over core).
Axes of the slice: x: 2, y: 2, z: 4, core: 2. Of those that a mesh axis runs over, the one named last changes fastest.
Arguments:
- traces: bfloat16 [16384, 1024], P(('shots', 'tr'), ('bfly', 'sub')), parts along dimension 0, may hold values from -6 to 6
- sampling: bfloat16 [8, 128, 128], P(('bfly', 'sub')), may hold values from -0.5 to 0.5
- skeleton: int32 [8, 3, 64], P(('bfly', 'sub')), may hold values from 0 to 127, as said below
- compress: bfloat16 [8, 3, 64, 128], P(('bfly', 'sub'))
- evaluation: bfloat16 [8, 128, 128], P(('bfly', 'sub')), may hold values from -0.5 to 0.5
Outputs:
- migrated: bfloat16 [16384, 1024], P(('shots', 'tr'), ('bfly', 'sub')), parts along dimension 0
The draws below stay inside these ranges and needn't reach their ends.
There are 2 independent parts, one for each index of `shots`. The reference program is written for one: setup_inputs(seed, part) draws one part's arguments, and reference() takes and returns one part's arrays. A program takes and returns all parts, laid end to end along the dimension named above; an argument that names none is the same for every part. Nothing has to cross between parts.
Inputs may be any that keep to these rules, and one draw needn't show every extreme that they name: The 64 entries of skeleton[b, s, :] are distinct; an entry below 64 picks a coefficient of box b, one of 64 or more a coefficient of its partner.
All inputs are finite; a program needn't handle non-finite values.
Results may differ from the reference program's by a relative error of at most 0.007.
Values may be sent and summed in bfloat16 or wider, within the bound.
No kernel may reach another device: no remote copies, remote signals or barrier semaphores. Data moves between devices by JAX's collectives and lax.ppermute only.
A program may use at most 64 MiB of HBM per device.

```python
import math
import jax
import jax.numpy as jnp
from jax import lax

R = 64
PTS = 128
LEVELS = 3
BOXES = 8
TRACES = 8192


def one_row(row_key):
    return jax.random.permutation(row_key, 2 * R)[:R]


def draw_skeleton(key, part):
    key = jax.random.fold_in(key, 11)
    row_keys = jax.random.split(key, BOXES * LEVELS)
    picked = jax.vmap(one_row)(row_keys)
    return picked.reshape(BOXES, LEVELS, R).astype(jnp.int32)


def draw_compress(key, part):
    key = jax.random.fold_in(key, 23)
    noise_key = jax.random.fold_in(key, 0)
    identity = jnp.eye(R, dtype=jnp.float32)
    noise = 0.4 / math.sqrt(R) * jax.random.normal(noise_key, (BOXES, LEVELS, R, 2 * R), jnp.float32)
    diagonal = 0.8 * jnp.ones((BOXES, LEVELS, R, 1), jnp.float32)
    real_part = diagonal * identity + noise[..., :R]
    return jnp.concatenate([real_part, noise[..., R:]], -1).astype(jnp.bfloat16)


def steps_of(stream_key, shape, shards, least, high):
    gain = 1.0
    for axis_at, parts in shards:
        draws = jax.random.uniform(jax.random.fold_in(jax.random.fold_in(stream_key, 6), axis_at), (parts,), jnp.float32, least / len(shards), high / len(shards))
        gain = gain * jnp.repeat(jnp.exp(draws), shape[axis_at] // parts).reshape((-1,) + (1,) * (len(shape) - 1 - axis_at))
    return gain


def centred(key, extent, deviation, bound, cuts=(), held_as=jnp.bfloat16):
    array = deviation * jax.random.normal(key, extent, jnp.float32)
    if cuts:
        array = array * steps_of(key, extent, cuts, -0.22, 0.18)
    return jnp.clip(array, -bound, bound).astype(held_as)


def setup_inputs(seed: int = 0, part: int = 0) -> dict:
    splits = jax.random.split(jax.random.key(seed), 6)
    part_splits = jax.random.split(jax.random.fold_in(splits[5], part), 6)
    traces = centred(part_splits[0], (TRACES, BOXES * PTS), 1.0, 6.0, ((0, 2), (1, 8)))
    sampling = centred(splits[1], (BOXES, PTS, 2 * R), PTS ** -0.5, 0.5, ((0, 8),))
    skeleton = draw_skeleton(jax.random.fold_in(splits[5], 71), part)
    compress = draw_compress(jax.random.fold_in(splits[5], 71), part)
    evaluation = centred(splits[4], (BOXES, 2 * R, PTS), (2 * R) ** -0.5, 0.5, ((0, 8),))
    return {"traces": traces, "sampling": sampling, "skeleton": skeleton, "compress": compress, "evaluation": evaluation}


def compress_box(packed):
    own_coeffs, partner, picked, matrix = packed
    rank_size = picked.shape[0]
    real_full = jnp.concatenate([own_coeffs[:, :rank_size], partner[:, :rank_size]], 1).astype(jnp.float32)
    imag_full = jnp.concatenate([own_coeffs[:, rank_size:], partner[:, rank_size:]], 1).astype(jnp.float32)
    pick_real = jnp.take(real_full, picked, axis=1)
    pick_imag = jnp.take(imag_full, picked, axis=1)
    mat_real = matrix[:, :rank_size].astype(jnp.float32).T
    mat_imag = matrix[:, rank_size:].astype(jnp.float32).T
    new_real = jnp.dot(pick_real, mat_real, preferred_element_type=jnp.float32) - jnp.dot(pick_imag, mat_imag, preferred_element_type=jnp.float32)
    new_imag = jnp.dot(pick_real, mat_imag, preferred_element_type=jnp.float32) + jnp.dot(pick_imag, mat_real, preferred_element_type=jnp.float32)
    return jnp.concatenate([new_real, new_imag], 1).astype(jnp.bfloat16)


def reference(traces, sampling, skeleton, compress, evaluation):
    box_count = sampling.shape[0]
    trace_rows = traces.shape[0]
    coeff_width = sampling.shape[2]
    blocks = traces.reshape(trace_rows, box_count, PTS).transpose(1, 0, 2)
    coeffs = jnp.einsum('btp,bpc->btc', blocks.astype(jnp.float32), sampling.astype(jnp.float32)).astype(jnp.bfloat16)
    for level_index in range(LEVELS):
        stride = 2 ** level_index
        grouped = coeffs.reshape(box_count // (2 * stride), 2, stride, trace_rows, coeff_width)
        partner = grouped[:, ::-1].reshape(box_count, trace_rows, coeff_width)
        coeffs = lax.map(compress_box, (coeffs, partner, skeleton[:, level_index], compress[:, level_index]))
    migrated = jnp.einsum('btc,bcp->btp', coeffs.astype(jnp.float32), evaluation.astype(jnp.float32)).astype(jnp.bfloat16)
    return migrated.transpose(1, 0, 2).reshape(trace_rows, box_count * PTS)
```

```python
import jax
import jax.numpy as jnp
from jax import lax
from jax.sharding import PartitionSpec as P

PIECES = 4


def from_partner(block, axis, apart):
    count = lax.axis_size(axis)
    route = []
    for low in range(count):
        high = low | 1 << apart
        if high != low and high < count:
            route += [(low, high), (high, low)]
    return lax.ppermute(block, axis, route)


def level_matrices(compress, skeleton):
    rank = skeleton.shape[-1]
    places = lax.broadcasted_iota(jnp.int32, (1, 2 * rank, 1), 1)
    chooser = (skeleton[:, None, :] == places).astype(jnp.bfloat16)
    both = jnp.einsum(
        "lik,ljk->lij",
        chooser,
        jnp.concatenate([compress[:, :, :rank], compress[:, :, rank:]], 1),
        preferred_element_type=jnp.float32,
    ).astype(jnp.bfloat16)
    real, imag = both[..., :rank], both[..., rank:]
    turned = jnp.concatenate([-imag, real], -1)
    return jnp.concatenate(
        [both[:, :rank], turned[:, :rank], both[:, rank:], turned[:, rank:]], 1
    )


def advance(coeffs, partner, matrix):
    joined = jnp.concatenate([coeffs, partner], -1)
    return jnp.dot(joined, matrix, preferred_element_type=jnp.float32).astype(jnp.bfloat16)


def local(traces, sampling, skeleton, compress, evaluation):
    low_bits = lax.axis_size("sub").bit_length() - 1
    high_bits = lax.axis_size("bfly").bit_length() - 1
    hops = [("sub", bit) for bit in range(low_bits)] + [("bfly", bit) for bit in range(high_bits)]
    matrices = level_matrices(compress[0], skeleton[0])
    rows = traces.shape[0] // PIECES
    coeffs = {}
    done = [None] * PIECES
    for step in range(PIECES + len(hops)):
        for level in range(len(hops), -1, -1):
            piece = step - level
            if not 0 <= piece < PIECES:
                continue
            if level == 0:
                block = traces[piece * rows : (piece + 1) * rows]
                coeffs[piece] = jnp.dot(
                    block, sampling[0], preferred_element_type=jnp.float32
                ).astype(jnp.bfloat16)
            if level < len(hops):
                axis, bit = hops[level]
                partner = from_partner(coeffs[piece], axis, bit)
                coeffs[piece] = advance(coeffs[piece], partner, matrices[level])
            else:
                done[piece] = jnp.dot(
                    coeffs[piece], evaluation[0], preferred_element_type=jnp.float32
                ).astype(jnp.bfloat16)
    return jnp.concatenate(done, 0)


def solution(mesh):
    placed = (
        P(("shots", "tr"), ("bfly", "sub")),
        P(("bfly", "sub"), None, None),
        P(("bfly", "sub"), None, None),
        P(("bfly", "sub"), None, None, None),
        P(("bfly", "sub"), None, None),
    )
    return jax.shard_map(
        local,
        mesh=mesh,
        in_specs=placed,
        out_specs=P(("shots", "tr"), ("bfly", "sub")),
        check_vma=False,
    )
```

```python
import jax
import jax.numpy as jnp
from jax import lax
from jax.sharding import PartitionSpec as P

SIXTEENTHS = (1, 3, 4, 4, 4)


def from_partner(block, axis, apart):
    count = lax.axis_size(axis)
    route = []
    for low in range(count):
        high = low | 1 << apart
        if high != low and high < count:
            route += [(low, high), (high, low)]
    return lax.ppermute(block, axis, route)


def level_matrices(compress, skeleton):
    rank = skeleton.shape[-1]
    places = lax.broadcasted_iota(jnp.int32, (1, 2 * rank, 1), 1)
    chooser = (skeleton[:, None, :] == places).astype(jnp.bfloat16)
    both = jnp.einsum(
        "lik,ljk->lij",
        chooser,
        jnp.concatenate([compress[:, :, :rank], compress[:, :, rank:]], 1),
        preferred_element_type=jnp.float32,
    ).astype(jnp.bfloat16)
    real, imag = both[..., :rank], both[..., rank:]
    turned = jnp.concatenate([-imag, real], -1)
    return jnp.concatenate(
        [both[:, :rank], turned[:, :rank], both[:, rank:], turned[:, rank:]], 1
    )


def advance(coeffs, partner, matrix):
    joined = jnp.concatenate([coeffs, partner], -1)
    return jnp.dot(joined, matrix, preferred_element_type=jnp.float32).astype(jnp.bfloat16)


def local(traces, sampling, skeleton, compress, evaluation):
    low_bits = lax.axis_size("sub").bit_length() - 1
    high_bits = lax.axis_size("bfly").bit_length() - 1
    hops = [("sub", bit) for bit in range(low_bits)] + [("bfly", bit) for bit in range(high_bits)]
    matrices = level_matrices(compress[0], skeleton[0])
    unit = traces.shape[0] // sum(SIXTEENTHS)
    pieces = len(SIXTEENTHS)
    starts = [unit * sum(SIXTEENTHS[:i]) for i in range(pieces + 1)]
    coeffs, partners, done = {}, {}, [None] * pieces
    last_sent = None
    for step in range(pieces + len(hops)):
        for level in range(len(hops) + 1):
            piece = step - level
            if not 0 <= piece < pieces:
                continue
            if level == 0:
                block = traces[starts[piece] : starts[piece + 1]]
                value = jnp.dot(
                    block, sampling[0], preferred_element_type=jnp.float32
                ).astype(jnp.bfloat16)
            else:
                arrived = partners[piece]
                if last_sent is not None:
                    arrived, _ = lax.optimization_barrier((arrived, last_sent))
                value = advance(coeffs[piece], arrived, matrices[level - 1])
            if level < len(hops):
                axis, bit = hops[level]
                coeffs[piece] = value
                partners[piece] = from_partner(value, axis, bit)
                if level > 0:
                    last_sent = value
            else:
                done[piece] = jnp.dot(
                    value, evaluation[0], preferred_element_type=jnp.float32
                ).astype(jnp.bfloat16)
    return jnp.concatenate(done, 0)


def solution(mesh):
    placed = (
        P(("shots", "tr"), ("bfly", "sub")),
        P(("bfly", "sub"), None, None),
        P(("bfly", "sub"), None, None),
        P(("bfly", "sub"), None, None, None),
        P(("bfly", "sub"), None, None),
    )
    return jax.shard_map(
        local,
        mesh=mesh,
        in_specs=placed,
        out_specs=P(("shots", "tr"), ("bfly", "sub")),
        check_vma=False,
    )
```

```python
import jax
import jax.numpy as jnp
from jax import lax
from jax.sharding import PartitionSpec as P

SIXTEENTHS = (1, 3, 4, 4, 4)
FIRST_COMPACT = 1
ROOM_EIGHTHS = 5


def route(axis, apart):
    count = lax.axis_size(axis)
    pairs = []
    for low in range(count):
        high = low | 1 << apart
        if high != low and high < count:
            pairs += [(low, high), (high, low)]
    return pairs


def from_partner(block, hop):
    return lax.ppermute(block, hop[0], route(*hop))


def real_form(both):
    rank = both.shape[-1] // 2
    turned = jnp.concatenate([-both[..., rank:], both[..., :rank]], -1)
    return jnp.concatenate([both, turned], -2)


def picked_rows(compress, skeleton):
    rank = skeleton.shape[-1]
    places = lax.broadcasted_iota(jnp.int32, (1, 2 * rank, 1), 1)
    chooser = (skeleton[:, None, :] == places).astype(jnp.bfloat16)
    stacked = jnp.concatenate([compress[:, :, :rank], compress[:, :, rank:]], 1)
    return jnp.einsum(
        "lik,ljk->lij", chooser, stacked, preferred_element_type=jnp.float32
    ).astype(jnp.bfloat16)


def slots(skeleton, room):
    rank = skeleton.shape[-1]
    places = rank + lax.broadcasted_iota(jnp.int32, (1, rank, 1), 1)
    picked = jnp.any(skeleton[:, None, :] == places, -1)
    before = lax.broadcasted_iota(jnp.int32, (rank, rank), 0) > lax.broadcasted_iota(
        jnp.int32, (rank, rank), 1
    )
    slot = jnp.sum(before[None] & picked[:, None, :], -1, dtype=jnp.int32)
    index = lax.broadcasted_iota(jnp.int32, (1, 1, room), 2)
    return (picked[..., None] & (slot[..., None] == index)).astype(jnp.bfloat16)


def compact_columns(matrix, slot):
    rank = slot.shape[1]
    parts = [
        jnp.einsum("lnr,lrj->lnj", half, slot, preferred_element_type=jnp.float32)
        for half in (matrix[..., :rank], matrix[..., rank:])
    ]
    return jnp.concatenate(parts, -1).astype(jnp.bfloat16)


def times(value, matrix):
    return jnp.dot(value, matrix, preferred_element_type=jnp.float32).astype(jnp.bfloat16)


def all_hops():
    low_bits = lax.axis_size("sub").bit_length() - 1
    high_bits = lax.axis_size("bfly").bit_length() - 1
    return [("sub", bit) for bit in range(low_bits)] + [("bfly", bit) for bit in range(high_bits)]


def full_width(traces, sampling, own_full, evaluation):
    coeffs = times(traces, sampling)
    for level, hop in enumerate(all_hops()):
        partner = from_partner(coeffs, hop)
        coeffs = times(jnp.concatenate([coeffs, partner], -1), own_full[level])
    return times(coeffs, evaluation)


def local(traces, sampling, skeleton, compress, evaluation):
    sampling, skeleton, compress, evaluation = sampling[0], skeleton[0], compress[0], evaluation[0]
    hops = all_hops()
    levels = len(hops)
    rank = skeleton.shape[-1]
    room = rank * ROOM_EIGHTHS // 8

    everyone = lax.all_gather(skeleton, ("bfly", "sub"))
    too_many = jnp.any(jnp.sum(everyone >= rank, -1) > room)
    box = lax.axis_index("bfly") * lax.axis_size("sub") + lax.axis_index("sub")
    partner_skeleton = jnp.stack([everyone[box ^ (1 << s), s] for s in range(levels)])

    rows = picked_rows(compress, skeleton)
    full = jnp.concatenate([real_form(rows[:, :rank]), real_form(rows[:, rank:])], 1)
    kept = jnp.einsum(
        "lrj,lrc->ljc", slots(skeleton, room), rows[:, rank:], preferred_element_type=jnp.float32
    ).astype(jnp.bfloat16)
    small = jnp.concatenate([real_form(rows[:, :rank]), real_form(kept)], 1)
    theirs = slots(partner_skeleton, room)
    sent_sampling = compact_columns(sampling[None], theirs[:1])[0]
    sent_full = compact_columns(full[:-1], theirs[1:])
    sent_small = compact_columns(small[:-1], theirs[1:])

    def is_compact(level, piece):
        return piece >= FIRST_COMPACT and level >= 0 and (level > 0 or piece > FIRST_COMPACT)

    unit = traces.shape[0] // sum(SIXTEENTHS)
    pieces = len(SIXTEENTHS)
    starts = [unit * sum(SIXTEENTHS[:i]) for i in range(pieces + 1)]
    inputs, partners, done = {}, {}, [None] * pieces
    last_sent = None
    for step in range(pieces + levels):
        for level in range(levels + 1):
            piece = step - level
            if not 0 <= piece < pieces:
                continue
            if level == 0:
                value = traces[starts[piece] : starts[piece + 1]]
                if piece >= 2:
                    value, _ = lax.optimization_barrier((value, last_sent))
                matrix, sending = sampling, sent_sampling
            else:
                arrived = partners[piece]
                if last_sent is not None:
                    arrived, _ = lax.optimization_barrier((arrived, last_sent))
                value = jnp.concatenate([inputs[piece], arrived], -1)
                if is_compact(level - 1, piece):
                    matrix = small[level - 1]
                    sending = sent_small[level - 1] if level < levels else None
                else:
                    matrix = full[level - 1]
                    sending = sent_full[level - 1] if level < levels else None
            own = times(value, matrix)
            if level < levels:
                outgoing = times(value, sending) if is_compact(level, piece) else own
                inputs[piece] = own
                partners[piece] = from_partner(outgoing, hops[level])
                if level > 0:
                    last_sent = outgoing
            else:
                done[piece] = times(own, evaluation)
    quick = jnp.concatenate(done, 0)
    return lax.cond(
        too_many,
        lambda: full_width(traces, sampling, full, evaluation),
        lambda: quick,
    )


def solution(mesh):
    placed = (
        P(("shots", "tr"), ("bfly", "sub")),
        P(("bfly", "sub"), None, None),
        P(("bfly", "sub"), None, None),
        P(("bfly", "sub"), None, None, None),
        P(("bfly", "sub"), None, None),
    )
    return jax.shard_map(
        local,
        mesh=mesh,
        in_specs=placed,
        out_specs=P(("shots", "tr"), ("bfly", "sub")),
        check_vma=False,
    )
```

```python
import jax
import jax.numpy as jnp
from jax import lax
from jax.sharding import PartitionSpec as P

SIXTEENTHS = (1, 3, 4, 4, 4)
COUNT_PIECE = 2
ROOM_SIXTEENTHS = 12
EXTRA = 128


def route(axis, apart):
    count = lax.axis_size(axis)
    pairs = []
    for low in range(count):
        high = low | 1 << apart
        if high != low and high < count:
            pairs += [(low, high), (high, low)]
    return pairs


def from_partner(block, hop):
    return lax.ppermute(block, hop[0], route(*hop))


def real_form(both):
    rank = both.shape[1] // 2
    turned = jnp.concatenate([-both[:, rank:], both[:, :rank]], 1)
    return jnp.concatenate([both, turned], 2)


def picked_columns(compress, skeleton):
    rank = skeleton.shape[-1]
    places = lax.broadcasted_iota(jnp.int32, (1, 1, 2 * rank), 2)
    chooser = (skeleton[:, :, None] == places).astype(jnp.bfloat16)
    stacked = jnp.concatenate([compress[:, :, :rank], compress[:, :, rank:]], 1)
    return jnp.einsum(
        "ljk,lki->lji", stacked, chooser, preferred_element_type=jnp.float32
    ).astype(jnp.bfloat16)


def slots(skeleton, room):
    rank = skeleton.shape[-1]
    places = rank + lax.broadcasted_iota(jnp.int32, (1, 1, rank), 2)
    picked = jnp.any(skeleton[:, :, None] == places, 1)
    before = lax.broadcasted_iota(jnp.int32, (rank, rank), 0) < lax.broadcasted_iota(
        jnp.int32, (rank, rank), 1
    )
    slot = jnp.sum(before[None] & picked[:, :, None], 1, dtype=jnp.int32)
    index = lax.broadcasted_iota(jnp.int32, (1, room, 1), 1)
    return (picked[:, None] & (slot[:, None] == index)).astype(jnp.bfloat16)


def compact_rows(matrix, slot):
    rank = slot.shape[1]
    parts = [
        jnp.dot(slot, half, preferred_element_type=jnp.float32)
        for half in (matrix[:rank], matrix[rank:])
    ]
    return jnp.concatenate(parts, 0).astype(jnp.bfloat16)


def times(matrix, value):
    return jnp.dot(matrix, value, preferred_element_type=jnp.float32).astype(jnp.bfloat16)


def sampled(sampling, traces):
    return jnp.einsum(
        "pc,tp->ct", sampling, traces, preferred_element_type=jnp.float32
    ).astype(jnp.bfloat16)


def evaluated(coeffs, evaluation):
    return jnp.einsum(
        "ct,cp->tp", coeffs, evaluation, preferred_element_type=jnp.float32
    ).astype(jnp.bfloat16)


def after(value, earlier):
    return value if earlier is None else lax.optimization_barrier((value, earlier))[0]


def all_hops():
    low_bits = lax.axis_size("sub").bit_length() - 1
    high_bits = lax.axis_size("bfly").bit_length() - 1
    return [("sub", bit) for bit in range(low_bits)] + [("bfly", bit) for bit in range(high_bits)]


def full_width(traces, sampling, full, evaluation):
    coeffs = sampled(sampling, traces)
    for level, hop in enumerate(all_hops()):
        partner = from_partner(coeffs, hop)
        coeffs = times(full[level], jnp.concatenate([coeffs, partner], 0))
    return evaluated(coeffs, evaluation)


def sequence(pieces, levels):
    def turn(at):
        level, piece = at
        if level == 0:
            return max(0, 2 * piece - 1)
        return 2 * (level + piece + (piece > 0))

    return sorted(
        [(level, piece) for level in range(levels + 1) for piece in range(pieces)],
        key=lambda at: (turn(at), at),
    )


def local(traces, sampling, skeleton, compress, evaluation):
    sampling, skeleton, compress, evaluation = sampling[0], skeleton[0], compress[0], evaluation[0]
    hops = all_hops()
    levels = len(hops)
    wide = lax.axis_size("sub").bit_length() - 1
    rank = skeleton.shape[-1]
    room = rank * ROOM_SIXTEENTHS // 16

    columns = picked_columns(compress, skeleton)
    slot = slots(skeleton, room)
    full = jnp.concatenate([real_form(columns[..., :rank]), real_form(columns[..., rank:])], 2)
    kept = jnp.einsum(
        "lcr,ljr->lcj", columns[..., rank:], slot, preferred_element_type=jnp.float32
    ).astype(jnp.bfloat16)
    small = jnp.concatenate([real_form(columns[..., :rank]), real_form(kept)], 2)
    small = jnp.pad(small, ((0, 0), (0, 0), (0, full.shape[2] - small.shape[2])))
    most = jnp.max(jnp.sum(skeleton[wide:] >= rank, -1)).astype(jnp.bfloat16)

    def compact(level, piece):
        return piece > 0 and level >= wide

    unit = traces.shape[0] // sum(SIXTEENTHS)
    pieces = len(SIXTEENTHS)
    starts = [unit * sum(SIXTEENTHS[:i]) for i in range(pieces + 1)]
    inputs, partners, theirs, done = {}, {}, {}, [None] * pieces
    previous = None
    for level, piece in sequence(pieces, levels):
        count = starts[piece + 1] - starts[piece]
        if level == 0:
            block = traces[starts[piece] : starts[piece + 1]]
            if piece > 1:
                block = after(block, previous)
            own = sampled(sampling, block)
        else:
            arrived = after(partners[piece], previous)
            if piece == 0 and level - 1 >= wide:
                theirs[level - 1] = arrived[:room, count : count + rank]
            if piece == COUNT_PIECE:
                most = jnp.maximum(most, arrived[0, count])
            value = jnp.concatenate([inputs[piece], arrived[:, :count]], 0)
            matrix = full[level - 1]
            if compact(level - 1, piece):
                value = jnp.pad(value, ((0, full.shape[2] - value.shape[0]), (0, 0)))
                matrix = small[level - 1]
            own = times(matrix, value)
        if level == levels:
            done[piece] = evaluated(own, evaluation)
            continue
        outgoing = own
        if compact(level, piece):
            outgoing = times(compact_rows(matrix, theirs[level]), value)
        if piece == 0 and level >= wide:
            extra = jnp.pad(slot[level], ((0, 2 * rank - room), (0, EXTRA - rank)))
            outgoing = jnp.concatenate([outgoing, extra], 1)
        if piece == COUNT_PIECE:
            extra = jnp.broadcast_to(most, (outgoing.shape[0], EXTRA))
            outgoing = jnp.concatenate([outgoing, extra], 1)
        inputs[piece] = own
        partners[piece] = from_partner(outgoing, hops[level])
        previous = outgoing
    quick = jnp.concatenate(done, 0)
    return lax.cond(
        most > room,
        lambda: full_width(traces, sampling, full, evaluation),
        lambda: quick,
    )


def solution(mesh):
    placed = (
        P(("shots", "tr"), ("bfly", "sub")),
        P(("bfly", "sub"), None, None),
        P(("bfly", "sub"), None, None),
        P(("bfly", "sub"), None, None, None),
        P(("bfly", "sub"), None, None),
    )
    return jax.shard_map(
        local,
        mesh=mesh,
        in_specs=placed,
        out_specs=P(("shots", "tr"), ("bfly", "sub")),
        check_vma=False,
    )
```

```python
import jax
import jax.numpy as jnp
from jax import lax
from jax.experimental import pallas as pl
from jax.experimental.pallas import tpu as pltpu
from jax.sharding import PartitionSpec as P

SIXTEENTHS = (1, 3, 4, 4, 4)
ROOM_SIXTEENTHS = 12


def route(axis, apart):
    count = lax.axis_size(axis)
    pairs = []
    for low in range(count):
        high = low | 1 << apart
        if high != low and high < count:
            pairs += [(low, high), (high, low)]
    return pairs


def from_partner(block, hop):
    return lax.ppermute(block, hop[0], route(*hop))


def across(left, right):
    return lax.dot_general(left, right, (((1,), (1,)), ((), ())), preferred_element_type=jnp.float32)


def one_hot(condition):
    return jnp.where(condition, 1.0, 0.0).astype(jnp.bfloat16)


def tables_kernel(wide, room, skeleton_ref, compress_ref, full_ref, small_ref, extra_ref):
    levels, rank = skeleton_ref.shape[1:]
    width = 2 * rank
    f32, i32 = jnp.float32, jnp.int32
    k = lax.broadcasted_iota(i32, (width, width), 1)
    twice = one_hot(lax.broadcasted_iota(i32, (width, rank), 0) % rank == lax.broadcasted_iota(i32, (width, rank), 1))
    earlier = one_hot(
        (lax.broadcasted_iota(i32, (width, width), 1) < lax.broadcasted_iota(i32, (width, width), 0) % rank)
    )
    column = lax.broadcasted_iota(i32, (2 * width, width), 0)
    is_real_entry = lax.broadcasted_iota(i32, (2 * width, width), 1) < rank
    partner_column = column >= width
    imag_column = column % width >= rank
    coefficient = column % rank + jnp.where(partner_column, rank, 0)
    slot_column = column - width
    slot_imag = slot_column >= room
    slot_of_column = jnp.where(slot_imag, slot_column - room, slot_column)
    row = lax.broadcasted_iota(i32, (width, width), 0)
    most = jnp.zeros((1, 1), f32)
    for level in range(levels):
        entry = jnp.broadcast_to(skeleton_ref[0, level : level + 1].astype(f32), (8, rank)).astype(jnp.bfloat16)
        entry = across(entry, twice)[:1]
        picked = jnp.where(entry >= rank, 1.0, 0.0)
        slot = across(jnp.broadcast_to(picked, (8, width)).astype(jnp.bfloat16), earlier)[:1].astype(i32)
        entry = entry.astype(i32)
        from_partner_entry = entry >= rank
        matrix = compress_ref[0, level]

        def halves(match, imag):
            same = is_real_entry != imag
            real = jnp.where(match & same, jnp.where(imag, -1.0, 1.0), 0.0).astype(jnp.bfloat16)
            turned = one_hot(match & jnp.logical_not(same))
            return across(matrix, real).astype(jnp.bfloat16), across(matrix, turned).astype(jnp.bfloat16)

        match = entry == coefficient
        full_ref[level, :rank], full_ref[level, rank:] = halves(match, imag_column)
        compacted = (slot == slot_of_column) & from_partner_entry
        match = (match & jnp.logical_not(partner_column)) | (compacted & partner_column)
        imag = (imag_column & jnp.logical_not(partner_column)) | (slot_imag & partner_column)
        small_ref[level, :rank], small_ref[level, rank:] = halves(match, imag)
        once = (k < rank) & from_partner_entry
        places = across(one_hot(once & (slot == row)), one_hot(once & (entry - rank == row)))
        extra_ref[level] = places.astype(jnp.bfloat16)
        if level >= wide:
            most = jnp.maximum(most, jnp.sum(picked, axis=1, keepdims=True) * 0.5)
    for level in range(wide, levels):
        extra_ref[level] = jnp.where(k < rank, extra_ref[level].astype(f32), most).astype(jnp.bfloat16)


def tables(skeleton, compress, wide, room):
    levels, rank = skeleton.shape[1:]
    shape = (levels, 2 * rank, 4 * rank)
    whole = pl.BlockSpec(memory_space=pltpu.VMEM)
    return pl.pallas_call(
        lambda *refs: tables_kernel(wide, room, *refs),
        out_shape=[
            jax.ShapeDtypeStruct(shape, jnp.bfloat16),
            jax.ShapeDtypeStruct(shape, jnp.bfloat16),
            jax.ShapeDtypeStruct((levels, 2 * rank, 2 * rank), jnp.bfloat16),
        ],
        in_specs=[whole] * 2,
        out_specs=[whole] * 3,
        compiler_params=pltpu.CompilerParams(vmem_limit_bytes=16 * 1024 * 1024),
        cost_estimate=pl.CostEstimate(flops=50_000_000, bytes_accessed=600_000, transcendentals=0),
        name="tables",
    )(skeleton, compress)


def compact_rows(matrix, slot):
    rank = slot.shape[1]
    parts = [
        jnp.dot(slot, half, preferred_element_type=jnp.float32)
        for half in (matrix[:rank], matrix[rank:])
    ]
    return jnp.concatenate(parts, 0).astype(jnp.bfloat16)


def times(matrix, value):
    return jnp.dot(matrix, value, preferred_element_type=jnp.float32).astype(jnp.bfloat16)


def sampled(sampling, traces):
    return jnp.einsum(
        "pc,tp->ct", sampling, traces, preferred_element_type=jnp.float32
    ).astype(jnp.bfloat16)


def evaluated(coeffs, evaluation):
    return jnp.einsum(
        "ct,cp->tp", coeffs, evaluation, preferred_element_type=jnp.float32
    ).astype(jnp.bfloat16)


def after(value, earlier):
    return value if earlier is None else lax.optimization_barrier((value, earlier))[0]


def all_hops():
    low_bits = lax.axis_size("sub").bit_length() - 1
    high_bits = lax.axis_size("bfly").bit_length() - 1
    return [("sub", bit) for bit in range(low_bits)] + [("bfly", bit) for bit in range(high_bits)]


def full_width(traces, sampling, full, evaluation):
    coeffs = sampled(sampling, traces)
    for level, hop in enumerate(all_hops()):
        partner = from_partner(coeffs, hop)
        coeffs = times(full[level], jnp.concatenate([coeffs, partner], 0))
    return evaluated(coeffs, evaluation)


def sequence(pieces, levels):
    def turn(at):
        level, piece = at
        if level == 0:
            return max(0, 2 * piece - 1)
        return 2 * (level + piece + (piece > 0))

    return sorted(
        [(level, piece) for level in range(levels + 1) for piece in range(pieces)],
        key=lambda at: (turn(at), at),
    )


def local(traces, sampling, skeleton, compress, evaluation):
    sampling, evaluation = sampling[0], evaluation[0]
    hops = all_hops()
    levels = len(hops)
    wide = lax.axis_size("sub").bit_length() - 1
    rank = skeleton.shape[-1]
    room = rank * ROOM_SIXTEENTHS // 16
    full, small, extra = tables(skeleton, compress, wide, room)
    most_here = lax.broadcasted_iota(jnp.int32, extra.shape[1:], 1) >= rank

    def compact(level, piece):
        return piece > 0 and level >= wide

    unit = traces.shape[0] // sum(SIXTEENTHS)
    pieces = len(SIXTEENTHS)
    starts = [unit * sum(SIXTEENTHS[:i]) for i in range(pieces + 1)]
    inputs, partners, theirs, done = {}, {}, {}, [None] * pieces
    previous, known = None, None
    for level, piece in sequence(pieces, levels):
        count = starts[piece + 1] - starts[piece]
        if level == 0:
            own = sampled(
                after(sampling, previous) if piece > 1 else sampling,
                traces[starts[piece] : starts[piece + 1]],
            )
        else:
            arrived = after(partners[piece], previous)
            if piece == 0 and level - 1 >= wide:
                known = arrived[:, count:]
                theirs[level - 1] = known[:room, :rank]
            value = jnp.concatenate([inputs[piece], arrived[:, :count]], 0)
            matrix = full[level - 1]
            if compact(level - 1, piece):
                value = jnp.pad(value, ((0, full.shape[2] - value.shape[0]), (0, 0)))
                matrix = small[level - 1]
            own = times(matrix, value)
        if level == levels:
            done[piece] = evaluated(own, evaluation)
            continue
        outgoing = own
        if compact(level, piece):
            outgoing = times(compact_rows(matrix, theirs[level]), value)
        if piece == 0 and level >= wide:
            block = extra[level]
            if known is not None:
                block = jnp.where(most_here, jnp.maximum(block, known), block)
            outgoing = jnp.concatenate([outgoing, block], 1)
        inputs[piece] = own
        partners[piece] = from_partner(outgoing, hops[level])
        previous = outgoing
    most = after(jnp.maximum(extra[levels - 1], known)[:8, rank:], previous)
    for hop in hops[:wide]:
        most = jnp.maximum(most, from_partner(most, hop))
    quick = jnp.concatenate(done, 0)
    return lax.cond(
        most[0, 0] > room,
        lambda: full_width(traces, sampling, full, evaluation),
        lambda: quick,
    )


def solution(mesh):
    placed = (
        P(("shots", "tr"), ("bfly", "sub")),
        P(("bfly", "sub"), None, None),
        P(("bfly", "sub"), None, None),
        P(("bfly", "sub"), None, None, None),
        P(("bfly", "sub"), None, None),
    )
    return jax.shard_map(
        local,
        mesh=mesh,
        in_specs=placed,
        out_specs=P(("shots", "tr"), ("bfly", "sub")),
        check_vma=False,
    )
```

```python
import jax
import jax.numpy as jnp
from jax import lax
from jax.experimental import pallas as pl
from jax.experimental.pallas import tpu as pltpu
from jax.sharding import PartitionSpec as P

SHARES = (2, 4, 8, 9, 9)
ROOM_SIXTEENTHS = 12


def route(axis, apart):
    count = lax.axis_size(axis)
    pairs = []
    for low in range(count):
        high = low | 1 << apart
        if high != low and high < count:
            pairs += [(low, high), (high, low)]
    return pairs


def from_partner(block, hop):
    return lax.ppermute(block, hop[0], route(*hop))


def across(left, right):
    return lax.dot_general(left, right, (((1,), (1,)), ((), ())), preferred_element_type=jnp.float32)


def one_hot(condition):
    return jnp.where(condition, 1.0, 0.0).astype(jnp.bfloat16)


def sampled_block(sampling, rows):
    turned = sampling.astype(jnp.float32).T.astype(jnp.bfloat16)
    return across(turned, rows).astype(jnp.bfloat16)


def first_kernel(
    wide, room, count, skeleton_hbm, compress_hbm, sampling_hbm, traces_hbm,
    full_ref, small_ref, extra_ref, coeffs_ref,
    skeleton_ref, compress_ref, sampling_ref, rows_ref, arrived,
):
    loads = [
        pltpu.make_async_copy(skeleton_hbm, skeleton_ref, arrived.at[0]),
        pltpu.make_async_copy(compress_hbm, compress_ref, arrived.at[1]),
        pltpu.make_async_copy(sampling_hbm, sampling_ref, arrived.at[2]),
        pltpu.make_async_copy(traces_hbm.at[pl.ds(0, count)], rows_ref, arrived.at[3]),
    ]
    for load in loads:
        load.start()
    for load in loads:
        load.wait()
    coeffs_ref[...] = sampled_block(sampling_ref[0], rows_ref[...])
    levels, rank = skeleton_ref.shape[0], skeleton_ref.shape[-1]
    width = 2 * rank
    f32, i32 = jnp.float32, jnp.int32
    k = lax.broadcasted_iota(i32, (width, width), 1)
    twice = one_hot(lax.broadcasted_iota(i32, (width, rank), 0) % rank == lax.broadcasted_iota(i32, (width, rank), 1))
    earlier = one_hot(
        (lax.broadcasted_iota(i32, (width, width), 1) < lax.broadcasted_iota(i32, (width, width), 0) % rank)
    )
    column = lax.broadcasted_iota(i32, (2 * width, width), 0)
    is_real_entry = lax.broadcasted_iota(i32, (2 * width, width), 1) < rank
    partner_column = column >= width
    imag_column = column % width >= rank
    coefficient = column % rank + jnp.where(partner_column, rank, 0)
    slot_column = column - width
    slot_imag = slot_column >= room
    slot_of_column = jnp.where(slot_imag, slot_column - room, slot_column)
    row = lax.broadcasted_iota(i32, (width, width), 0)
    most = jnp.zeros((1, 1), f32)
    for level in range(levels):
        entry = jnp.broadcast_to(skeleton_ref[level].astype(f32), (8, rank)).astype(jnp.bfloat16)
        entry = across(entry, twice)[:1]
        picked = jnp.where(entry >= rank, 1.0, 0.0)
        slot = across(jnp.broadcast_to(picked, (8, width)).astype(jnp.bfloat16), earlier)[:1].astype(i32)
        entry = entry.astype(i32)
        from_partner_entry = entry >= rank
        matrix = compress_ref[0, level]

        def halves(match, imag):
            same = is_real_entry != imag
            real = jnp.where(match & same, jnp.where(imag, -1.0, 1.0), 0.0).astype(jnp.bfloat16)
            turned = one_hot(match & jnp.logical_not(same))
            return across(matrix, real).astype(jnp.bfloat16), across(matrix, turned).astype(jnp.bfloat16)

        match = entry == coefficient
        full_ref[level, :rank], full_ref[level, rank:] = halves(match, imag_column)
        compacted = (slot == slot_of_column) & from_partner_entry
        match = (match & jnp.logical_not(partner_column)) | (compacted & partner_column)
        imag = (imag_column & jnp.logical_not(partner_column)) | (slot_imag & partner_column)
        small_ref[level, :rank], small_ref[level, rank:] = halves(match, imag)
        once = (k < rank) & from_partner_entry
        places = across(one_hot(once & (slot == row)), one_hot(once & (entry - rank == row)))
        extra_ref[level] = places.astype(jnp.bfloat16)
        if level >= wide:
            most = jnp.maximum(most, jnp.sum(picked, axis=1, keepdims=True) * 0.5)
    for level in range(wide, levels):
        extra_ref[level] = jnp.where(k < rank, extra_ref[level].astype(f32), most).astype(jnp.bfloat16)


def first(skeleton, compress, sampling, traces, wide, room, count):
    levels, rank = skeleton.shape[1:]
    shape = (levels, 2 * rank, 4 * rank)
    width = sampling.shape[-1]
    whole = pl.BlockSpec(memory_space=pltpu.VMEM)
    return pl.pallas_call(
        lambda *refs: first_kernel(wide, room, count, *refs),
        out_shape=[
            jax.ShapeDtypeStruct(shape, jnp.bfloat16),
            jax.ShapeDtypeStruct(shape, jnp.bfloat16),
            jax.ShapeDtypeStruct((levels, 2 * rank, 2 * rank), jnp.bfloat16),
            jax.ShapeDtypeStruct((width, count), jnp.bfloat16),
        ],
        in_specs=[pl.BlockSpec(memory_space=pl.ANY)] * 4,
        out_specs=[whole] * 4,
        scratch_shapes=[
            pltpu.VMEM((levels, 1, rank), jnp.int32),
            pltpu.VMEM(compress.shape, jnp.bfloat16),
            pltpu.VMEM(sampling.shape, jnp.bfloat16),
            pltpu.VMEM((count, traces.shape[1]), jnp.bfloat16),
            pltpu.SemaphoreType.DMA((4,)),
        ],
        compiler_params=pltpu.CompilerParams(vmem_limit_bytes=16 * 1024 * 1024),
        cost_estimate=pl.CostEstimate(flops=50_000_000, bytes_accessed=600_000, transcendentals=0),
        name="first",
    )(skeleton.transpose(1, 0, 2), compress, sampling, traces)


def rest_kernel(starts, sampling_hbm, traces_hbm, *refs):
    pieces = len(starts) - 1
    outs, (sampling_ref, rows_ref, arrived) = refs[:pieces], refs[pieces:]
    base = starts[0]
    loads = [pltpu.make_async_copy(sampling_hbm, sampling_ref, arrived.at[pieces])]
    for i in range(pieces):
        span = pl.ds(starts[i], starts[i + 1] - starts[i])
        here = pl.ds(starts[i] - base, starts[i + 1] - starts[i])
        loads.append(pltpu.make_async_copy(traces_hbm.at[span], rows_ref.at[here], arrived.at[i]))
    for load in loads:
        load.start()
    loads[0].wait()
    for i in range(pieces):
        loads[i + 1].wait()
        here = pl.ds(starts[i] - base, starts[i + 1] - starts[i])
        outs[i][...] = sampled_block(sampling_ref[0], rows_ref[here])


def rest(sampling, traces, starts):
    pieces = len(starts) - 1
    width = sampling.shape[-1]
    total = starts[-1] - starts[0]
    return pl.pallas_call(
        lambda *refs: rest_kernel(starts, *refs),
        out_shape=[
            jax.ShapeDtypeStruct((width, starts[i + 1] - starts[i]), jnp.bfloat16) for i in range(pieces)
        ],
        in_specs=[pl.BlockSpec(memory_space=pl.ANY)] * 2,
        out_specs=[pl.BlockSpec(memory_space=pltpu.VMEM)] * pieces,
        scratch_shapes=[
            pltpu.VMEM(sampling.shape, jnp.bfloat16),
            pltpu.VMEM((total, traces.shape[1]), jnp.bfloat16),
            pltpu.SemaphoreType.DMA((pieces + 1,)),
        ],
        compiler_params=pltpu.CompilerParams(vmem_limit_bytes=16 * 1024 * 1024),
        cost_estimate=pl.CostEstimate(
            flops=2 * total * width * width, bytes_accessed=4 * total * width, transcendentals=0
        ),
        name="rest",
    )(sampling, traces)


def compact_rows(matrix, slot):
    rank = slot.shape[1]
    parts = [
        jnp.dot(slot, half, preferred_element_type=jnp.float32)
        for half in (matrix[:rank], matrix[rank:])
    ]
    return jnp.concatenate(parts, 0).astype(jnp.bfloat16)


def times(matrix, value):
    return jnp.dot(matrix, value, preferred_element_type=jnp.float32).astype(jnp.bfloat16)


def sampled(sampling, traces):
    return jnp.einsum(
        "pc,tp->ct", sampling, traces, preferred_element_type=jnp.float32
    ).astype(jnp.bfloat16)


def evaluated(coeffs, evaluation):
    return jnp.einsum(
        "ct,cp->tp", coeffs, evaluation, preferred_element_type=jnp.float32
    ).astype(jnp.bfloat16)


def after(value, earlier):
    return value if earlier is None else lax.optimization_barrier((value, earlier))[0]


def all_hops():
    low_bits = lax.axis_size("sub").bit_length() - 1
    high_bits = lax.axis_size("bfly").bit_length() - 1
    return [("sub", bit) for bit in range(low_bits)] + [("bfly", bit) for bit in range(high_bits)]


def full_width(traces, sampling, full, evaluation):
    coeffs = sampled(sampling, traces)
    for level, hop in enumerate(all_hops()):
        partner = from_partner(coeffs, hop)
        coeffs = times(full[level], jnp.concatenate([coeffs, partner], 0))
    return evaluated(coeffs, evaluation)


def sequence(pieces, levels):
    def turn(at):
        level, piece = at
        if level == 0:
            return 0 if piece < 2 else 3 if piece == 2 else 2 * piece + 1
        return 2 * (level + piece + (piece > 0))

    return sorted(
        [(level, piece) for level in range(levels + 1) for piece in range(pieces)],
        key=lambda at: (turn(at), at),
    )


def local(traces, sampling, skeleton, compress, evaluation):
    hops = all_hops()
    levels = len(hops)
    wide = lax.axis_size("sub").bit_length() - 1
    rank = skeleton.shape[-1]
    room = rank * ROOM_SIXTEENTHS // 16
    unit = traces.shape[0] // sum(SHARES)
    pieces = len(SHARES)
    starts = [unit * sum(SHARES[:i]) for i in range(pieces + 1)]
    full, small, extra, coeffs = first(skeleton, compress, sampling, traces, wide, room, starts[1])
    sampling, evaluation = after(sampling, coeffs), evaluation[0]
    coeffs = [coeffs] + list(rest(sampling, traces, starts[1:]))
    most_here = lax.broadcasted_iota(jnp.int32, extra.shape[1:], 1) >= rank

    def compact(level, piece):
        return piece > 0 and level >= wide

    inputs, partners, theirs, done = {}, {}, {}, [None] * pieces
    previous, known = None, None
    for level, piece in sequence(pieces, levels):
        count = starts[piece + 1] - starts[piece]
        if level == 0:
            own = after(coeffs[piece], previous if piece > 1 else None)
        else:
            arrived = after(partners[piece], previous)
            if piece == 0 and level - 1 >= wide:
                known = arrived[:, count:]
                theirs[level - 1] = known[:room, :rank]
            value = jnp.concatenate([inputs[piece], arrived[:, :count]], 0)
            matrix = full[level - 1]
            if compact(level - 1, piece):
                value = jnp.pad(value, ((0, full.shape[2] - value.shape[0]), (0, 0)))
                matrix = small[level - 1]
            own = times(matrix, value)
        if level == levels:
            done[piece] = evaluated(own, evaluation)
            continue
        outgoing = own
        if compact(level, piece):
            outgoing = times(compact_rows(matrix, theirs[level]), value)
        if piece == 0 and level >= wide:
            block = extra[level]
            if known is not None:
                block = jnp.where(most_here, jnp.maximum(block, known), block)
            outgoing = jnp.concatenate([outgoing, block], 1)
        inputs[piece] = own
        partners[piece] = from_partner(outgoing, hops[level])
        previous = outgoing
    most = after(jnp.maximum(extra[levels - 1], known)[:8, rank:], previous)
    for hop in hops[:wide]:
        most = jnp.maximum(most, from_partner(most, hop))
    quick = jnp.concatenate(done, 0)
    return lax.cond(
        most[0, 0] > room,
        lambda: full_width(traces, sampling[0], full, evaluation),
        lambda: quick,
    )


def solution(mesh):
    placed = (
        P(("shots", "tr"), ("bfly", "sub")),
        P(("bfly", "sub"), None, None),
        P(("bfly", "sub"), None, None),
        P(("bfly", "sub"), None, None, None),
        P(("bfly", "sub"), None, None),
    )
    return jax.shard_map(
        local,
        mesh=mesh,
        in_specs=placed,
        out_specs=P(("shots", "tr"), ("bfly", "sub")),
        check_vma=False,
    )
```

```python
import jax
import jax.numpy as jnp
from jax import lax
from jax.experimental import pallas as pl
from jax.experimental.pallas import tpu as pltpu
from jax.sharding import PartitionSpec as P

SHARES = (1, 3, 8, 10, 10)
FULL_PIECES = 2
KERNEL_VMEM = 60 * 1024 * 1024
ROOM_SIXTEENTHS = 12


def route(axis, apart):
    count = lax.axis_size(axis)
    pairs = []
    for low in range(count):
        high = low | 1 << apart
        if high != low and high < count:
            pairs += [(low, high), (high, low)]
    return pairs


def from_partner(block, hop):
    return lax.ppermute(block, hop[0], route(*hop))


def across(left, right):
    return lax.dot_general(left, right, (((1,), (1,)), ((), ())), preferred_element_type=jnp.float32)


def one_hot(condition):
    return jnp.where(condition, 1.0, 0.0).astype(jnp.bfloat16)


def sampled_block(sampling, rows):
    turned = sampling.astype(jnp.float32).T.astype(jnp.bfloat16)
    return across(turned, rows).astype(jnp.bfloat16)


def first_kernel(
    wide, room, count, skeleton_hbm, compress_hbm, sampling_hbm, traces_hbm,
    full_ref, small_ref, extra_ref, coeffs_ref,
    skeleton_ref, compress_ref, sampling_ref, rows_ref, arrived,
):
    loads = [
        pltpu.make_async_copy(skeleton_hbm, skeleton_ref, arrived.at[0]),
        pltpu.make_async_copy(compress_hbm, compress_ref, arrived.at[1]),
        pltpu.make_async_copy(sampling_hbm, sampling_ref, arrived.at[2]),
        pltpu.make_async_copy(traces_hbm.at[pl.ds(0, count)], rows_ref, arrived.at[3]),
    ]
    for load in loads:
        load.start()
    for load in loads:
        load.wait()
    coeffs_ref[...] = sampled_block(sampling_ref[0], rows_ref[...])
    levels, rank = skeleton_ref.shape[0], skeleton_ref.shape[-1]
    width = 2 * rank
    f32, i32 = jnp.float32, jnp.int32
    k = lax.broadcasted_iota(i32, (width, width), 1)
    twice = one_hot(lax.broadcasted_iota(i32, (width, rank), 0) % rank == lax.broadcasted_iota(i32, (width, rank), 1))
    earlier = one_hot(
        (lax.broadcasted_iota(i32, (width, width), 1) < lax.broadcasted_iota(i32, (width, width), 0) % rank)
    )
    column = lax.broadcasted_iota(i32, (2 * width, width), 0)
    is_real_entry = lax.broadcasted_iota(i32, (2 * width, width), 1) < rank
    partner_column = column >= width
    imag_column = column % width >= rank
    coefficient = column % rank + jnp.where(partner_column, rank, 0)
    slot_column = column - width
    slot_imag = slot_column >= room
    slot_of_column = jnp.where(slot_imag, slot_column - room, slot_column)
    row = lax.broadcasted_iota(i32, (width, width), 0)
    most = jnp.zeros((1, 1), f32)
    for level in range(levels):
        entry = jnp.broadcast_to(skeleton_ref[level].astype(f32), (8, rank)).astype(jnp.bfloat16)
        entry = across(entry, twice)[:1]
        picked = jnp.where(entry >= rank, 1.0, 0.0)
        slot = across(jnp.broadcast_to(picked, (8, width)).astype(jnp.bfloat16), earlier)[:1].astype(i32)
        entry = entry.astype(i32)
        from_partner_entry = entry >= rank
        matrix = compress_ref[0, level]

        def halves(match, imag):
            same = is_real_entry != imag
            real = jnp.where(match & same, jnp.where(imag, -1.0, 1.0), 0.0).astype(jnp.bfloat16)
            turned = one_hot(match & jnp.logical_not(same))
            return across(matrix, real).astype(jnp.bfloat16), across(matrix, turned).astype(jnp.bfloat16)

        match = entry == coefficient
        full_ref[level, :rank], full_ref[level, rank:] = halves(match, imag_column)
        compacted = (slot == slot_of_column) & from_partner_entry
        match = (match & jnp.logical_not(partner_column)) | (compacted & partner_column)
        imag = (imag_column & jnp.logical_not(partner_column)) | (slot_imag & partner_column)
        small_ref[level, :rank], small_ref[level, rank:] = halves(match, imag)
        once = (k < rank) & from_partner_entry
        places = across(one_hot(once & (slot == row)), one_hot(once & (entry - rank == row)))
        extra_ref[level] = places.astype(jnp.bfloat16)
        if level >= wide:
            most = jnp.maximum(most, jnp.sum(picked, axis=1, keepdims=True) * 0.5)
    for level in range(wide, levels):
        extra_ref[level] = jnp.where(k < rank, extra_ref[level].astype(f32), most).astype(jnp.bfloat16)


def first(skeleton, compress, sampling, traces, wide, room, count):
    levels, rank = skeleton.shape[1:]
    shape = (levels, 2 * rank, 4 * rank)
    width = sampling.shape[-1]
    whole = pl.BlockSpec(memory_space=pltpu.VMEM)
    return pl.pallas_call(
        lambda *refs: first_kernel(wide, room, count, *refs),
        out_shape=[
            jax.ShapeDtypeStruct(shape, jnp.bfloat16),
            jax.ShapeDtypeStruct(shape, jnp.bfloat16),
            jax.ShapeDtypeStruct((levels, 2 * rank, 2 * rank), jnp.bfloat16),
            jax.ShapeDtypeStruct((width, count), jnp.bfloat16),
        ],
        in_specs=[pl.BlockSpec(memory_space=pl.ANY)] * 4,
        out_specs=[whole] * 4,
        scratch_shapes=[
            pltpu.VMEM((levels, 1, rank), jnp.int32),
            pltpu.VMEM(compress.shape, jnp.bfloat16),
            pltpu.VMEM(sampling.shape, jnp.bfloat16),
            pltpu.VMEM((count, traces.shape[1]), jnp.bfloat16),
            pltpu.SemaphoreType.DMA((4,)),
        ],
        compiler_params=pltpu.CompilerParams(vmem_limit_bytes=KERNEL_VMEM),
        cost_estimate=pl.CostEstimate(flops=50_000_000, bytes_accessed=600_000, transcendentals=0),
        name="first",
    )(skeleton.transpose(1, 0, 2), compress, sampling, traces)


def sampled_apart(sampling, traces):
    count, width = traces.shape
    block = count // 8

    def kernel(sampling_ref, rows_ref, coeffs_ref):
        coeffs_ref[...] = sampled_block(sampling_ref[...], rows_ref[...])

    return pl.pallas_call(
        kernel,
        grid=(count // block,),
        out_shape=jax.ShapeDtypeStruct((sampling.shape[1], count), jnp.bfloat16),
        in_specs=[
            pl.BlockSpec(sampling.shape, lambda i: (0, 0)),
            pl.BlockSpec((block, width), lambda i: (i, 0)),
        ],
        out_specs=pl.BlockSpec((sampling.shape[1], block), lambda i: (0, i)),
        compiler_params=pltpu.CompilerParams(vmem_limit_bytes=63 * 1024 * 1024),
        name="sampled_apart",
    )(sampling, traces)


def picked_columns(compress, skeleton):
    rank = skeleton.shape[-1]
    places = lax.broadcasted_iota(jnp.int32, (1, 1, 2 * rank), 2)
    chooser = (skeleton[:, :, None] == places).astype(jnp.bfloat16)
    stacked = jnp.concatenate([compress[:, :, :rank], compress[:, :, rank:]], 1)
    return jnp.einsum(
        "ljk,lki->lji", stacked, chooser, preferred_element_type=jnp.float32
    ).astype(jnp.bfloat16)


def real_form(both):
    rank = both.shape[1] // 2
    turned = jnp.concatenate([-both[:, rank:], both[:, :rank]], 1)
    return jnp.concatenate([both, turned], 2)


def compact_rows(matrix, slot):
    rank = slot.shape[1]
    parts = [
        jnp.dot(slot, half, preferred_element_type=jnp.float32)
        for half in (matrix[:rank], matrix[rank:])
    ]
    return jnp.concatenate(parts, 0).astype(jnp.bfloat16)


def times(matrix, value):
    return jnp.dot(matrix, value, preferred_element_type=jnp.float32).astype(jnp.bfloat16)


def sampled(sampling, traces):
    return jnp.einsum(
        "pc,tp->ct", sampling, traces, preferred_element_type=jnp.float32
    ).astype(jnp.bfloat16)


def evaluated(coeffs, evaluation):
    return jnp.einsum(
        "ct,cp->tp", coeffs, evaluation, preferred_element_type=jnp.float32
    ).astype(jnp.bfloat16)


def after(value, earlier):
    return value if earlier is None else lax.optimization_barrier((value, earlier))[0]


def all_hops():
    low_bits = lax.axis_size("sub").bit_length() - 1
    high_bits = lax.axis_size("bfly").bit_length() - 1
    return [("sub", bit) for bit in range(low_bits)] + [("bfly", bit) for bit in range(high_bits)]


def full_width(traces, sampling, skeleton, compress, evaluation):
    rank = skeleton.shape[-1]
    columns = picked_columns(compress, skeleton)
    full = jnp.concatenate([real_form(columns[..., :rank]), real_form(columns[..., rank:])], 2)
    coeffs = sampled_apart(sampling, traces)
    for level, hop in enumerate(all_hops()):
        partner = from_partner(coeffs, hop)
        coeffs = times(full[level], jnp.concatenate([coeffs, partner], 0))
    return evaluated(coeffs, evaluation)


def sequence(pieces, levels):
    def turn(at):
        level, piece = at
        if piece < FULL_PIECES:
            late = 1.5 if level == levels and piece else 0
            return 2 * level + 0.5 * piece + late
        if level == 0:
            return 2.2 if piece == 2 else 5.5 if piece == 3 else 7.05 + 2.1 * (piece - 4)
        late = 2.15 if level == levels else 0
        return 2 * level + 3 + 2.1 * (piece - 2) + late

    return sorted(
        [(level, piece) for level in range(levels + 1) for piece in range(pieces)], key=turn
    )


def local(traces, sampling, skeleton, compress, evaluation):
    hops = all_hops()
    levels = len(hops)
    wide = lax.axis_size("sub").bit_length() - 1
    rank = skeleton.shape[-1]
    room = rank * ROOM_SIXTEENTHS // 16
    unit = traces.shape[0] // sum(SHARES)
    pieces = len(SHARES)
    starts = [unit * sum(SHARES[:i]) for i in range(pieces + 1)]
    full, small, extra, coeffs = first(skeleton, compress, sampling, traces, wide, room, starts[1])
    sampling, evaluation = sampling[0], evaluation[0]
    most_here = lax.broadcasted_iota(jnp.int32, extra.shape[1:], 1) >= rank

    def compact(level, piece):
        return piece >= FULL_PIECES and level >= wide

    inputs, partners, theirs, done = {}, {}, {}, [None] * pieces
    previous, known = None, None
    for level, piece in sequence(pieces, levels):
        count = starts[piece + 1] - starts[piece]
        if level == 0:
            own = coeffs
            if piece > 0:
                block = traces[starts[piece] : starts[piece + 1]]
                own = sampled(after(sampling, coeffs if piece == 1 else previous), block)
        else:
            arrived = after(partners[piece], previous)
            if piece == 0 and level - 1 >= wide:
                known = arrived[:, count:]
                theirs[level - 1] = known[:room, :rank]
            value = jnp.concatenate([inputs[piece], arrived[:, :count]], 0)
            matrix = full[level - 1]
            if compact(level - 1, piece):
                value = jnp.pad(value, ((0, full.shape[2] - value.shape[0]), (0, 0)))
                matrix = small[level - 1]
            own = times(matrix, value)
        if level == levels:
            done[piece] = evaluated(own, evaluation)
            continue
        outgoing = own
        if compact(level, piece):
            outgoing = times(compact_rows(matrix, theirs[level]), value)
        if piece == 0 and level >= wide:
            block = extra[level]
            if known is not None:
                block = jnp.where(most_here, jnp.maximum(block, known), block)
            outgoing = jnp.concatenate([outgoing, block], 1)
        inputs[piece] = own
        partners[piece] = from_partner(outgoing, hops[level])
        previous = outgoing
    most = after(jnp.maximum(extra[levels - 1], known)[:8, rank:], previous)
    for hop in hops[:wide]:
        most = jnp.maximum(most, from_partner(most, hop))
    quick = jnp.concatenate(done, 0)
    return lax.cond(
        most[0, 0] > room,
        lambda: full_width(traces, sampling, skeleton[0], compress[0], evaluation),
        lambda: quick,
    )


def solution(mesh):
    placed = (
        P(("shots", "tr"), ("bfly", "sub")),
        P(("bfly", "sub"), None, None),
        P(("bfly", "sub"), None, None),
        P(("bfly", "sub"), None, None, None),
        P(("bfly", "sub"), None, None),
    )
    return jax.shard_map(
        local,
        mesh=mesh,
        in_specs=placed,
        out_specs=P(("shots", "tr"), ("bfly", "sub")),
        check_vma=False,
    )
```

```python
import jax
import jax.numpy as jnp
from jax import lax
from jax.experimental import pallas as pl
from jax.experimental.pallas import tpu as pltpu
from jax.sharding import PartitionSpec as P

SHARES = (1, 3, 8, 9, 11)
FULL_PIECES = 2
KERNEL_VMEM = 16 * 1024 * 1024
ROOM_SIXTEENTHS = 12


def route(axis, apart):
    count = lax.axis_size(axis)
    pairs = []
    for low in range(count):
        high = low | 1 << apart
        if high != low and high < count:
            pairs += [(low, high), (high, low)]
    return pairs


def from_partner(block, hop):
    return lax.ppermute(block, hop[0], route(*hop))


def across(left, right):
    return lax.dot_general(left, right, (((1,), (1,)), ((), ())), preferred_element_type=jnp.float32)


def one_hot(condition):
    return jnp.where(condition, 1.0, 0.0).astype(jnp.bfloat16)


def sampled_block(sampling, rows):
    turned = sampling.astype(jnp.float32).T.astype(jnp.bfloat16)
    return across(turned, rows).astype(jnp.bfloat16)


def first_kernel(
    wide, room, count, skeleton_hbm, compress_hbm, sampling_hbm, traces_hbm,
    full_ref, small_ref, extra_ref, coeffs_ref,
    skeleton_ref, compress_ref, sampling_ref, rows_ref, arrived,
):
    loads = [
        pltpu.make_async_copy(skeleton_hbm, skeleton_ref, arrived.at[0]),
        pltpu.make_async_copy(compress_hbm, compress_ref, arrived.at[1]),
        pltpu.make_async_copy(sampling_hbm, sampling_ref, arrived.at[2]),
        pltpu.make_async_copy(traces_hbm.at[pl.ds(0, count)], rows_ref, arrived.at[3]),
    ]
    for load in loads:
        load.start()
    for load in loads:
        load.wait()
    coeffs_ref[...] = sampled_block(sampling_ref[0], rows_ref[...])
    levels, rank = skeleton_ref.shape[0], skeleton_ref.shape[-1]
    width = 2 * rank
    f32, i32 = jnp.float32, jnp.int32
    k = lax.broadcasted_iota(i32, (width, width), 1)
    twice = one_hot(lax.broadcasted_iota(i32, (width, rank), 0) % rank == lax.broadcasted_iota(i32, (width, rank), 1))
    earlier = one_hot(
        (lax.broadcasted_iota(i32, (width, width), 1) < lax.broadcasted_iota(i32, (width, width), 0) % rank)
    )
    column = lax.broadcasted_iota(i32, (2 * width, width), 0)
    is_real_entry = lax.broadcasted_iota(i32, (2 * width, width), 1) < rank
    partner_column = column >= width
    imag_column = column % width >= rank
    coefficient = column % rank + jnp.where(partner_column, rank, 0)
    slot_column = column - width
    slot_imag = slot_column >= room
    slot_of_column = jnp.where(slot_imag, slot_column - room, slot_column)
    row = lax.broadcasted_iota(i32, (width, width), 0)
    most = jnp.zeros((1, 1), f32)
    for level in range(levels):
        entry = jnp.broadcast_to(skeleton_ref[level].astype(f32), (8, rank)).astype(jnp.bfloat16)
        entry = across(entry, twice)[:1]
        picked = jnp.where(entry >= rank, 1.0, 0.0)
        slot = across(jnp.broadcast_to(picked, (8, width)).astype(jnp.bfloat16), earlier)[:1].astype(i32)
        entry = entry.astype(i32)
        from_partner_entry = entry >= rank
        matrix = compress_ref[0, level]

        def halves(match, imag):
            same = is_real_entry != imag
            real = jnp.where(match & same, jnp.where(imag, -1.0, 1.0), 0.0).astype(jnp.bfloat16)
            turned = one_hot(match & jnp.logical_not(same))
            return across(matrix, real).astype(jnp.bfloat16), across(matrix, turned).astype(jnp.bfloat16)

        match = entry == coefficient
        full_ref[level, :rank], full_ref[level, rank:] = halves(match, imag_column)
        compacted = (slot == slot_of_column) & from_partner_entry
        match = (match & jnp.logical_not(partner_column)) | (compacted & partner_column)
        imag = (imag_column & jnp.logical_not(partner_column)) | (slot_imag & partner_column)
        small_ref[level, :rank], small_ref[level, rank:] = halves(match, imag)
        once = (k < rank) & from_partner_entry
        places = across(one_hot(once & (slot == row)), one_hot(once & (entry - rank == row)))
        extra_ref[level] = places.astype(jnp.bfloat16)
        if level >= wide:
            most = jnp.maximum(most, jnp.sum(picked, axis=1, keepdims=True) * 0.5)
    for level in range(wide, levels):
        extra_ref[level] = jnp.where(k < rank, extra_ref[level].astype(f32), most).astype(jnp.bfloat16)


def first(skeleton, compress, sampling, traces, wide, room, count):
    levels, rank = skeleton.shape[1:]
    shape = (levels, 2 * rank, 4 * rank)
    width = sampling.shape[-1]
    whole = pl.BlockSpec(memory_space=pltpu.VMEM)
    return pl.pallas_call(
        lambda *refs: first_kernel(wide, room, count, *refs),
        out_shape=[
            jax.ShapeDtypeStruct(shape, jnp.bfloat16),
            jax.ShapeDtypeStruct(shape, jnp.bfloat16),
            jax.ShapeDtypeStruct((levels, 2 * rank, 2 * rank), jnp.bfloat16),
            jax.ShapeDtypeStruct((width, count), jnp.bfloat16),
        ],
        in_specs=[pl.BlockSpec(memory_space=pltpu.HBM)] * 4,
        out_specs=[whole] * 4,
        scratch_shapes=[
            pltpu.VMEM((levels, 1, rank), jnp.int32),
            pltpu.VMEM(compress.shape, jnp.bfloat16),
            pltpu.VMEM(sampling.shape, jnp.bfloat16),
            pltpu.VMEM((count, traces.shape[1]), jnp.bfloat16),
            pltpu.SemaphoreType.DMA((4,)),
        ],
        compiler_params=pltpu.CompilerParams(vmem_limit_bytes=KERNEL_VMEM),
        cost_estimate=pl.CostEstimate(flops=50_000_000, bytes_accessed=600_000, transcendentals=0),
        name="first",
    )(skeleton.transpose(1, 0, 2), compress, sampling, traces)


def sampled_apart(sampling, traces):
    count, width = traces.shape
    block = count // 8

    def kernel(sampling_ref, rows_ref, coeffs_ref):
        coeffs_ref[...] = sampled_block(sampling_ref[...], rows_ref[...])

    return pl.pallas_call(
        kernel,
        grid=(count // block,),
        out_shape=jax.ShapeDtypeStruct((sampling.shape[1], count), jnp.bfloat16),
        in_specs=[
            pl.BlockSpec(sampling.shape, lambda i: (0, 0)),
            pl.BlockSpec((block, width), lambda i: (i, 0)),
        ],
        out_specs=pl.BlockSpec((sampling.shape[1], block), lambda i: (0, i)),
        compiler_params=pltpu.CompilerParams(vmem_limit_bytes=63 * 1024 * 1024),
        name="sampled_apart",
    )(sampling, traces)


def picked_columns(compress, skeleton):
    rank = skeleton.shape[-1]
    places = lax.broadcasted_iota(jnp.int32, (1, 1, 2 * rank), 2)
    chooser = (skeleton[:, :, None] == places).astype(jnp.bfloat16)
    stacked = jnp.concatenate([compress[:, :, :rank], compress[:, :, rank:]], 1)
    return jnp.einsum(
        "ljk,lki->lji", stacked, chooser, preferred_element_type=jnp.float32
    ).astype(jnp.bfloat16)


def real_form(both):
    rank = both.shape[1] // 2
    turned = jnp.concatenate([-both[:, rank:], both[:, :rank]], 1)
    return jnp.concatenate([both, turned], 2)


def compact_rows(matrix, slot):
    rank = slot.shape[1]
    parts = [
        jnp.dot(slot, half, preferred_element_type=jnp.float32)
        for half in (matrix[:rank], matrix[rank:])
    ]
    return jnp.concatenate(parts, 0).astype(jnp.bfloat16)


def times(matrix, value):
    return jnp.dot(matrix, value, preferred_element_type=jnp.float32).astype(jnp.bfloat16)


def sampled(sampling, traces):
    return jnp.einsum(
        "pc,tp->ct", sampling, traces, preferred_element_type=jnp.float32
    ).astype(jnp.bfloat16)


def evaluated(coeffs, evaluation):
    return jnp.einsum(
        "ct,cp->tp", coeffs, evaluation, preferred_element_type=jnp.float32
    ).astype(jnp.bfloat16)


def after(value, earlier):
    return value if earlier is None else lax.optimization_barrier((value, earlier))[0]


def all_hops():
    low_bits = lax.axis_size("sub").bit_length() - 1
    high_bits = lax.axis_size("bfly").bit_length() - 1
    return [("sub", bit) for bit in range(low_bits)] + [("bfly", bit) for bit in range(high_bits)]


def full_width(traces, sampling, skeleton, compress, evaluation):
    rank = skeleton.shape[-1]
    columns = picked_columns(compress, skeleton)
    full = jnp.concatenate([real_form(columns[..., :rank]), real_form(columns[..., rank:])], 2)
    coeffs = sampled_apart(sampling, traces)
    for level, hop in enumerate(all_hops()):
        partner = from_partner(coeffs, hop)
        coeffs = times(full[level], jnp.concatenate([coeffs, partner], 0))
    return evaluated(coeffs, evaluation)


def sequence(pieces, levels):
    def turn(at):
        level, piece = at
        if piece < FULL_PIECES:
            if level == 0:
                return piece
            late = 2 if level == levels and piece else 0
            return 3 * level + 1.5 * piece + late
        if level == 0:
            return 3.5 if piece == 2 else 6.5 if piece == 3 else 11.02 + 3.05 * (piece - 4)
        late = 3 if level == levels else 0
        return 3 * level + 5 + 3.05 * (piece - 2) + late

    return sorted(
        [(level, piece) for level in range(levels + 1) for piece in range(pieces)], key=turn
    )


def local(traces, sampling, skeleton, compress, evaluation):
    hops = all_hops()
    levels = len(hops)
    wide = lax.axis_size("sub").bit_length() - 1
    rank = skeleton.shape[-1]
    room = rank * ROOM_SIXTEENTHS // 16
    unit = traces.shape[0] // sum(SHARES)
    pieces = len(SHARES)
    starts = [unit * sum(SHARES[:i]) for i in range(pieces + 1)]
    full, small, extra, coeffs = first(skeleton, compress, sampling, traces, wide, room, starts[1])
    sampling, evaluation = sampling[0], evaluation[0]
    most_here = lax.broadcasted_iota(jnp.int32, extra.shape[1:], 1) >= rank

    def compact(level, piece):
        return piece >= FULL_PIECES and level >= wide

    inputs, partners, theirs, done = {}, {}, {}, [None] * pieces
    previous, known = None, None
    for level, piece in sequence(pieces, levels):
        count = starts[piece + 1] - starts[piece]
        if level == 0:
            own = coeffs
            if piece > 0:
                block = traces[starts[piece] : starts[piece + 1]]
                own = sampled(after(sampling, coeffs if piece == 1 else previous), block)
        else:
            arrived = after(partners[piece], previous)
            if piece == 0 and level - 1 >= wide:
                known = arrived[:, count:]
                theirs[level - 1] = known[:room, :rank]
            value = jnp.concatenate([inputs[piece], arrived[:, :count]], 0)
            matrix = full[level - 1]
            if compact(level - 1, piece):
                value = jnp.pad(value, ((0, full.shape[2] - value.shape[0]), (0, 0)))
                matrix = small[level - 1]
            own = times(matrix, value)
        if level == levels:
            done[piece] = evaluated(own, evaluation)
            continue
        outgoing = own
        if compact(level, piece):
            outgoing = times(compact_rows(matrix, theirs[level]), value)
        if piece == 0 and level >= wide:
            block = extra[level]
            if known is not None:
                block = jnp.where(most_here, jnp.maximum(block, known), block)
            outgoing = jnp.concatenate([outgoing, block], 1)
        inputs[piece] = own
        partners[piece] = from_partner(outgoing, hops[level])
        previous = outgoing
    most = after(jnp.maximum(extra[levels - 1], known)[:8, rank:], previous)
    for hop in hops[:wide]:
        most = jnp.maximum(most, from_partner(most, hop))
    quick = jnp.concatenate(done, 0)
    return lax.cond(
        most[0, 0] > room,
        lambda: full_width(traces, sampling, skeleton[0], compress[0], evaluation),
        lambda: quick,
    )


def solution(mesh):
    placed = (
        P(("shots", "tr"), ("bfly", "sub")),
        P(("bfly", "sub"), None, None),
        P(("bfly", "sub"), None, None),
        P(("bfly", "sub"), None, None, None),
        P(("bfly", "sub"), None, None),
    )
    return jax.shard_map(
        local,
        mesh=mesh,
        in_specs=placed,
        out_specs=P(("shots", "tr"), ("bfly", "sub")),
        check_vma=False,
    )
```

```python
import jax
import jax.numpy as jnp
from jax import lax
from jax.experimental import pallas as pl
from jax.experimental.pallas import tpu as pltpu
from jax.sharding import PartitionSpec as P

SHARES = (2, 6, 8, 9, 7)
POOL_EIGHTHS = 5

UP = [(0, 1), (3, 2)]
MIDDLE = [(1, 2), (2, 1)]
DOWN = [(1, 0), (2, 3)]


def route(axis, apart):
    count = lax.axis_size(axis)
    pairs = []
    for low in range(count):
        high = low | 1 << apart
        if high != low and high < count:
            pairs += [(low, high), (high, low)]
    return pairs


def from_partner(block, hop):
    return lax.ppermute(block, hop[0], route(*hop))


def across(left, right):
    return lax.dot_general(left, right, (((1,), (1,)), ((), ())), preferred_element_type=jnp.float32)


def one_hot(condition):
    return jnp.where(condition, 1.0, 0.0).astype(jnp.bfloat16)


def sampled_block(sampling, rows):
    turned = sampling.astype(jnp.float32).T.astype(jnp.bfloat16)
    return across(turned, rows).astype(jnp.bfloat16)


def tables_kernel(
    wide, pool, own_skeleton_hbm, own_compress_hbm, out_skeleton_hbm, out_compress_hbm,
    low_ref, both_ref, last_ref, last_full_ref, extra_ref,
    own_skeleton, own_compress, out_skeleton, out_compress, arrived,
):
    loads = [
        pltpu.make_async_copy(own_skeleton_hbm, own_skeleton, arrived.at[0]),
        pltpu.make_async_copy(own_compress_hbm, own_compress, arrived.at[1]),
        pltpu.make_async_copy(out_skeleton_hbm, out_skeleton, arrived.at[2]),
        pltpu.make_async_copy(out_compress_hbm, out_compress, arrived.at[3]),
    ]
    for load in loads:
        load.start()
    for load in loads:
        load.wait()
    rank = own_skeleton.shape[-1]
    width = 2 * rank
    f32, i32 = jnp.float32, jnp.int32
    twice = one_hot(
        lax.broadcasted_iota(i32, (width, rank), 0) % rank == lax.broadcasted_iota(i32, (width, rank), 1)
    )
    square_row = lax.broadcasted_iota(i32, (width, width), 0)
    square_lane = lax.broadcasted_iota(i32, (width, width), 1)
    earlier = one_hot(square_lane < square_row % rank)
    column = lax.broadcasted_iota(i32, (2 * width, width), 0)
    real_entry = lax.broadcasted_iota(i32, (2 * width, width), 1) < rank
    coefficient = column % rank

    def entries(skeleton, level):
        row = jnp.broadcast_to(skeleton[level].astype(f32), (8, rank)).astype(jnp.bfloat16)
        return across(row, twice)[:1].astype(i32)

    def halves(matrix, match, imag):
        same = real_entry != imag
        real = jnp.where(match & same, jnp.where(imag, -1.0, 1.0), 0.0).astype(jnp.bfloat16)
        turned = one_hot(match & jnp.logical_not(same))
        return across(matrix, real).astype(jnp.bfloat16), across(matrix, turned).astype(jnp.bfloat16)

    by_box_imag = column % width >= rank
    second_box = column >= width
    for level in range(wide):
        match = entries(own_skeleton, level) == coefficient + jnp.where(second_box, rank, 0)
        low_ref[level, :rank], low_ref[level, rank:] = halves(own_compress[0, level], match, by_box_imag)

    boxes = ((own_skeleton, own_compress), (out_skeleton, out_compress))
    for box, (skeleton, compress) in enumerate(boxes):
        partner = second_box if box == 0 else jnp.logical_not(second_box)
        match = entries(skeleton, wide) == coefficient + jnp.where(partner, rank, 0)
        real, imag = halves(compress[0, wide], match, by_box_imag)
        both_ref[box * rank : (box + 1) * rank] = real
        both_ref[width + box * rank : width + (box + 1) * rank] = imag

    by_part_imag = column >= width
    column_box = column % width // rank
    slot_imag = column >= pool
    slot_column = jnp.where(slot_imag, column - pool, column)
    used = jnp.zeros((1, 1), f32)
    places = jnp.zeros((width, width), f32)
    for box, (skeleton, compress) in enumerate(boxes):
        entry = entries(skeleton, wide + 1)
        matrix = compress[0, wide + 1]
        picked = jnp.where(entry >= rank, 1.0, 0.0)
        slot = across(jnp.broadcast_to(picked, (8, width)).astype(jnp.bfloat16), earlier)[:1]
        slot = jnp.where(entry >= rank, slot + used, -1.0).astype(i32)
        used = used + jnp.sum(picked, axis=1, keepdims=True) * 0.5
        rows = slice(box * width, box * width + rank)
        turned_rows = slice(box * width + rank, (box + 1) * width)
        match = (entry == coefficient) & (column_box == box)
        real, imag = halves(matrix, match, by_part_imag)
        last_ref[rows, : 2 * width] = real
        last_ref[turned_rows, : 2 * width] = imag
        last_full_ref[rows, : 2 * width] = real
        last_full_ref[turned_rows, : 2 * width] = imag
        real, imag = halves(matrix, slot == slot_column, slot_imag)
        last_ref[rows, 2 * width :] = real
        last_ref[turned_rows, 2 * width :] = imag
        match = (entry - rank == coefficient) & (column_box == 1 - box)
        real, imag = halves(matrix, match, by_part_imag)
        last_full_ref[rows, 2 * width :] = real
        last_full_ref[turned_rows, 2 * width :] = imag
        once = square_lane < rank
        here = entry - rank == square_row - (1 - box) * rank
        here = here & (entry >= rank) & (square_row // rank == 1 - box)
        places = places + across(one_hot(once & (slot == square_row)), one_hot(once & here))
    extra_ref[:width] = places.astype(jnp.bfloat16)
    extra_ref[width:] = jnp.broadcast_to(used, (width, width)).astype(jnp.bfloat16)


def tables(skeleton, compress, out_skeleton, out_compress, wide, pool):
    levels, rank = skeleton.shape[1:]
    width = 2 * rank
    out_shape = [
        jax.ShapeDtypeStruct(shape, jnp.bfloat16)
        for shape in (
            (wide, width, 2 * width),
            (2 * width, 2 * width),
            (2 * width, 4 * width),
            (2 * width, 4 * width),
            (2 * width, width),
        )
    ]
    small = [pltpu.VMEM((levels, 1, rank), jnp.int32), pltpu.VMEM(compress.shape, jnp.bfloat16)]
    return pl.pallas_call(
        lambda *refs: tables_kernel(wide, pool, *refs),
        out_shape=out_shape,
        in_specs=[pl.BlockSpec(memory_space=pltpu.HBM)] * 4,
        out_specs=[pl.BlockSpec(memory_space=pltpu.VMEM)] * 5,
        scratch_shapes=small + small + [pltpu.SemaphoreType.DMA((4,))],
        compiler_params=pltpu.CompilerParams(vmem_limit_bytes=16 * 1024 * 1024),
        cost_estimate=pl.CostEstimate(flops=50_000_000, bytes_accessed=1_000_000, transcendentals=0),
        name="tables",
    )(skeleton.transpose(1, 0, 2), compress, out_skeleton.transpose(1, 0, 2), out_compress)


def sampled_apart(sampling, traces):
    count, width = traces.shape
    block = count // 8

    def kernel(sampling_ref, rows_ref, coeffs_ref):
        coeffs_ref[...] = sampled_block(sampling_ref[...], rows_ref[...])

    return pl.pallas_call(
        kernel,
        grid=(count // block,),
        out_shape=jax.ShapeDtypeStruct((sampling.shape[1], count), jnp.bfloat16),
        in_specs=[
            pl.BlockSpec(sampling.shape, lambda i: (0, 0)),
            pl.BlockSpec((block, width), lambda i: (i, 0)),
        ],
        out_specs=pl.BlockSpec((sampling.shape[1], block), lambda i: (0, i)),
        compiler_params=pltpu.CompilerParams(vmem_limit_bytes=63 * 1024 * 1024),
        name="sampled_apart",
    )(sampling, traces)


def picked_columns(compress, skeleton):
    rank = skeleton.shape[-1]
    places = lax.broadcasted_iota(jnp.int32, (1, 1, 2 * rank), 2)
    chooser = (skeleton[:, :, None] == places).astype(jnp.bfloat16)
    stacked = jnp.concatenate([compress[:, :, :rank], compress[:, :, rank:]], 1)
    return jnp.einsum(
        "ljk,lki->lji", stacked, chooser, preferred_element_type=jnp.float32
    ).astype(jnp.bfloat16)


def real_form(both):
    rank = both.shape[1] // 2
    turned = jnp.concatenate([-both[:, rank:], both[:, :rank]], 1)
    return jnp.concatenate([both, turned], 2)


def times(matrix, value):
    return jnp.dot(matrix, value, preferred_element_type=jnp.float32).astype(jnp.bfloat16)


def sampled(sampling, traces):
    return jnp.einsum(
        "pc,tp->ct", sampling, traces, preferred_element_type=jnp.float32
    ).astype(jnp.bfloat16)


def evaluated(coeffs, evaluation):
    return jnp.einsum(
        "ct,cp->tp", coeffs, evaluation, preferred_element_type=jnp.float32
    ).astype(jnp.bfloat16)


def after(value, earlier):
    return value if earlier is None else lax.optimization_barrier((value, earlier))[0]


def all_hops():
    low_bits = lax.axis_size("sub").bit_length() - 1
    high_bits = lax.axis_size("bfly").bit_length() - 1
    return [("sub", bit) for bit in range(low_bits)] + [("bfly", bit) for bit in range(high_bits)]


def full_width(traces, sampling, skeleton, compress, evaluation):
    rank = skeleton.shape[-1]
    columns = picked_columns(compress, skeleton)
    full = jnp.concatenate([real_form(columns[..., :rank]), real_form(columns[..., rank:])], 2)
    coeffs = sampled_apart(sampling, traces)
    for level, hop in enumerate(all_hops()):
        partner = from_partner(coeffs, hop)
        coeffs = times(full[level], jnp.concatenate([coeffs, partner], 0))
    return evaluated(coeffs, evaluation)


def sequence(pieces, middle):
    def turn(at):
        stage, piece = at
        if stage == 0:
            return max(0, 2 * piece - 1.5)
        ahead = 0.45 if stage == middle and piece > 1 else 0
        late = 2.05 if stage == middle + 2 else 0
        return 2 * stage + 2.1 * piece - ahead + late

    return sorted(
        [(stage, piece) for stage in range(middle + 3) for piece in range(pieces)], key=turn
    )


def local(traces, sampling, skeleton, compress, evaluation):
    if lax.axis_size("bfly") != 4:
        return full_width(traces, sampling[0], skeleton[0], compress[0], evaluation[0])
    hops = all_hops()
    wide = len(hops) - 2
    middle = wide + 1
    rank = skeleton.shape[-1]
    width = 2 * rank
    pool = width * POOL_EIGHTHS // 8
    unit = traces.shape[0] // sum(SHARES)
    pieces = len(SHARES)
    starts = [unit * sum(SHARES[:i]) for i in range(pieces + 1)]
    place = lax.axis_index("bfly")
    inner = (place == 1) | (place == 2)

    out_compress = lax.ppermute(compress, "bfly", UP)
    out_skeleton = lax.ppermute(skeleton, "bfly", UP)
    low, both, last, last_full, extra = tables(
        skeleton, compress, out_skeleton, out_compress, wide, pool
    )
    sampling, evaluation = sampling[0], evaluation[0]

    inputs, arrivals, done = {}, {}, [None] * pieces
    previous, sending, most = None, None, None
    for stage, piece in sequence(pieces, middle):
        count = starts[piece + 1] - starts[piece]
        arrived = after(arrivals[piece], previous) if stage else None
        if stage == 0:
            block = traces[starts[piece] : starts[piece + 1]]
            own = outgoing = sampled(after(sampling, previous if piece > 1 else None), block)
        elif stage <= wide:
            own = outgoing = times(low[stage - 1], jnp.concatenate([inputs[piece], arrived], 0))
        elif stage == middle:
            value = jnp.concatenate([inputs[piece], arrived], 0)
            own = times(both, value)
            if piece == 0:
                outgoing = jnp.concatenate([own, extra], 1)
            else:
                outgoing = times(sending, value)
        elif stage == middle + 1:
            if piece == 0:
                theirs = arrived[:pool, count:]
                sending = jnp.concatenate(
                    [
                        jnp.dot(theirs, half, preferred_element_type=jnp.float32)
                        for half in (both[:width], both[width:])
                    ],
                    0,
                ).astype(jnp.bfloat16)
                most = jnp.maximum(extra[width : width + 8], arrived[width : width + 8, count:])
                value = jnp.concatenate([inputs[piece], arrived[:, :count]], 0)
                matrix = last_full
            else:
                value = jnp.concatenate([inputs[piece], arrived], 0)
                value = jnp.pad(value, ((0, 4 * width - value.shape[0]), (0, 0)))
                matrix = last
            outgoing = times(matrix[width:], value)
            own = times(matrix[:width], value)
        else:
            done[piece] = evaluated(jnp.where(inner, inputs[piece], arrived), evaluation)
            continue
        inputs[piece] = own
        if stage < wide:
            arrivals[piece] = from_partner(outgoing, hops[stage])
        else:
            arrivals[piece] = lax.ppermute(outgoing, "bfly", (UP, MIDDLE, DOWN)[stage - wide])
        previous = outgoing
        if stage == middle and piece == pieces - 1:
            most = after(most, previous)
            for hop in hops[:wide]:
                most = jnp.maximum(most, from_partner(most, hop))
            most = jnp.where(inner, most, lax.ppermute(most, "bfly", DOWN))
    quick = jnp.concatenate(done, 0)
    return lax.cond(
        most[0, 0] > pool,
        lambda: full_width(traces, sampling, skeleton[0], compress[0], evaluation),
        lambda: quick,
    )


def solution(mesh):
    placed = (
        P(("shots", "tr"), ("bfly", "sub")),
        P(("bfly", "sub"), None, None),
        P(("bfly", "sub"), None, None),
        P(("bfly", "sub"), None, None, None),
        P(("bfly", "sub"), None, None),
    )
    return jax.shard_map(
        local,
        mesh=mesh,
        in_specs=placed,
        out_specs=P(("shots", "tr"), ("bfly", "sub")),
        check_vma=False,
    )
```

```python
import jax
import jax.numpy as jnp
from jax import lax
from jax.experimental import pallas as pl
from jax.experimental.pallas import tpu as pltpu
from jax.sharding import PartitionSpec as P

SHARES = (2, 7, 11, 8, 4)
FULL_PIECES = 1
ORDER = (
    (0, 0), (0, 1), (1, 0), (0, 2), (2, 0), (1, 1), (0, 3), (3, 0), (1, 2), (2, 1), (1, 3), (2, 2),
    (0, 4), (3, 1), (1, 4), (2, 3), (2, 4), (3, 2), (3, 3), (3, 4),
)
KERNEL_VMEM = 16 * 1024 * 1024
ROOM_SIXTEENTHS = 11


def route(axis, apart):
    count = lax.axis_size(axis)
    pairs = []
    for low in range(count):
        high = low | 1 << apart
        if high != low and high < count:
            pairs += [(low, high), (high, low)]
    return pairs


def from_partner(block, hop):
    return lax.ppermute(block, hop[0], route(*hop))


def across(left, right):
    return lax.dot_general(left, right, (((1,), (1,)), ((), ())), preferred_element_type=jnp.float32)


def one_hot(condition):
    return jnp.where(condition, 1.0, 0.0).astype(jnp.bfloat16)


def sampled_block(sampling, rows):
    turned = sampling.astype(jnp.float32).T.astype(jnp.bfloat16)
    return across(turned, rows).astype(jnp.bfloat16)


def first_kernel(
    wide, room, count, skeleton_hbm, compress_hbm, sampling_hbm, traces_hbm,
    full_ref, small_ref, extra_ref, coeffs_ref,
    skeleton_ref, compress_ref, sampling_ref, rows_ref, arrived,
):
    loads = [
        pltpu.make_async_copy(skeleton_hbm, skeleton_ref, arrived.at[0]),
        pltpu.make_async_copy(compress_hbm, compress_ref, arrived.at[1]),
        pltpu.make_async_copy(sampling_hbm, sampling_ref, arrived.at[2]),
        pltpu.make_async_copy(traces_hbm.at[pl.ds(0, count)], rows_ref, arrived.at[3]),
    ]
    for load in loads:
        load.start()
    for load in loads:
        load.wait()
    coeffs_ref[...] = sampled_block(sampling_ref[0], rows_ref[...])
    levels, rank = skeleton_ref.shape[0], skeleton_ref.shape[-1]
    width = 2 * rank
    f32, i32 = jnp.float32, jnp.int32
    k = lax.broadcasted_iota(i32, (width, width), 1)
    twice = one_hot(lax.broadcasted_iota(i32, (width, rank), 0) % rank == lax.broadcasted_iota(i32, (width, rank), 1))
    earlier = one_hot(
        (lax.broadcasted_iota(i32, (width, width), 1) < lax.broadcasted_iota(i32, (width, width), 0) % rank)
    )
    column = lax.broadcasted_iota(i32, (2 * width, width), 0)
    is_real_entry = lax.broadcasted_iota(i32, (2 * width, width), 1) < rank
    partner_column = column >= width
    imag_column = column % width >= rank
    coefficient = column % rank + jnp.where(partner_column, rank, 0)
    slot_column = column - width
    slot_imag = slot_column >= room
    slot_of_column = jnp.where(slot_imag, slot_column - room, slot_column)
    row = lax.broadcasted_iota(i32, (width, width), 0)
    most = jnp.zeros((1, 1), f32)
    for level in range(levels):
        entry = jnp.broadcast_to(skeleton_ref[level].astype(f32), (8, rank)).astype(jnp.bfloat16)
        entry = across(entry, twice)[:1]
        picked = jnp.where(entry >= rank, 1.0, 0.0)
        slot = across(jnp.broadcast_to(picked, (8, width)).astype(jnp.bfloat16), earlier)[:1].astype(i32)
        entry = entry.astype(i32)
        from_partner_entry = entry >= rank
        matrix = compress_ref[0, level]

        def halves(match, imag):
            same = is_real_entry != imag
            real = jnp.where(match & same, jnp.where(imag, -1.0, 1.0), 0.0).astype(jnp.bfloat16)
            turned = one_hot(match & jnp.logical_not(same))
            return across(matrix, real).astype(jnp.bfloat16), across(matrix, turned).astype(jnp.bfloat16)

        match = entry == coefficient
        full_ref[level, :rank], full_ref[level, rank:] = halves(match, imag_column)
        compacted = (slot == slot_of_column) & from_partner_entry
        match = (match & jnp.logical_not(partner_column)) | (compacted & partner_column)
        imag = (imag_column & jnp.logical_not(partner_column)) | (slot_imag & partner_column)
        small_ref[level, :rank], small_ref[level, rank:] = halves(match, imag)
        once = (k < rank) & from_partner_entry
        places = across(one_hot(once & (slot == row)), one_hot(once & (entry - rank == row)))
        extra_ref[level] = places.astype(jnp.bfloat16)
        if level >= wide:
            most = jnp.maximum(most, jnp.sum(picked, axis=1, keepdims=True) * 0.5)
    for level in range(wide, levels):
        extra_ref[level] = jnp.where(k < rank, extra_ref[level].astype(f32), most).astype(jnp.bfloat16)


def first(skeleton, compress, sampling, traces, wide, room, count):
    levels, rank = skeleton.shape[1:]
    shape = (levels, 2 * rank, 4 * rank)
    width = sampling.shape[-1]
    whole = pl.BlockSpec(memory_space=pltpu.VMEM)
    return pl.pallas_call(
        lambda *refs: first_kernel(wide, room, count, *refs),
        out_shape=[
            jax.ShapeDtypeStruct(shape, jnp.bfloat16),
            jax.ShapeDtypeStruct(shape, jnp.bfloat16),
            jax.ShapeDtypeStruct((levels, 2 * rank, 2 * rank), jnp.bfloat16),
            jax.ShapeDtypeStruct((width, count), jnp.bfloat16),
        ],
        in_specs=[pl.BlockSpec(memory_space=pltpu.HBM)] * 4,
        out_specs=[whole] * 4,
        scratch_shapes=[
            pltpu.VMEM((levels, 1, rank), jnp.int32),
            pltpu.VMEM(compress.shape, jnp.bfloat16),
            pltpu.VMEM(sampling.shape, jnp.bfloat16),
            pltpu.VMEM((count, traces.shape[1]), jnp.bfloat16),
            pltpu.SemaphoreType.DMA((4,)),
        ],
        compiler_params=pltpu.CompilerParams(vmem_limit_bytes=KERNEL_VMEM),
        cost_estimate=pl.CostEstimate(flops=50_000_000, bytes_accessed=600_000, transcendentals=0),
        name="first",
    )(skeleton.transpose(1, 0, 2), compress, sampling, traces)


def sampled_apart(sampling, traces):
    count, width = traces.shape
    block = count // 8

    def kernel(sampling_ref, rows_ref, coeffs_ref):
        coeffs_ref[...] = sampled_block(sampling_ref[...], rows_ref[...])

    return pl.pallas_call(
        kernel,
        grid=(count // block,),
        out_shape=jax.ShapeDtypeStruct((sampling.shape[1], count), jnp.bfloat16),
        in_specs=[
            pl.BlockSpec(sampling.shape, lambda i: (0, 0)),
            pl.BlockSpec((block, width), lambda i: (i, 0)),
        ],
        out_specs=pl.BlockSpec((sampling.shape[1], block), lambda i: (0, i)),
        compiler_params=pltpu.CompilerParams(vmem_limit_bytes=63 * 1024 * 1024),
        name="sampled_apart",
    )(sampling, traces)


def picked_columns(compress, skeleton):
    rank = skeleton.shape[-1]
    places = lax.broadcasted_iota(jnp.int32, (1, 1, 2 * rank), 2)
    chooser = (skeleton[:, :, None] == places).astype(jnp.bfloat16)
    stacked = jnp.concatenate([compress[:, :, :rank], compress[:, :, rank:]], 1)
    return jnp.einsum(
        "ljk,lki->lji", stacked, chooser, preferred_element_type=jnp.float32
    ).astype(jnp.bfloat16)


def real_form(both):
    rank = both.shape[1] // 2
    turned = jnp.concatenate([-both[:, rank:], both[:, :rank]], 1)
    return jnp.concatenate([both, turned], 2)


def compact_rows(matrix, slot):
    rank = slot.shape[1]
    parts = [
        jnp.dot(slot, half, preferred_element_type=jnp.float32)
        for half in (matrix[:rank], matrix[rank:])
    ]
    return jnp.concatenate(parts, 0).astype(jnp.bfloat16)


def times(matrix, value):
    return jnp.dot(matrix, value, preferred_element_type=jnp.float32).astype(jnp.bfloat16)


def sampled(sampling, traces):
    return jnp.einsum(
        "pc,tp->ct", sampling, traces, preferred_element_type=jnp.float32
    ).astype(jnp.bfloat16)


def evaluated(coeffs, evaluation):
    return jnp.einsum(
        "ct,cp->tp", coeffs, evaluation, preferred_element_type=jnp.float32
    ).astype(jnp.bfloat16)


def after(value, earlier):
    return value if earlier is None else lax.optimization_barrier((value, earlier))[0]


def all_hops():
    low_bits = lax.axis_size("sub").bit_length() - 1
    high_bits = lax.axis_size("bfly").bit_length() - 1
    return [("sub", bit) for bit in range(low_bits)] + [("bfly", bit) for bit in range(high_bits)]


def full_width(traces, sampling, skeleton, compress, evaluation):
    rank = skeleton.shape[-1]
    columns = picked_columns(compress, skeleton)
    full = jnp.concatenate([real_form(columns[..., :rank]), real_form(columns[..., rank:])], 2)
    coeffs = sampled_apart(sampling, traces)
    for level, hop in enumerate(all_hops()):
        partner = from_partner(coeffs, hop)
        coeffs = times(full[level], jnp.concatenate([coeffs, partner], 0))
    return evaluated(coeffs, evaluation)


def local(traces, sampling, skeleton, compress, evaluation):
    hops = all_hops()
    levels = len(hops)
    if levels != max(level for level, _ in ORDER):
        return full_width(traces, sampling[0], skeleton[0], compress[0], evaluation[0])
    wide = lax.axis_size("sub").bit_length() - 1
    rank = skeleton.shape[-1]
    room = rank * ROOM_SIXTEENTHS // 16
    unit = traces.shape[0] // sum(SHARES)
    pieces = len(SHARES)
    starts = [unit * sum(SHARES[:i]) for i in range(pieces + 1)]
    full, small, extra, coeffs = first(skeleton, compress, sampling, traces, wide, room, starts[1])
    sampling, evaluation = sampling[0], evaluation[0]
    most_here = lax.broadcasted_iota(jnp.int32, extra.shape[1:], 1) >= rank

    def compact(level, piece):
        return piece >= FULL_PIECES and level >= wide

    inputs, partners, theirs, done = {}, {}, {}, [None] * pieces
    previous, known = None, None
    for level, piece in ORDER:
        count = starts[piece + 1] - starts[piece]
        if level == 0:
            own = coeffs
            if piece > 0:
                block = traces[starts[piece] : starts[piece + 1]]
                own = sampled(after(sampling, coeffs if piece == 1 else previous), block)
        else:
            arrived = after(partners[piece], previous)
            if piece == 0 and level - 1 >= wide:
                known = arrived[:, count:]
                theirs[level - 1] = known[:room, :rank]
            value = jnp.concatenate([inputs[piece], arrived[:, :count]], 0)
            matrix = full[level - 1]
            if compact(level - 1, piece):
                value = jnp.pad(value, ((0, full.shape[2] - value.shape[0]), (0, 0)))
                matrix = small[level - 1]
            own = times(matrix, value)
        if level == levels:
            done[piece] = previous = evaluated(own, evaluation)
            continue
        outgoing = own
        if compact(level, piece):
            outgoing = times(compact_rows(matrix, theirs[level]), value)
        if piece == 0 and level >= wide:
            block = extra[level]
            if known is not None:
                block = jnp.where(most_here, jnp.maximum(block, known), block)
            outgoing = jnp.concatenate([outgoing, block], 1)
        inputs[piece] = own
        partners[piece] = from_partner(outgoing, hops[level])
        previous = outgoing
    most = after(jnp.maximum(extra[levels - 1], known)[:8, rank:], previous)
    for hop in hops[:wide]:
        most = jnp.maximum(most, from_partner(most, hop))
    quick = jnp.concatenate(done, 0)
    return lax.cond(
        most[0, 0] > room,
        lambda: full_width(traces, sampling, skeleton[0], compress[0], evaluation),
        lambda: quick,
    )


def solution(mesh):
    placed = (
        P(("shots", "tr"), ("bfly", "sub")),
        P(("bfly", "sub"), None, None),
        P(("bfly", "sub"), None, None),
        P(("bfly", "sub"), None, None, None),
        P(("bfly", "sub"), None, None),
    )
    return jax.shard_map(
        local,
        mesh=mesh,
        in_specs=placed,
        out_specs=P(("shots", "tr"), ("bfly", "sub")),
        check_vma=False,
    )
```

```python
import jax
import jax.numpy as jnp
from jax import lax
from jax.experimental import pallas as pl
from jax.experimental.pallas import tpu as pltpu
from jax.sharding import PartitionSpec as P

SHARES = (2, 5, 9, 10, 6)
FULL_PIECES = 2
EARLY_PIECES = 3
COUNT_PIECE = 2
ORDER = (
    (0, 0), (0, 1), (0, 2), (1, 0), (0, 3), (1, 1), (2, 0), (1, 2), (2, 1), (3, 0), (0, 4), (1, 3),
    (2, 2), (1, 4), (2, 3), (3, 1), (2, 4), (3, 2), (3, 3), (3, 4),
)
KERNEL_VMEM = 16 * 1024 * 1024
ROOM_SIXTEENTHS = 11


def route(axis, apart):
    count = lax.axis_size(axis)
    pairs = []
    for low in range(count):
        high = low | 1 << apart
        if high != low and high < count:
            pairs += [(low, high), (high, low)]
    return pairs


def from_partner(block, hop):
    return lax.ppermute(block, hop[0], route(*hop))


def across(left, right):
    return lax.dot_general(left, right, (((1,), (1,)), ((), ())), preferred_element_type=jnp.float32)


def one_hot(condition):
    return jnp.where(condition, 1.0, 0.0).astype(jnp.bfloat16)


def sampled_block(sampling, rows):
    turned = sampling.astype(jnp.float32).T.astype(jnp.bfloat16)
    return across(turned, rows).astype(jnp.bfloat16)


def early_kernel(starts, sampling_hbm, traces_hbm, *refs):
    pieces = len(starts) - 1
    outs, (sampling_ref, rows_ref, arrived) = refs[:pieces], refs[pieces:]
    loads = [pltpu.make_async_copy(sampling_hbm, sampling_ref, arrived.at[pieces])]
    for i in range(pieces):
        span = pl.ds(starts[i], starts[i + 1] - starts[i])
        loads.append(pltpu.make_async_copy(traces_hbm.at[span], rows_ref.at[span], arrived.at[i]))
    for load in loads:
        load.start()
    loads[0].wait()
    for i in range(pieces):
        loads[i + 1].wait()
        span = pl.ds(starts[i], starts[i + 1] - starts[i])
        outs[i][...] = sampled_block(sampling_ref[0], rows_ref[span])


def early(sampling, traces, starts):
    pieces = len(starts) - 1
    width = sampling.shape[-1]
    total = starts[-1]
    return pl.pallas_call(
        lambda *refs: early_kernel(starts, *refs),
        out_shape=[
            jax.ShapeDtypeStruct((width, starts[i + 1] - starts[i]), jnp.bfloat16) for i in range(pieces)
        ],
        in_specs=[pl.BlockSpec(memory_space=pltpu.HBM)] * 2,
        out_specs=[pl.BlockSpec(memory_space=pltpu.VMEM)] * pieces,
        scratch_shapes=[
            pltpu.VMEM(sampling.shape, jnp.bfloat16),
            pltpu.VMEM((total, traces.shape[1]), jnp.bfloat16),
            pltpu.SemaphoreType.DMA((pieces + 1,)),
        ],
        compiler_params=pltpu.CompilerParams(vmem_limit_bytes=KERNEL_VMEM),
        cost_estimate=pl.CostEstimate(
            flops=2 * total * width * width, bytes_accessed=4 * total * width, transcendentals=0
        ),
        name="early",
    )(sampling, traces)


def tables_kernel(
    wide, room, skeleton_hbm, compress_hbm, full_ref, small_ref, extra_ref,
    skeleton_ref, compress_ref, arrived,
):
    loads = [
        pltpu.make_async_copy(skeleton_hbm, skeleton_ref, arrived.at[0]),
        pltpu.make_async_copy(compress_hbm, compress_ref, arrived.at[1]),
    ]
    for load in loads:
        load.start()
    for load in loads:
        load.wait()
    levels, rank = skeleton_ref.shape[0], skeleton_ref.shape[-1]
    width = 2 * rank
    f32, i32 = jnp.float32, jnp.int32
    k = lax.broadcasted_iota(i32, (width, width), 1)
    twice = one_hot(lax.broadcasted_iota(i32, (width, rank), 0) % rank == lax.broadcasted_iota(i32, (width, rank), 1))
    earlier = one_hot(
        (lax.broadcasted_iota(i32, (width, width), 1) < lax.broadcasted_iota(i32, (width, width), 0) % rank)
    )
    column = lax.broadcasted_iota(i32, (2 * width, width), 0)
    is_real_entry = lax.broadcasted_iota(i32, (2 * width, width), 1) < rank
    partner_column = column >= width
    imag_column = column % width >= rank
    coefficient = column % rank + jnp.where(partner_column, rank, 0)
    slot_column = column - width
    slot_imag = slot_column >= room
    slot_of_column = jnp.where(slot_imag, slot_column - room, slot_column)
    row = lax.broadcasted_iota(i32, (width, width), 0)
    most = jnp.zeros((1, 1), f32)
    for level in range(levels):
        entry = jnp.broadcast_to(skeleton_ref[level].astype(f32), (8, rank)).astype(jnp.bfloat16)
        entry = across(entry, twice)[:1]
        picked = jnp.where(entry >= rank, 1.0, 0.0)
        slot = across(jnp.broadcast_to(picked, (8, width)).astype(jnp.bfloat16), earlier)[:1].astype(i32)
        entry = entry.astype(i32)
        from_partner_entry = entry >= rank
        matrix = compress_ref[0, level]

        def halves(match, imag):
            same = is_real_entry != imag
            real = jnp.where(match & same, jnp.where(imag, -1.0, 1.0), 0.0).astype(jnp.bfloat16)
            turned = one_hot(match & jnp.logical_not(same))
            return across(matrix, real).astype(jnp.bfloat16), across(matrix, turned).astype(jnp.bfloat16)

        match = entry == coefficient
        full_ref[level, :rank], full_ref[level, rank:] = halves(match, imag_column)
        compacted = (slot == slot_of_column) & from_partner_entry
        match = (match & jnp.logical_not(partner_column)) | (compacted & partner_column)
        imag = (imag_column & jnp.logical_not(partner_column)) | (slot_imag & partner_column)
        small_ref[level, :rank], small_ref[level, rank:] = halves(match, imag)
        once = (k < rank) & from_partner_entry
        places = across(one_hot(once & (slot == row)), one_hot(once & (entry - rank == row)))
        extra_ref[level] = places.astype(jnp.bfloat16)
        if level >= wide:
            most = jnp.maximum(most, jnp.sum(picked, axis=1, keepdims=True) * 0.5)
    for level in range(wide, levels):
        extra_ref[level] = jnp.where(k < rank, extra_ref[level].astype(f32), most).astype(jnp.bfloat16)


def tables(skeleton, compress, wide, room):
    levels, rank = skeleton.shape[1:]
    shape = (levels, 2 * rank, 4 * rank)
    return pl.pallas_call(
        lambda *refs: tables_kernel(wide, room, *refs),
        out_shape=[
            jax.ShapeDtypeStruct(shape, jnp.bfloat16),
            jax.ShapeDtypeStruct(shape, jnp.bfloat16),
            jax.ShapeDtypeStruct((levels, 2 * rank, 2 * rank), jnp.bfloat16),
        ],
        in_specs=[pl.BlockSpec(memory_space=pltpu.HBM)] * 2,
        out_specs=[pl.BlockSpec(memory_space=pltpu.VMEM)] * 3,
        scratch_shapes=[
            pltpu.VMEM((levels, 1, rank), jnp.int32),
            pltpu.VMEM(compress.shape, jnp.bfloat16),
            pltpu.SemaphoreType.DMA((2,)),
        ],
        compiler_params=pltpu.CompilerParams(vmem_limit_bytes=KERNEL_VMEM),
        cost_estimate=pl.CostEstimate(flops=50_000_000, bytes_accessed=600_000, transcendentals=0),
        name="tables",
    )(skeleton.transpose(1, 0, 2), compress)


def sampled_apart(sampling, traces):
    count, width = traces.shape
    block = count // 8

    def kernel(sampling_ref, rows_ref, coeffs_ref):
        coeffs_ref[...] = sampled_block(sampling_ref[...], rows_ref[...])

    return pl.pallas_call(
        kernel,
        grid=(count // block,),
        out_shape=jax.ShapeDtypeStruct((sampling.shape[1], count), jnp.bfloat16),
        in_specs=[
            pl.BlockSpec(sampling.shape, lambda i: (0, 0)),
            pl.BlockSpec((block, width), lambda i: (i, 0)),
        ],
        out_specs=pl.BlockSpec((sampling.shape[1], block), lambda i: (0, i)),
        compiler_params=pltpu.CompilerParams(vmem_limit_bytes=63 * 1024 * 1024),
        name="sampled_apart",
    )(sampling, traces)


def picked_columns(compress, skeleton):
    rank = skeleton.shape[-1]
    places = lax.broadcasted_iota(jnp.int32, (1, 1, 2 * rank), 2)
    chooser = (skeleton[:, :, None] == places).astype(jnp.bfloat16)
    stacked = jnp.concatenate([compress[:, :, :rank], compress[:, :, rank:]], 1)
    return jnp.einsum(
        "ljk,lki->lji", stacked, chooser, preferred_element_type=jnp.float32
    ).astype(jnp.bfloat16)


def real_form(both):
    rank = both.shape[1] // 2
    turned = jnp.concatenate([-both[:, rank:], both[:, :rank]], 1)
    return jnp.concatenate([both, turned], 2)


def compact_rows(matrix, slot):
    rank = slot.shape[1]
    parts = [
        jnp.dot(slot, half, preferred_element_type=jnp.float32)
        for half in (matrix[:rank], matrix[rank:])
    ]
    return jnp.concatenate(parts, 0).astype(jnp.bfloat16)


def times(matrix, value):
    return jnp.dot(matrix, value, preferred_element_type=jnp.float32).astype(jnp.bfloat16)


def sampled(sampling, traces):
    return jnp.einsum(
        "pc,tp->ct", sampling, traces, preferred_element_type=jnp.float32
    ).astype(jnp.bfloat16)


def evaluated(coeffs, evaluation):
    return jnp.einsum(
        "ct,cp->tp", coeffs, evaluation, preferred_element_type=jnp.float32
    ).astype(jnp.bfloat16)


def after(value, earlier):
    return value if earlier is None else lax.optimization_barrier((value, earlier))[0]


def all_hops():
    low_bits = lax.axis_size("sub").bit_length() - 1
    high_bits = lax.axis_size("bfly").bit_length() - 1
    return [("sub", bit) for bit in range(low_bits)] + [("bfly", bit) for bit in range(high_bits)]


def full_width(traces, sampling, skeleton, compress, evaluation):
    rank = skeleton.shape[-1]
    columns = picked_columns(compress, skeleton)
    full = jnp.concatenate([real_form(columns[..., :rank]), real_form(columns[..., rank:])], 2)
    coeffs = sampled_apart(sampling, traces)
    for level, hop in enumerate(all_hops()):
        partner = from_partner(coeffs, hop)
        coeffs = times(full[level], jnp.concatenate([coeffs, partner], 0))
    return evaluated(coeffs, evaluation)


def local(traces, sampling, skeleton, compress, evaluation):
    hops = all_hops()
    levels = len(hops)
    if levels != max(level for level, _ in ORDER):
        return full_width(traces, sampling[0], skeleton[0], compress[0], evaluation[0])
    wide = lax.axis_size("sub").bit_length() - 1
    rank = skeleton.shape[-1]
    room = rank * ROOM_SIXTEENTHS // 16
    unit = traces.shape[0] // sum(SHARES)
    pieces = len(SHARES)
    starts = [unit * sum(SHARES[:i]) for i in range(pieces + 1)]
    coeffs = early(sampling, traces, starts[: EARLY_PIECES + 1])
    full, small, extra = tables(after(skeleton, coeffs[0]), compress, wide, room)
    sampling, evaluation = sampling[0], evaluation[0]
    most_here = lax.broadcasted_iota(jnp.int32, extra.shape[1:], 1) >= rank

    def compact(level, piece):
        return piece >= FULL_PIECES and level >= wide

    inputs, partners, theirs, done = {}, {}, {}, [None] * pieces
    previous, known = None, None
    for level, piece in ORDER:
        count = starts[piece + 1] - starts[piece]
        if level == 0:
            if piece < EARLY_PIECES:
                own = coeffs[piece]
            else:
                block = traces[starts[piece] : starts[piece + 1]]
                own = sampled(after(sampling, previous), block)
        else:
            arrived = after(partners[piece], previous)
            if piece == 0 and level - 1 >= wide:
                known = arrived[:, count:]
                theirs[level - 1] = known[:room, :rank]
            value = jnp.concatenate([inputs[piece], arrived[:, :count]], 0)
            matrix = full[level - 1]
            if compact(level - 1, piece):
                value = jnp.pad(value, ((0, full.shape[2] - value.shape[0]), (0, 0)))
                matrix = small[level - 1]
            own = times(matrix, value)
        if level == levels:
            done[piece] = previous = evaluated(own, evaluation)
            if piece == COUNT_PIECE:
                most = after(jnp.maximum(extra[levels - 1], known)[:8, rank:], previous)
                for hop in hops[:wide]:
                    most = jnp.maximum(most, from_partner(most, hop))
            continue
        outgoing = own
        if compact(level, piece):
            outgoing = times(compact_rows(matrix, theirs[level]), value)
        if piece == 0 and level >= wide:
            block = extra[level]
            if known is not None:
                block = jnp.where(most_here, jnp.maximum(block, known), block)
            outgoing = jnp.concatenate([outgoing, block], 1)
        inputs[piece] = own
        partners[piece] = from_partner(outgoing, hops[level])
        previous = outgoing
    quick = jnp.concatenate(done, 0)
    return lax.cond(
        most[0, 0] > room,
        lambda: full_width(traces, sampling, skeleton[0], compress[0], evaluation),
        lambda: quick,
    )


def solution(mesh):
    placed = (
        P(("shots", "tr"), ("bfly", "sub")),
        P(("bfly", "sub"), None, None),
        P(("bfly", "sub"), None, None),
        P(("bfly", "sub"), None, None, None),
        P(("bfly", "sub"), None, None),
    )
    return jax.shard_map(
        local,
        mesh=mesh,
        in_specs=placed,
        out_specs=P(("shots", "tr"), ("bfly", "sub")),
        check_vma=False,
    )
```

```python
import jax
import jax.numpy as jnp
from jax import lax
from jax.experimental import pallas as pl
from jax.experimental.pallas import tpu as pltpu
from jax.sharding import PartitionSpec as P

SHARES = (2, 5, 7, 10, 8)
FULL_PIECES = (2, 1)
EARLY_PIECES = 3
COUNT_PIECE = 2
LOOK = (3, -1)
ORDER = (
    (0, 0), (0, 1), (1, 0), (0, 2), (1, 1), (2, 0), (0, 3), (1, 2), LOOK, (2, 1), (0, 4), (1, 3),
    (2, 2), (3, 0), (1, 4), (2, 3), (3, 1), (2, 4), (3, 2), (3, 3), (3, 4),
)
KERNEL_VMEM = 16 * 1024 * 1024
ROOM_SIXTEENTHS = 11


def route(axis, apart):
    count = lax.axis_size(axis)
    pairs = []
    for low in range(count):
        high = low | 1 << apart
        if high != low and high < count:
            pairs += [(low, high), (high, low)]
    return pairs


def from_partner(block, hop):
    return lax.ppermute(block, hop[0], route(*hop))


def across(left, right):
    return lax.dot_general(left, right, (((1,), (1,)), ((), ())), preferred_element_type=jnp.float32)


def one_hot(condition):
    return jnp.where(condition, 1.0, 0.0).astype(jnp.bfloat16)


def sampled_block(sampling, rows):
    turned = sampling.astype(jnp.float32).T.astype(jnp.bfloat16)
    return across(turned, rows).astype(jnp.bfloat16)


def early_kernel(starts, sampling_hbm, traces_hbm, *refs):
    pieces = len(starts) - 1
    outs, (sampling_ref, rows_ref, arrived) = refs[:pieces], refs[pieces:]
    loads = [pltpu.make_async_copy(sampling_hbm, sampling_ref, arrived.at[pieces])]
    for i in range(pieces):
        span = pl.ds(starts[i], starts[i + 1] - starts[i])
        loads.append(pltpu.make_async_copy(traces_hbm.at[span], rows_ref.at[span], arrived.at[i]))
    for load in loads:
        load.start()
    loads[0].wait()
    for i in range(pieces):
        loads[i + 1].wait()
        span = pl.ds(starts[i], starts[i + 1] - starts[i])
        outs[i][...] = sampled_block(sampling_ref[0], rows_ref[span])


def early(sampling, traces, starts):
    pieces = len(starts) - 1
    width = sampling.shape[-1]
    total = starts[-1]
    return pl.pallas_call(
        lambda *refs: early_kernel(starts, *refs),
        out_shape=[
            jax.ShapeDtypeStruct((width, starts[i + 1] - starts[i]), jnp.bfloat16) for i in range(pieces)
        ],
        in_specs=[pl.BlockSpec(memory_space=pltpu.HBM)] * 2,
        out_specs=[pl.BlockSpec(memory_space=pltpu.VMEM)] * pieces,
        scratch_shapes=[
            pltpu.VMEM(sampling.shape, jnp.bfloat16),
            pltpu.VMEM((total, traces.shape[1]), jnp.bfloat16),
            pltpu.SemaphoreType.DMA((pieces + 1,)),
        ],
        compiler_params=pltpu.CompilerParams(vmem_limit_bytes=KERNEL_VMEM),
        cost_estimate=pl.CostEstimate(
            flops=2 * total * width * width, bytes_accessed=4 * total * width, transcendentals=0
        ),
        name="early",
    )(sampling, traces)


def tables_kernel(
    wide, room, skeleton_hbm, compress_hbm, full_ref, small_ref, extra_ref,
    skeleton_ref, compress_ref, arrived,
):
    loads = [
        pltpu.make_async_copy(skeleton_hbm, skeleton_ref, arrived.at[0]),
        pltpu.make_async_copy(compress_hbm, compress_ref, arrived.at[1]),
    ]
    for load in loads:
        load.start()
    for load in loads:
        load.wait()
    levels, rank = skeleton_ref.shape[0], skeleton_ref.shape[-1]
    width = 2 * rank
    f32, i32 = jnp.float32, jnp.int32
    k = lax.broadcasted_iota(i32, (width, width), 1)
    twice = one_hot(lax.broadcasted_iota(i32, (width, rank), 0) % rank == lax.broadcasted_iota(i32, (width, rank), 1))
    earlier = one_hot(
        (lax.broadcasted_iota(i32, (width, width), 1) < lax.broadcasted_iota(i32, (width, width), 0) % rank)
    )
    column = lax.broadcasted_iota(i32, (2 * width, width), 0)
    is_real_entry = lax.broadcasted_iota(i32, (2 * width, width), 1) < rank
    partner_column = column >= width
    imag_column = column % width >= rank
    coefficient = column % rank + jnp.where(partner_column, rank, 0)
    slot_column = column - width
    slot_imag = slot_column >= room
    slot_of_column = jnp.where(slot_imag, slot_column - room, slot_column)
    row = lax.broadcasted_iota(i32, (width, width), 0)
    most = jnp.zeros((1, 1), f32)
    for level in range(levels):
        entry = jnp.broadcast_to(skeleton_ref[level].astype(f32), (8, rank)).astype(jnp.bfloat16)
        entry = across(entry, twice)[:1]
        picked = jnp.where(entry >= rank, 1.0, 0.0)
        slot = across(jnp.broadcast_to(picked, (8, width)).astype(jnp.bfloat16), earlier)[:1].astype(i32)
        entry = entry.astype(i32)
        from_partner_entry = entry >= rank
        matrix = compress_ref[0, level]

        def halves(match, imag):
            same = is_real_entry != imag
            real = jnp.where(match & same, jnp.where(imag, -1.0, 1.0), 0.0).astype(jnp.bfloat16)
            turned = one_hot(match & jnp.logical_not(same))
            return across(matrix, real).astype(jnp.bfloat16), across(matrix, turned).astype(jnp.bfloat16)

        match = entry == coefficient
        full_ref[level, :rank], full_ref[level, rank:] = halves(match, imag_column)
        compacted = (slot == slot_of_column) & from_partner_entry
        match = (match & jnp.logical_not(partner_column)) | (compacted & partner_column)
        imag = (imag_column & jnp.logical_not(partner_column)) | (slot_imag & partner_column)
        small_ref[level, :rank], small_ref[level, rank:] = halves(match, imag)
        once = (k < rank) & from_partner_entry
        places = across(one_hot(once & (slot == row)), one_hot(once & (entry - rank == row)))
        extra_ref[level] = places.astype(jnp.bfloat16)
        if level >= wide:
            most = jnp.maximum(most, jnp.sum(picked, axis=1, keepdims=True) * 0.5)
    for level in range(wide, levels):
        extra_ref[level] = jnp.where(k < rank, extra_ref[level].astype(f32), most).astype(jnp.bfloat16)


def tables(skeleton, compress, wide, room):
    levels, rank = skeleton.shape[1:]
    shape = (levels, 2 * rank, 4 * rank)
    return pl.pallas_call(
        lambda *refs: tables_kernel(wide, room, *refs),
        out_shape=[
            jax.ShapeDtypeStruct(shape, jnp.bfloat16),
            jax.ShapeDtypeStruct(shape, jnp.bfloat16),
            jax.ShapeDtypeStruct((levels, 2 * rank, 2 * rank), jnp.bfloat16),
        ],
        in_specs=[pl.BlockSpec(memory_space=pltpu.HBM)] * 2,
        out_specs=[pl.BlockSpec(memory_space=pltpu.VMEM)] * 3,
        scratch_shapes=[
            pltpu.VMEM((levels, 1, rank), jnp.int32),
            pltpu.VMEM(compress.shape, jnp.bfloat16),
            pltpu.SemaphoreType.DMA((2,)),
        ],
        compiler_params=pltpu.CompilerParams(vmem_limit_bytes=KERNEL_VMEM),
        cost_estimate=pl.CostEstimate(flops=50_000_000, bytes_accessed=600_000, transcendentals=0),
        name="tables",
    )(skeleton.transpose(1, 0, 2), compress)


def sampled_apart(sampling, traces):
    count, width = traces.shape
    block = count // 8

    def kernel(sampling_ref, rows_ref, coeffs_ref):
        coeffs_ref[...] = sampled_block(sampling_ref[...], rows_ref[...])

    return pl.pallas_call(
        kernel,
        grid=(count // block,),
        out_shape=jax.ShapeDtypeStruct((sampling.shape[1], count), jnp.bfloat16),
        in_specs=[
            pl.BlockSpec(sampling.shape, lambda i: (0, 0)),
            pl.BlockSpec((block, width), lambda i: (i, 0)),
        ],
        out_specs=pl.BlockSpec((sampling.shape[1], block), lambda i: (0, i)),
        compiler_params=pltpu.CompilerParams(vmem_limit_bytes=63 * 1024 * 1024),
        name="sampled_apart",
    )(sampling, traces)


def picked_columns(compress, skeleton):
    rank = skeleton.shape[-1]
    places = lax.broadcasted_iota(jnp.int32, (1, 1, 2 * rank), 2)
    chooser = (skeleton[:, :, None] == places).astype(jnp.bfloat16)
    stacked = jnp.concatenate([compress[:, :, :rank], compress[:, :, rank:]], 1)
    return jnp.einsum(
        "ljk,lki->lji", stacked, chooser, preferred_element_type=jnp.float32
    ).astype(jnp.bfloat16)


def real_form(both):
    rank = both.shape[1] // 2
    turned = jnp.concatenate([-both[:, rank:], both[:, :rank]], 1)
    return jnp.concatenate([both, turned], 2)


def compact_rows(matrix, slot):
    rank = slot.shape[1]
    parts = [
        jnp.dot(slot, half, preferred_element_type=jnp.float32)
        for half in (matrix[:rank], matrix[rank:])
    ]
    return jnp.concatenate(parts, 0).astype(jnp.bfloat16)


def times(matrix, value):
    return jnp.dot(matrix, value, preferred_element_type=jnp.float32).astype(jnp.bfloat16)


def sampled(sampling, traces):
    return jnp.einsum(
        "pc,tp->ct", sampling, traces, preferred_element_type=jnp.float32
    ).astype(jnp.bfloat16)


def evaluated(coeffs, evaluation):
    return jnp.einsum(
        "ct,cp->tp", coeffs, evaluation, preferred_element_type=jnp.float32
    ).astype(jnp.bfloat16)


def after(value, earlier):
    return value if earlier is None else lax.optimization_barrier((value, earlier))[0]


def all_hops():
    low_bits = lax.axis_size("sub").bit_length() - 1
    high_bits = lax.axis_size("bfly").bit_length() - 1
    return [("sub", bit) for bit in range(low_bits)] + [("bfly", bit) for bit in range(high_bits)]


def full_width(traces, sampling, skeleton, compress, evaluation):
    rank = skeleton.shape[-1]
    columns = picked_columns(compress, skeleton)
    full = jnp.concatenate([real_form(columns[..., :rank]), real_form(columns[..., rank:])], 2)
    coeffs = sampled_apart(sampling, traces)
    for level, hop in enumerate(all_hops()):
        partner = from_partner(coeffs, hop)
        coeffs = times(full[level], jnp.concatenate([coeffs, partner], 0))
    return evaluated(coeffs, evaluation)


def local(traces, sampling, skeleton, compress, evaluation):
    hops = all_hops()
    levels = len(hops)
    if levels != max(level for level, _ in ORDER):
        return full_width(traces, sampling[0], skeleton[0], compress[0], evaluation[0])
    wide = lax.axis_size("sub").bit_length() - 1
    rank = skeleton.shape[-1]
    room = rank * ROOM_SIXTEENTHS // 16
    unit = traces.shape[0] // sum(SHARES)
    pieces = len(SHARES)
    starts = [unit * sum(SHARES[:i]) for i in range(pieces + 1)]
    coeffs = early(sampling, traces, starts[: EARLY_PIECES + 1])
    full, small, extra = tables(after(skeleton, coeffs[0]), compress, wide, room)
    sampling, evaluation = sampling[0], evaluation[0]
    most_here = lax.broadcasted_iota(jnp.int32, extra.shape[1:], 1) >= rank

    def compact(level, piece):
        return level >= wide and piece >= FULL_PIECES[level - wide]

    inputs, partners, theirs, done = {}, {}, {}, [None] * pieces
    previous, finished, known = None, None, None
    for level, piece in ORDER:
        if (level, piece) == LOOK:
            known = after(partners[0], previous)[:, starts[1] :]
            theirs[levels - 1] = known[:room, :rank]
            continue
        count = starts[piece + 1] - starts[piece]
        if level == 0:
            if piece < EARLY_PIECES:
                own = coeffs[piece]
            else:
                block = traces[starts[piece] : starts[piece + 1]]
                own = sampled(after(sampling, previous), block)
        else:
            arrived = after(partners[piece], previous)
            if level == levels:
                arrived = after(arrived, finished)
            elif piece == 0 and level - 1 >= wide:
                known = arrived[:, count:]
                theirs[level - 1] = known[:room, :rank]
            value = jnp.concatenate([inputs[piece], arrived[:, :count]], 0)
            matrix = full[level - 1]
            if compact(level - 1, piece):
                value = jnp.pad(value, ((0, full.shape[2] - value.shape[0]), (0, 0)))
                matrix = small[level - 1]
            own = times(matrix, value)
        if level == levels:
            done[piece] = finished = evaluated(own, evaluation)
            if piece == COUNT_PIECE:
                most = after(jnp.maximum(extra[levels - 1], known)[:8, rank:], finished)
                for hop in hops[:wide]:
                    most = jnp.maximum(most, from_partner(most, hop))
            continue
        outgoing = own
        if level == 0 and 1 < piece < EARLY_PIECES:
            outgoing = after(own, previous)
        if compact(level, piece):
            outgoing = times(compact_rows(matrix, theirs[level]), value)
        if piece == 0 and level >= wide:
            block = extra[level]
            if known is not None:
                block = jnp.where(most_here, jnp.maximum(block, known), block)
            outgoing = jnp.concatenate([outgoing, block], 1)
        inputs[piece] = own
        partners[piece] = from_partner(outgoing, hops[level])
        previous = outgoing
    quick = jnp.concatenate(done, 0)
    return lax.cond(
        most[0, 0] > room,
        lambda: full_width(traces, sampling, skeleton[0], compress[0], evaluation),
        lambda: quick,
    )


def solution(mesh):
    placed = (
        P(("shots", "tr"), ("bfly", "sub")),
        P(("bfly", "sub"), None, None),
        P(("bfly", "sub"), None, None),
        P(("bfly", "sub"), None, None, None),
        P(("bfly", "sub"), None, None),
    )
    return jax.shard_map(
        local,
        mesh=mesh,
        in_specs=placed,
        out_specs=P(("shots", "tr"), ("bfly", "sub")),
        check_vma=False,
    )
```

```python
import jax
import jax.numpy as jnp
from jax import lax
from jax.experimental import pallas as pl
from jax.experimental.pallas import tpu as pltpu
from jax.sharding import PartitionSpec as P

SHARES = (1, 5, 8, 10, 8)
FULL_PIECES = (2, 1)
EARLY_PIECES = 3
COUNT_PIECE = 2
LOOK = (3, -1)
ORDER = (
    (0, 0), (0, 1), (0, 2), (1, 0), (0, 3), (1, 1), (2, 0), (1, 2), LOOK, (2, 1), (0, 4), (1, 3),
    (2, 2), (3, 0), (1, 4), (2, 3), (3, 1), (2, 4), (3, 2), (3, 3), (3, 4),
)
KERNEL_VMEM = 16 * 1024 * 1024
ROOM_SIXTEENTHS = 11


def route(axis, apart):
    count = lax.axis_size(axis)
    pairs = []
    for low in range(count):
        high = low | 1 << apart
        if high != low and high < count:
            pairs += [(low, high), (high, low)]
    return pairs


def from_partner(block, hop):
    return lax.ppermute(block, hop[0], route(*hop))


def across(left, right):
    return lax.dot_general(left, right, (((1,), (1,)), ((), ())), preferred_element_type=jnp.float32)


def one_hot(condition):
    return jnp.where(condition, 1.0, 0.0).astype(jnp.bfloat16)


def sampled_block(sampling, rows):
    turned = sampling.astype(jnp.float32).T.astype(jnp.bfloat16)
    return across(turned, rows).astype(jnp.bfloat16)


def early_kernel(starts, sampling_hbm, traces_hbm, *refs):
    pieces = len(starts) - 1
    outs, (sampling_ref, rows_ref, arrived) = refs[:pieces], refs[pieces:]
    loads = [pltpu.make_async_copy(sampling_hbm, sampling_ref, arrived.at[pieces])]
    for i in range(pieces):
        span = pl.ds(starts[i], starts[i + 1] - starts[i])
        loads.append(pltpu.make_async_copy(traces_hbm.at[span], rows_ref.at[span], arrived.at[i]))
    for load in loads:
        load.start()
    loads[0].wait()
    for i in range(pieces):
        loads[i + 1].wait()
        span = pl.ds(starts[i], starts[i + 1] - starts[i])
        outs[i][...] = sampled_block(sampling_ref[0], rows_ref[span])


def early(sampling, traces, starts):
    pieces = len(starts) - 1
    width = sampling.shape[-1]
    total = starts[-1]
    return pl.pallas_call(
        lambda *refs: early_kernel(starts, *refs),
        out_shape=[
            jax.ShapeDtypeStruct((width, starts[i + 1] - starts[i]), jnp.bfloat16) for i in range(pieces)
        ],
        in_specs=[pl.BlockSpec(memory_space=pltpu.HBM)] * 2,
        out_specs=[pl.BlockSpec(memory_space=pltpu.VMEM)] * pieces,
        scratch_shapes=[
            pltpu.VMEM(sampling.shape, jnp.bfloat16),
            pltpu.VMEM((total, traces.shape[1]), jnp.bfloat16),
            pltpu.SemaphoreType.DMA((pieces + 1,)),
        ],
        compiler_params=pltpu.CompilerParams(vmem_limit_bytes=KERNEL_VMEM),
        cost_estimate=pl.CostEstimate(
            flops=2 * total * width * width, bytes_accessed=4 * total * width, transcendentals=0
        ),
        name="early",
    )(sampling, traces)


def tables_kernel(
    wide, room, skeleton_hbm, compress_hbm, full_ref, small_ref, extra_ref,
    skeleton_ref, compress_ref, arrived,
):
    loads = [
        pltpu.make_async_copy(skeleton_hbm, skeleton_ref, arrived.at[0]),
        pltpu.make_async_copy(compress_hbm, compress_ref, arrived.at[1]),
    ]
    for load in loads:
        load.start()
    for load in loads:
        load.wait()
    levels, rank = skeleton_ref.shape[0], skeleton_ref.shape[-1]
    width = 2 * rank
    f32, i32 = jnp.float32, jnp.int32
    k = lax.broadcasted_iota(i32, (width, width), 1)
    twice = one_hot(lax.broadcasted_iota(i32, (width, rank), 0) % rank == lax.broadcasted_iota(i32, (width, rank), 1))
    earlier = one_hot(
        (lax.broadcasted_iota(i32, (width, width), 1) < lax.broadcasted_iota(i32, (width, width), 0) % rank)
    )
    column = lax.broadcasted_iota(i32, (2 * width, width), 0)
    is_real_entry = lax.broadcasted_iota(i32, (2 * width, width), 1) < rank
    partner_column = column >= width
    imag_column = column % width >= rank
    coefficient = column % rank + jnp.where(partner_column, rank, 0)
    slot_column = column - width
    slot_imag = slot_column >= room
    slot_of_column = jnp.where(slot_imag, slot_column - room, slot_column)
    row = lax.broadcasted_iota(i32, (width, width), 0)
    most = jnp.zeros((1, 1), f32)
    for level in range(levels):
        entry = jnp.broadcast_to(skeleton_ref[level].astype(f32), (8, rank)).astype(jnp.bfloat16)
        entry = across(entry, twice)[:1]
        picked = jnp.where(entry >= rank, 1.0, 0.0)
        slot = across(jnp.broadcast_to(picked, (8, width)).astype(jnp.bfloat16), earlier)[:1].astype(i32)
        entry = entry.astype(i32)
        from_partner_entry = entry >= rank
        matrix = compress_ref[0, level]

        def halves(match, imag):
            same = is_real_entry != imag
            real = jnp.where(match & same, jnp.where(imag, -1.0, 1.0), 0.0).astype(jnp.bfloat16)
            turned = one_hot(match & jnp.logical_not(same))
            return across(matrix, real).astype(jnp.bfloat16), across(matrix, turned).astype(jnp.bfloat16)

        match = entry == coefficient
        full_ref[level, :rank], full_ref[level, rank:] = halves(match, imag_column)
        compacted = (slot == slot_of_column) & from_partner_entry
        match = (match & jnp.logical_not(partner_column)) | (compacted & partner_column)
        imag = (imag_column & jnp.logical_not(partner_column)) | (slot_imag & partner_column)
        small_ref[level, :rank], small_ref[level, rank:] = halves(match, imag)
        once = (k < rank) & from_partner_entry
        places = across(one_hot(once & (slot == row)), one_hot(once & (entry - rank == row)))
        extra_ref[level] = places.astype(jnp.bfloat16)
        if level >= wide:
            most = jnp.maximum(most, jnp.sum(picked, axis=1, keepdims=True) * 0.5)
    for level in range(wide, levels):
        extra_ref[level] = jnp.where(k < rank, extra_ref[level].astype(f32), most).astype(jnp.bfloat16)


def tables(skeleton, compress, wide, room):
    levels, rank = skeleton.shape[1:]
    shape = (levels, 2 * rank, 4 * rank)
    return pl.pallas_call(
        lambda *refs: tables_kernel(wide, room, *refs),
        out_shape=[
            jax.ShapeDtypeStruct(shape, jnp.bfloat16),
            jax.ShapeDtypeStruct(shape, jnp.bfloat16),
            jax.ShapeDtypeStruct((levels, 2 * rank, 2 * rank), jnp.bfloat16),
        ],
        in_specs=[pl.BlockSpec(memory_space=pltpu.HBM)] * 2,
        out_specs=[pl.BlockSpec(memory_space=pltpu.VMEM)] * 3,
        scratch_shapes=[
            pltpu.VMEM((levels, 1, rank), jnp.int32),
            pltpu.VMEM(compress.shape, jnp.bfloat16),
            pltpu.SemaphoreType.DMA((2,)),
        ],
        compiler_params=pltpu.CompilerParams(vmem_limit_bytes=KERNEL_VMEM),
        cost_estimate=pl.CostEstimate(flops=50_000_000, bytes_accessed=600_000, transcendentals=0),
        name="tables",
    )(skeleton.transpose(1, 0, 2), compress)


def sampled_apart(sampling, traces):
    count, width = traces.shape
    block = count // 8

    def kernel(sampling_ref, rows_ref, coeffs_ref):
        coeffs_ref[...] = sampled_block(sampling_ref[...], rows_ref[...])

    return pl.pallas_call(
        kernel,
        grid=(count // block,),
        out_shape=jax.ShapeDtypeStruct((sampling.shape[1], count), jnp.bfloat16),
        in_specs=[
            pl.BlockSpec(sampling.shape, lambda i: (0, 0)),
            pl.BlockSpec((block, width), lambda i: (i, 0)),
        ],
        out_specs=pl.BlockSpec((sampling.shape[1], block), lambda i: (0, i)),
        compiler_params=pltpu.CompilerParams(vmem_limit_bytes=63 * 1024 * 1024),
        name="sampled_apart",
    )(sampling, traces)


def picked_columns(compress, skeleton):
    rank = skeleton.shape[-1]
    places = lax.broadcasted_iota(jnp.int32, (1, 1, 2 * rank), 2)
    chooser = (skeleton[:, :, None] == places).astype(jnp.bfloat16)
    stacked = jnp.concatenate([compress[:, :, :rank], compress[:, :, rank:]], 1)
    return jnp.einsum(
        "ljk,lki->lji", stacked, chooser, preferred_element_type=jnp.float32
    ).astype(jnp.bfloat16)


def real_form(both):
    rank = both.shape[1] // 2
    turned = jnp.concatenate([-both[:, rank:], both[:, :rank]], 1)
    return jnp.concatenate([both, turned], 2)


def compact_rows(matrix, slot):
    rank = slot.shape[1]
    parts = [
        jnp.dot(slot, half, preferred_element_type=jnp.float32)
        for half in (matrix[:rank], matrix[rank:])
    ]
    return jnp.concatenate(parts, 0).astype(jnp.bfloat16)


def times(matrix, value):
    return jnp.dot(matrix, value, preferred_element_type=jnp.float32).astype(jnp.bfloat16)


def sampled(sampling, traces):
    return jnp.einsum(
        "pc,tp->ct", sampling, traces, preferred_element_type=jnp.float32
    ).astype(jnp.bfloat16)


def evaluated(coeffs, evaluation):
    return jnp.einsum(
        "ct,cp->tp", coeffs, evaluation, preferred_element_type=jnp.float32
    ).astype(jnp.bfloat16)


def after(value, earlier):
    return value if earlier is None else lax.optimization_barrier((value, earlier))[0]


def all_hops():
    low_bits = lax.axis_size("sub").bit_length() - 1
    high_bits = lax.axis_size("bfly").bit_length() - 1
    return [("sub", bit) for bit in range(low_bits)] + [("bfly", bit) for bit in range(high_bits)]


def full_width(traces, sampling, skeleton, compress, evaluation):
    rank = skeleton.shape[-1]
    columns = picked_columns(compress, skeleton)
    full = jnp.concatenate([real_form(columns[..., :rank]), real_form(columns[..., rank:])], 2)
    coeffs = sampled_apart(sampling, traces)
    for level, hop in enumerate(all_hops()):
        partner = from_partner(coeffs, hop)
        coeffs = times(full[level], jnp.concatenate([coeffs, partner], 0))
    return evaluated(coeffs, evaluation)


def local(traces, sampling, skeleton, compress, evaluation):
    hops = all_hops()
    levels = len(hops)
    if levels != max(level for level, _ in ORDER):
        return full_width(traces, sampling[0], skeleton[0], compress[0], evaluation[0])
    wide = lax.axis_size("sub").bit_length() - 1
    rank = skeleton.shape[-1]
    room = rank * ROOM_SIXTEENTHS // 16
    unit = traces.shape[0] // sum(SHARES)
    pieces = len(SHARES)
    starts = [unit * sum(SHARES[:i]) for i in range(pieces + 1)]
    coeffs = early(sampling, traces, starts[: EARLY_PIECES + 1])
    full, small, extra = tables(after(skeleton, coeffs[0]), compress, wide, room)
    sampling, evaluation = sampling[0], evaluation[0]
    most_here = lax.broadcasted_iota(jnp.int32, extra.shape[1:], 1) >= rank

    def compact(level, piece):
        return level >= wide and piece >= FULL_PIECES[level - wide]

    inputs, partners, theirs, done = {}, {}, {}, [None] * pieces
    previous, finished, known = None, None, None
    for level, piece in ORDER:
        if (level, piece) == LOOK:
            known = after(partners[0], previous)[:, starts[1] :]
            theirs[levels - 1] = known[:room, :rank]
            continue
        count = starts[piece + 1] - starts[piece]
        if level == 0:
            if piece < EARLY_PIECES:
                own = coeffs[piece]
            else:
                block = traces[starts[piece] : starts[piece + 1]]
                own = sampled(after(sampling, previous), block)
        else:
            arrived = after(partners[piece], previous)
            if level == levels:
                arrived = after(arrived, finished)
            elif piece == 0 and level - 1 >= wide:
                known = arrived[:, count:]
                theirs[level - 1] = known[:room, :rank]
            value = jnp.concatenate([inputs[piece], arrived[:, :count]], 0)
            matrix = full[level - 1]
            if compact(level - 1, piece):
                value = jnp.pad(value, ((0, full.shape[2] - value.shape[0]), (0, 0)))
                matrix = small[level - 1]
            own = times(matrix, value)
        if level == levels:
            done[piece] = finished = evaluated(own, evaluation)
            if piece == COUNT_PIECE:
                most = after(jnp.maximum(extra[levels - 1], known)[:8, rank:], finished)
                for hop in hops[:wide]:
                    most = jnp.maximum(most, from_partner(most, hop))
            continue
        outgoing = own
        if compact(level, piece):
            outgoing = times(compact_rows(matrix, theirs[level]), value)
        if piece == 0 and level >= wide:
            block = extra[level]
            if known is not None:
                block = jnp.where(most_here, jnp.maximum(block, known), block)
            outgoing = jnp.concatenate([outgoing, block], 1)
        inputs[piece] = own
        partners[piece] = from_partner(outgoing, hops[level])
        previous = outgoing
    quick = jnp.concatenate(done, 0)
    return lax.cond(
        most[0, 0] > room,
        lambda: full_width(traces, sampling, skeleton[0], compress[0], evaluation),
        lambda: quick,
    )


def solution(mesh):
    placed = (
        P(("shots", "tr"), ("bfly", "sub")),
        P(("bfly", "sub"), None, None),
        P(("bfly", "sub"), None, None),
        P(("bfly", "sub"), None, None, None),
        P(("bfly", "sub"), None, None),
    )
    return jax.shard_map(
        local,
        mesh=mesh,
        in_specs=placed,
        out_specs=P(("shots", "tr"), ("bfly", "sub")),
        check_vma=False,
    )
```

```python
import jax
import jax.numpy as jnp
from jax import lax
from jax.experimental import pallas as pl
from jax.experimental.pallas import tpu as pltpu
from jax.sharding import PartitionSpec as P

SHARES = (2, 5, 9, 9, 7)
FULL_PIECES = (2, 1)
EARLY_PIECES = 2
COUNT_PIECE = 2
LOOK = (3, -1)
ORDER = (
    (0, 0), (0, 1), (0, 2), (1, 0), (0, 3), (1, 1), (2, 0), (1, 2), LOOK, (2, 1), (0, 4), (1, 3),
    (2, 2), (3, 0), (1, 4), (2, 3), (3, 1), (2, 4), (3, 2), (3, 3), (3, 4),
)
KERNEL_VMEM = 16 * 1024 * 1024
ROOM_SIXTEENTHS = 11


def route(axis, apart):
    count = lax.axis_size(axis)
    pairs = []
    for low in range(count):
        high = low | 1 << apart
        if high != low and high < count:
            pairs += [(low, high), (high, low)]
    return pairs


def from_partner(block, hop):
    return lax.ppermute(block, hop[0], route(*hop))


def across(left, right):
    return lax.dot_general(left, right, (((1,), (1,)), ((), ())), preferred_element_type=jnp.float32)


def one_hot(condition):
    return jnp.where(condition, 1.0, 0.0).astype(jnp.bfloat16)


def sampled_block(sampling, rows):
    turned = sampling.astype(jnp.float32).T.astype(jnp.bfloat16)
    return across(turned, rows).astype(jnp.bfloat16)


def early_kernel(starts, sampling_hbm, traces_hbm, *refs):
    pieces = len(starts) - 1
    outs, (sampling_ref, rows_ref, arrived) = refs[:pieces], refs[pieces:]
    loads = [pltpu.make_async_copy(sampling_hbm, sampling_ref, arrived.at[pieces])]
    for i in range(pieces):
        span = pl.ds(starts[i], starts[i + 1] - starts[i])
        loads.append(pltpu.make_async_copy(traces_hbm.at[span], rows_ref.at[span], arrived.at[i]))
    for load in loads:
        load.start()
    loads[0].wait()
    for i in range(pieces):
        loads[i + 1].wait()
        span = pl.ds(starts[i], starts[i + 1] - starts[i])
        outs[i][...] = sampled_block(sampling_ref[0], rows_ref[span])


def early(sampling, traces, starts):
    pieces = len(starts) - 1
    width = sampling.shape[-1]
    total = starts[-1]
    return pl.pallas_call(
        lambda *refs: early_kernel(starts, *refs),
        out_shape=[
            jax.ShapeDtypeStruct((width, starts[i + 1] - starts[i]), jnp.bfloat16) for i in range(pieces)
        ],
        in_specs=[pl.BlockSpec(memory_space=pltpu.HBM)] * 2,
        out_specs=[pl.BlockSpec(memory_space=pltpu.VMEM)] * pieces,
        scratch_shapes=[
            pltpu.VMEM(sampling.shape, jnp.bfloat16),
            pltpu.VMEM((total, traces.shape[1]), jnp.bfloat16),
            pltpu.SemaphoreType.DMA((pieces + 1,)),
        ],
        compiler_params=pltpu.CompilerParams(vmem_limit_bytes=KERNEL_VMEM),
        cost_estimate=pl.CostEstimate(
            flops=2 * total * width * width, bytes_accessed=4 * total * width, transcendentals=0
        ),
        name="early",
    )(sampling, traces)


def tables_kernel(
    wide, room, skeleton_hbm, compress_hbm, full_ref, small_ref, extra_ref,
    skeleton_ref, compress_ref, arrived,
):
    loads = [
        pltpu.make_async_copy(skeleton_hbm, skeleton_ref, arrived.at[0]),
        pltpu.make_async_copy(compress_hbm, compress_ref, arrived.at[1]),
    ]
    for load in loads:
        load.start()
    for load in loads:
        load.wait()
    levels, rank = skeleton_ref.shape[0], skeleton_ref.shape[-1]
    width = 2 * rank
    f32, i32 = jnp.float32, jnp.int32
    k = lax.broadcasted_iota(i32, (width, width), 1)
    twice = one_hot(lax.broadcasted_iota(i32, (width, rank), 0) % rank == lax.broadcasted_iota(i32, (width, rank), 1))
    earlier = one_hot(
        (lax.broadcasted_iota(i32, (width, width), 1) < lax.broadcasted_iota(i32, (width, width), 0) % rank)
    )
    column = lax.broadcasted_iota(i32, (2 * width, width), 0)
    is_real_entry = lax.broadcasted_iota(i32, (2 * width, width), 1) < rank
    partner_column = column >= width
    imag_column = column % width >= rank
    coefficient = column % rank + jnp.where(partner_column, rank, 0)
    slot_column = column - width
    slot_imag = slot_column >= room
    slot_of_column = jnp.where(slot_imag, slot_column - room, slot_column)
    row = lax.broadcasted_iota(i32, (width, width), 0)
    most = jnp.zeros((1, 1), f32)
    for level in range(levels):
        entry = jnp.broadcast_to(skeleton_ref[level].astype(f32), (8, rank)).astype(jnp.bfloat16)
        entry = across(entry, twice)[:1]
        picked = jnp.where(entry >= rank, 1.0, 0.0)
        slot = across(jnp.broadcast_to(picked, (8, width)).astype(jnp.bfloat16), earlier)[:1].astype(i32)
        entry = entry.astype(i32)
        from_partner_entry = entry >= rank
        matrix = compress_ref[0, level]

        def halves(match, imag):
            same = is_real_entry != imag
            real = jnp.where(match & same, jnp.where(imag, -1.0, 1.0), 0.0).astype(jnp.bfloat16)
            turned = one_hot(match & jnp.logical_not(same))
            return across(matrix, real).astype(jnp.bfloat16), across(matrix, turned).astype(jnp.bfloat16)

        match = entry == coefficient
        full_ref[level, :rank], full_ref[level, rank:] = halves(match, imag_column)
        compacted = (slot == slot_of_column) & from_partner_entry
        match = (match & jnp.logical_not(partner_column)) | (compacted & partner_column)
        imag = (imag_column & jnp.logical_not(partner_column)) | (slot_imag & partner_column)
        small_ref[level, :rank], small_ref[level, rank:] = halves(match, imag)
        once = (k < rank) & from_partner_entry
        places = across(one_hot(once & (slot == row)), one_hot(once & (entry - rank == row)))
        extra_ref[level] = places.astype(jnp.bfloat16)
        if level >= wide:
            most = jnp.maximum(most, jnp.sum(picked, axis=1, keepdims=True) * 0.5)
    for level in range(wide, levels):
        extra_ref[level] = jnp.where(k < rank, extra_ref[level].astype(f32), most).astype(jnp.bfloat16)


def tables(skeleton, compress, wide, room):
    levels, rank = skeleton.shape[1:]
    shape = (levels, 2 * rank, 4 * rank)
    return pl.pallas_call(
        lambda *refs: tables_kernel(wide, room, *refs),
        out_shape=[
            jax.ShapeDtypeStruct(shape, jnp.bfloat16),
            jax.ShapeDtypeStruct(shape, jnp.bfloat16),
            jax.ShapeDtypeStruct((levels, 2 * rank, 2 * rank), jnp.bfloat16),
        ],
        in_specs=[pl.BlockSpec(memory_space=pltpu.HBM)] * 2,
        out_specs=[pl.BlockSpec(memory_space=pltpu.VMEM)] * 3,
        scratch_shapes=[
            pltpu.VMEM((levels, 1, rank), jnp.int32),
            pltpu.VMEM(compress.shape, jnp.bfloat16),
            pltpu.SemaphoreType.DMA((2,)),
        ],
        compiler_params=pltpu.CompilerParams(vmem_limit_bytes=KERNEL_VMEM),
        cost_estimate=pl.CostEstimate(flops=50_000_000, bytes_accessed=600_000, transcendentals=0),
        name="tables",
    )(skeleton.transpose(1, 0, 2), compress)


def sampled_apart(sampling, traces):
    count, width = traces.shape
    block = count // 8

    def kernel(sampling_ref, rows_ref, coeffs_ref):
        coeffs_ref[...] = sampled_block(sampling_ref[...], rows_ref[...])

    return pl.pallas_call(
        kernel,
        grid=(count // block,),
        out_shape=jax.ShapeDtypeStruct((sampling.shape[1], count), jnp.bfloat16),
        in_specs=[
            pl.BlockSpec(sampling.shape, lambda i: (0, 0)),
            pl.BlockSpec((block, width), lambda i: (i, 0)),
        ],
        out_specs=pl.BlockSpec((sampling.shape[1], block), lambda i: (0, i)),
        compiler_params=pltpu.CompilerParams(vmem_limit_bytes=63 * 1024 * 1024),
        name="sampled_apart",
    )(sampling, traces)


def picked_columns(compress, skeleton):
    rank = skeleton.shape[-1]
    places = lax.broadcasted_iota(jnp.int32, (1, 1, 2 * rank), 2)
    chooser = (skeleton[:, :, None] == places).astype(jnp.bfloat16)
    stacked = jnp.concatenate([compress[:, :, :rank], compress[:, :, rank:]], 1)
    return jnp.einsum(
        "ljk,lki->lji", stacked, chooser, preferred_element_type=jnp.float32
    ).astype(jnp.bfloat16)


def real_form(both):
    rank = both.shape[1] // 2
    turned = jnp.concatenate([-both[:, rank:], both[:, :rank]], 1)
    return jnp.concatenate([both, turned], 2)


def compact_rows(matrix, slot):
    rank = slot.shape[1]
    parts = [
        jnp.dot(slot, half, preferred_element_type=jnp.float32)
        for half in (matrix[:rank], matrix[rank:])
    ]
    return jnp.concatenate(parts, 0).astype(jnp.bfloat16)


def times(matrix, value):
    return jnp.dot(matrix, value, preferred_element_type=jnp.float32).astype(jnp.bfloat16)


def sampled(sampling, traces):
    return jnp.einsum(
        "pc,tp->ct", sampling, traces, preferred_element_type=jnp.float32
    ).astype(jnp.bfloat16)


def evaluated(coeffs, evaluation):
    return jnp.einsum(
        "ct,cp->tp", coeffs, evaluation, preferred_element_type=jnp.float32
    ).astype(jnp.bfloat16)


def after(value, earlier):
    return value if earlier is None else lax.optimization_barrier((value, earlier))[0]


def all_hops():
    low_bits = lax.axis_size("sub").bit_length() - 1
    high_bits = lax.axis_size("bfly").bit_length() - 1
    return [("sub", bit) for bit in range(low_bits)] + [("bfly", bit) for bit in range(high_bits)]


def full_width(traces, sampling, skeleton, compress, evaluation):
    rank = skeleton.shape[-1]
    columns = picked_columns(compress, skeleton)
    full = jnp.concatenate([real_form(columns[..., :rank]), real_form(columns[..., rank:])], 2)
    coeffs = sampled_apart(sampling, traces)
    for level, hop in enumerate(all_hops()):
        partner = from_partner(coeffs, hop)
        coeffs = times(full[level], jnp.concatenate([coeffs, partner], 0))
    return evaluated(coeffs, evaluation)


def local(traces, sampling, skeleton, compress, evaluation):
    hops = all_hops()
    levels = len(hops)
    if levels != max(level for level, _ in ORDER):
        return full_width(traces, sampling[0], skeleton[0], compress[0], evaluation[0])
    wide = lax.axis_size("sub").bit_length() - 1
    rank = skeleton.shape[-1]
    room = rank * ROOM_SIXTEENTHS // 16
    unit = traces.shape[0] // sum(SHARES)
    pieces = len(SHARES)
    starts = [unit * sum(SHARES[:i]) for i in range(pieces + 1)]
    coeffs = early(sampling, traces, starts[: EARLY_PIECES + 1])
    full, small, extra = tables(after(skeleton, coeffs[0]), compress, wide, room)
    sampling, evaluation = sampling[0], evaluation[0]
    most_here = lax.broadcasted_iota(jnp.int32, extra.shape[1:], 1) >= rank

    def compact(level, piece):
        return level >= wide and piece >= FULL_PIECES[level - wide]

    inputs, partners, theirs, done = {}, {}, {}, [None] * pieces
    previous, finished, known = None, None, None
    for level, piece in ORDER:
        if (level, piece) == LOOK:
            known = after(partners[0], previous)[:, starts[1] :]
            theirs[levels - 1] = known[:room, :rank]
            continue
        count = starts[piece + 1] - starts[piece]
        if level == 0:
            if piece < EARLY_PIECES:
                own = coeffs[piece]
            else:
                block = traces[starts[piece] : starts[piece + 1]]
                own = sampled(after(sampling, previous), block)
        else:
            arrived = after(partners[piece], previous)
            if level == levels:
                arrived = after(arrived, finished)
            elif piece == 0 and level - 1 >= wide:
                known = arrived[:, count:]
                theirs[level - 1] = known[:room, :rank]
            value = jnp.concatenate([inputs[piece], arrived[:, :count]], 0)
            matrix = full[level - 1]
            if compact(level - 1, piece):
                value = jnp.pad(value, ((0, full.shape[2] - value.shape[0]), (0, 0)))
                matrix = small[level - 1]
            if level < levels and compact(level, piece):
                outgoing = times(compact_rows(matrix, theirs[level]), value)
                own = times(after(matrix, outgoing), value)
            else:
                own = outgoing = times(matrix, value)
        if level == levels:
            done[piece] = finished = evaluated(own, evaluation)
            if piece == COUNT_PIECE:
                most = after(jnp.maximum(extra[levels - 1], known)[:8, rank:], finished)
                for hop in hops[:wide]:
                    most = jnp.maximum(most, from_partner(most, hop))
            continue
        if level == 0:
            outgoing = own
        if piece == 0 and level >= wide:
            block = extra[level]
            if known is not None:
                block = jnp.where(most_here, jnp.maximum(block, known), block)
            outgoing = jnp.concatenate([outgoing, block], 1)
        inputs[piece] = own
        partners[piece] = from_partner(outgoing, hops[level])
        previous = outgoing
    quick = jnp.concatenate(done, 0)
    return lax.cond(
        most[0, 0] > room,
        lambda: full_width(traces, sampling, skeleton[0], compress[0], evaluation),
        lambda: quick,
    )


def solution(mesh):
    placed = (
        P(("shots", "tr"), ("bfly", "sub")),
        P(("bfly", "sub"), None, None),
        P(("bfly", "sub"), None, None),
        P(("bfly", "sub"), None, None, None),
        P(("bfly", "sub"), None, None),
    )
    return jax.shard_map(
        local,
        mesh=mesh,
        in_specs=placed,
        out_specs=P(("shots", "tr"), ("bfly", "sub")),
        check_vma=False,
    )
```

```python
import jax
import jax.numpy as jnp
from jax import lax
from jax.experimental import pallas as pl
from jax.experimental.pallas import tpu as pltpu
from jax.sharding import PartitionSpec as P

SHARES = (2, 5, 9, 9, 7)
FULL_PIECES = (2, 1)
EARLY_PIECES = 2
COUNT_PIECE = 2
COUNT_READ = 2
LOOK = (3, -1)
ORDER = (
    (0, 0), (0, 1), (0, 2), (1, 0), (1, 1), (0, 3), (2, 0), (0, 4), (1, 2), LOOK, (2, 1), (1, 3),
    (2, 2), (1, 4), (2, 3), (3, 0), (3, 1), (2, 4), (3, 2), (3, 3), (3, 4),
)
KERNEL_VMEM = 16 * 1024 * 1024
ROOM_SIXTEENTHS = 11


def route(axis, apart):
    count = lax.axis_size(axis)
    pairs = []
    for low in range(count):
        high = low | 1 << apart
        if high != low and high < count:
            pairs += [(low, high), (high, low)]
    return pairs


def from_partner(block, hop):
    return lax.ppermute(block, hop[0], route(*hop))


def across(left, right):
    return lax.dot_general(left, right, (((1,), (1,)), ((), ())), preferred_element_type=jnp.float32)


def one_hot(condition):
    return jnp.where(condition, 1.0, 0.0).astype(jnp.bfloat16)


def sampled_block(sampling, rows):
    turned = sampling.astype(jnp.float32).T.astype(jnp.bfloat16)
    return across(turned, rows).astype(jnp.bfloat16)


def early_kernel(starts, sampling_hbm, traces_hbm, *refs):
    pieces = len(starts) - 1
    outs, (sampling_ref, rows_ref, arrived) = refs[:pieces], refs[pieces:]
    loads = [pltpu.make_async_copy(sampling_hbm, sampling_ref, arrived.at[pieces])]
    for i in range(pieces):
        span = pl.ds(starts[i], starts[i + 1] - starts[i])
        loads.append(pltpu.make_async_copy(traces_hbm.at[span], rows_ref.at[span], arrived.at[i]))
    for load in loads:
        load.start()
    loads[0].wait()
    for i in range(pieces):
        loads[i + 1].wait()
        span = pl.ds(starts[i], starts[i + 1] - starts[i])
        outs[i][...] = sampled_block(sampling_ref[0], rows_ref[span])


def early(sampling, traces, starts):
    pieces = len(starts) - 1
    width = sampling.shape[-1]
    total = starts[-1]
    return pl.pallas_call(
        lambda *refs: early_kernel(starts, *refs),
        out_shape=[
            jax.ShapeDtypeStruct((width, starts[i + 1] - starts[i]), jnp.bfloat16) for i in range(pieces)
        ],
        in_specs=[pl.BlockSpec(memory_space=pltpu.HBM)] * 2,
        out_specs=[pl.BlockSpec(memory_space=pltpu.VMEM)] * pieces,
        scratch_shapes=[
            pltpu.VMEM(sampling.shape, jnp.bfloat16),
            pltpu.VMEM((total, traces.shape[1]), jnp.bfloat16),
            pltpu.SemaphoreType.DMA((pieces + 1,)),
        ],
        compiler_params=pltpu.CompilerParams(vmem_limit_bytes=KERNEL_VMEM),
        cost_estimate=pl.CostEstimate(
            flops=2 * total * width * width, bytes_accessed=4 * total * width, transcendentals=0
        ),
        name="early",
    )(sampling, traces)


def tables_kernel(
    wide, room, skeleton_hbm, compress_hbm, full_ref, small_ref, extra_ref,
    skeleton_ref, compress_ref, arrived,
):
    loads = [
        pltpu.make_async_copy(skeleton_hbm, skeleton_ref, arrived.at[0]),
        pltpu.make_async_copy(compress_hbm, compress_ref, arrived.at[1]),
    ]
    for load in loads:
        load.start()
    for load in loads:
        load.wait()
    levels, rank = skeleton_ref.shape[0], skeleton_ref.shape[-1]
    width = 2 * rank
    f32, i32 = jnp.float32, jnp.int32
    k = lax.broadcasted_iota(i32, (width, width), 1)
    twice = one_hot(lax.broadcasted_iota(i32, (width, rank), 0) % rank == lax.broadcasted_iota(i32, (width, rank), 1))
    earlier = one_hot(
        (lax.broadcasted_iota(i32, (width, width), 1) < lax.broadcasted_iota(i32, (width, width), 0) % rank)
    )
    column = lax.broadcasted_iota(i32, (2 * width, width), 0)
    is_real_entry = lax.broadcasted_iota(i32, (2 * width, width), 1) < rank
    partner_column = column >= width
    imag_column = column % width >= rank
    coefficient = column % rank + jnp.where(partner_column, rank, 0)
    slot_column = column - width
    slot_imag = slot_column >= room
    slot_of_column = jnp.where(slot_imag, slot_column - room, slot_column)
    row = lax.broadcasted_iota(i32, (width, width), 0)
    most = jnp.zeros((1, 1), f32)
    for level in range(levels):
        entry = jnp.broadcast_to(skeleton_ref[level].astype(f32), (8, rank)).astype(jnp.bfloat16)
        entry = across(entry, twice)[:1]
        picked = jnp.where(entry >= rank, 1.0, 0.0)
        slot = across(jnp.broadcast_to(picked, (8, width)).astype(jnp.bfloat16), earlier)[:1].astype(i32)
        entry = entry.astype(i32)
        from_partner_entry = entry >= rank
        matrix = compress_ref[0, level]

        def halves(match, imag):
            same = is_real_entry != imag
            real = jnp.where(match & same, jnp.where(imag, -1.0, 1.0), 0.0).astype(jnp.bfloat16)
            turned = one_hot(match & jnp.logical_not(same))
            return across(matrix, real).astype(jnp.bfloat16), across(matrix, turned).astype(jnp.bfloat16)

        match = entry == coefficient
        full_ref[level, :rank], full_ref[level, rank:] = halves(match, imag_column)
        compacted = (slot == slot_of_column) & from_partner_entry
        match = (match & jnp.logical_not(partner_column)) | (compacted & partner_column)
        imag = (imag_column & jnp.logical_not(partner_column)) | (slot_imag & partner_column)
        small_ref[level, :rank], small_ref[level, rank:] = halves(match, imag)
        once = (k < rank) & from_partner_entry
        places = across(one_hot(once & (slot == row)), one_hot(once & (entry - rank == row)))
        extra_ref[level] = places.astype(jnp.bfloat16)
        if level >= wide:
            most = jnp.maximum(most, jnp.sum(picked, axis=1, keepdims=True) * 0.5)
    for level in range(wide, levels):
        extra_ref[level] = jnp.where(k < rank, extra_ref[level].astype(f32), most).astype(jnp.bfloat16)


def tables(skeleton, compress, wide, room):
    levels, rank = skeleton.shape[1:]
    shape = (levels, 2 * rank, 4 * rank)
    return pl.pallas_call(
        lambda *refs: tables_kernel(wide, room, *refs),
        out_shape=[
            jax.ShapeDtypeStruct(shape, jnp.bfloat16),
            jax.ShapeDtypeStruct(shape, jnp.bfloat16),
            jax.ShapeDtypeStruct((levels, 2 * rank, 2 * rank), jnp.bfloat16),
        ],
        in_specs=[pl.BlockSpec(memory_space=pltpu.HBM)] * 2,
        out_specs=[pl.BlockSpec(memory_space=pltpu.VMEM)] * 3,
        scratch_shapes=[
            pltpu.VMEM((levels, 1, rank), jnp.int32),
            pltpu.VMEM(compress.shape, jnp.bfloat16),
            pltpu.SemaphoreType.DMA((2,)),
        ],
        compiler_params=pltpu.CompilerParams(vmem_limit_bytes=KERNEL_VMEM),
        cost_estimate=pl.CostEstimate(flops=50_000_000, bytes_accessed=600_000, transcendentals=0),
        name="tables",
    )(skeleton.transpose(1, 0, 2), compress)


def sampled_apart(sampling, traces):
    count, width = traces.shape
    block = count // 8

    def kernel(sampling_ref, rows_ref, coeffs_ref):
        coeffs_ref[...] = sampled_block(sampling_ref[...], rows_ref[...])

    return pl.pallas_call(
        kernel,
        grid=(count // block,),
        out_shape=jax.ShapeDtypeStruct((sampling.shape[1], count), jnp.bfloat16),
        in_specs=[
            pl.BlockSpec(sampling.shape, lambda i: (0, 0)),
            pl.BlockSpec((block, width), lambda i: (i, 0)),
        ],
        out_specs=pl.BlockSpec((sampling.shape[1], block), lambda i: (0, i)),
        compiler_params=pltpu.CompilerParams(vmem_limit_bytes=63 * 1024 * 1024),
        name="sampled_apart",
    )(sampling, traces)


def picked_columns(compress, skeleton):
    rank = skeleton.shape[-1]
    places = lax.broadcasted_iota(jnp.int32, (1, 1, 2 * rank), 2)
    chooser = (skeleton[:, :, None] == places).astype(jnp.bfloat16)
    stacked = jnp.concatenate([compress[:, :, :rank], compress[:, :, rank:]], 1)
    return jnp.einsum(
        "ljk,lki->lji", stacked, chooser, preferred_element_type=jnp.float32
    ).astype(jnp.bfloat16)


def real_form(both):
    rank = both.shape[1] // 2
    turned = jnp.concatenate([-both[:, rank:], both[:, :rank]], 1)
    return jnp.concatenate([both, turned], 2)


def compact_rows(matrix, slot):
    rank = slot.shape[1]
    parts = [
        jnp.dot(slot, half, preferred_element_type=jnp.float32)
        for half in (matrix[:rank], matrix[rank:])
    ]
    return jnp.concatenate(parts, 0).astype(jnp.bfloat16)


def times(matrix, value):
    return jnp.dot(matrix, value, preferred_element_type=jnp.float32).astype(jnp.bfloat16)


def sampled(sampling, traces):
    return jnp.einsum(
        "pc,tp->ct", sampling, traces, preferred_element_type=jnp.float32
    ).astype(jnp.bfloat16)


def evaluated(coeffs, evaluation):
    return jnp.einsum(
        "ct,cp->tp", coeffs, evaluation, preferred_element_type=jnp.float32
    ).astype(jnp.bfloat16)


def after(value, earlier):
    return value if earlier is None else lax.optimization_barrier((value, earlier))[0]


def all_hops():
    low_bits = lax.axis_size("sub").bit_length() - 1
    high_bits = lax.axis_size("bfly").bit_length() - 1
    return [("sub", bit) for bit in range(low_bits)] + [("bfly", bit) for bit in range(high_bits)]


def full_width(traces, sampling, skeleton, compress, evaluation):
    rank = skeleton.shape[-1]
    columns = picked_columns(compress, skeleton)
    full = jnp.concatenate([real_form(columns[..., :rank]), real_form(columns[..., rank:])], 2)
    coeffs = sampled_apart(sampling, traces)
    for level, hop in enumerate(all_hops()):
        partner = from_partner(coeffs, hop)
        coeffs = times(full[level], jnp.concatenate([coeffs, partner], 0))
    return evaluated(coeffs, evaluation)


def local(traces, sampling, skeleton, compress, evaluation):
    hops = all_hops()
    levels = len(hops)
    if levels != max(level for level, _ in ORDER):
        return full_width(traces, sampling[0], skeleton[0], compress[0], evaluation[0])
    wide = lax.axis_size("sub").bit_length() - 1
    rank = skeleton.shape[-1]
    room = rank * ROOM_SIXTEENTHS // 16
    unit = traces.shape[0] // sum(SHARES)
    pieces = len(SHARES)
    starts = [unit * sum(SHARES[:i]) for i in range(pieces + 1)]
    coeffs = early(sampling, traces, starts[: EARLY_PIECES + 1])
    full, small, extra = tables(after(skeleton, coeffs[0]), compress, wide, room)
    sampling, evaluation = sampling[0], evaluation[0]
    most_here = lax.broadcasted_iota(jnp.int32, extra.shape[1:], 1) >= rank

    def compact(level, piece):
        return level >= wide and piece >= FULL_PIECES[level - wide]

    inputs, partners, theirs, done = {}, {}, {}, [None] * pieces
    previous, finished, known = None, None, None
    for level, piece in ORDER:
        if (level, piece) == LOOK:
            known = after(after(partners[0], previous), partners[1])[:, starts[1] :]
            theirs[levels - 1] = known[:room, :rank]
            continue
        count = starts[piece + 1] - starts[piece]
        if level == 0:
            if piece < EARLY_PIECES:
                own = coeffs[piece]
            else:
                block = traces[starts[piece] : starts[piece + 1]]
                own = sampled(after(sampling, previous), block)
        else:
            arrived = after(partners[piece], previous)
            if level == levels:
                arrived = after(arrived, finished)
            elif piece == 0 and level - 1 >= wide:
                known = arrived[:, count:]
                theirs[level - 1] = known[:room, :rank]
            value = jnp.concatenate([inputs[piece], arrived[:, :count]], 0)
            matrix = full[level - 1]
            if compact(level - 1, piece):
                value = jnp.pad(value, ((0, full.shape[2] - value.shape[0]), (0, 0)))
                matrix = small[level - 1]
            if level < levels and compact(level, piece):
                outgoing = times(compact_rows(matrix, theirs[level]), value)
                own = times(after(matrix, outgoing), value)
            else:
                own = outgoing = times(matrix, value)
        if level == levels:
            done[piece] = finished = previous = evaluated(own, evaluation)
            if piece == COUNT_READ:
                most = jnp.maximum(most, after(counted, finished))
            continue
        if level == 0:
            outgoing = own
        if piece == 0 and level >= wide:
            block = extra[level]
            if known is not None:
                block = jnp.where(most_here, jnp.maximum(block, known), block)
            outgoing = jnp.concatenate([outgoing, block], 1)
        inputs[piece] = own
        partners[piece] = from_partner(outgoing, hops[level])
        previous = outgoing
        if (level, piece) == (levels - 1, COUNT_PIECE):
            most = after(jnp.maximum(extra[levels - 1], known)[:8, rank:], outgoing)
            for hop in hops[: wide - 1]:
                most = jnp.maximum(most, from_partner(most, hop))
            counted = from_partner(most, hops[wide - 1])
    quick = jnp.concatenate(done, 0)
    return lax.cond(
        most[0, 0] > room,
        lambda: full_width(traces, sampling, skeleton[0], compress[0], evaluation),
        lambda: quick,
    )


def solution(mesh):
    placed = (
        P(("shots", "tr"), ("bfly", "sub")),
        P(("bfly", "sub"), None, None),
        P(("bfly", "sub"), None, None),
        P(("bfly", "sub"), None, None, None),
        P(("bfly", "sub"), None, None),
    )
    return jax.shard_map(
        local,
        mesh=mesh,
        in_specs=placed,
        out_specs=P(("shots", "tr"), ("bfly", "sub")),
        check_vma=False,
    )
```

```python
import jax
import jax.numpy as jnp
from jax import lax
from jax.experimental import pallas as pl
from jax.experimental.pallas import tpu as pltpu
from jax.sharding import PartitionSpec as P

SHARES = (2, 5, 9, 9, 7)
FULL_PIECES = (2, 1)
EARLY_PIECES = 2
COUNT_PIECE = 2
COUNT_READ = 2
LOOK = (3, -1)
ORDER = (
    (0, 0), (0, 1), (0, 2), (1, 0), (1, 1), (0, 3), (2, 0), (1, 2), LOOK, (2, 1), (0, 4), (1, 3),
    (2, 2), (3, 0), (1, 4), (2, 3), (3, 1), (2, 4), (3, 2), (3, 3), (3, 4),
)
KERNEL_VMEM = 16 * 1024 * 1024
ROOM_SIXTEENTHS = 11


def route(axis, apart):
    count = lax.axis_size(axis)
    pairs = []
    for low in range(count):
        high = low | 1 << apart
        if high != low and high < count:
            pairs += [(low, high), (high, low)]
    return pairs


def from_partner(block, hop):
    return lax.ppermute(block, hop[0], route(*hop))


def across(left, right):
    return lax.dot_general(left, right, (((1,), (1,)), ((), ())), preferred_element_type=jnp.float32)


def one_hot(condition):
    return jnp.where(condition, 1.0, 0.0).astype(jnp.bfloat16)


def sampled_block(sampling, rows):
    turned = sampling.astype(jnp.float32).T.astype(jnp.bfloat16)
    return across(turned, rows).astype(jnp.bfloat16)


def early_kernel(starts, sampling_hbm, traces_hbm, *refs):
    pieces = len(starts) - 1
    outs, (sampling_ref, rows_ref, arrived) = refs[:pieces], refs[pieces:]
    loads = [pltpu.make_async_copy(sampling_hbm, sampling_ref, arrived.at[pieces])]
    for i in range(pieces):
        span = pl.ds(starts[i], starts[i + 1] - starts[i])
        loads.append(pltpu.make_async_copy(traces_hbm.at[span], rows_ref.at[span], arrived.at[i]))
    for load in loads:
        load.start()
    loads[0].wait()
    for i in range(pieces):
        loads[i + 1].wait()
        span = pl.ds(starts[i], starts[i + 1] - starts[i])
        outs[i][...] = sampled_block(sampling_ref[0], rows_ref[span])


def early(sampling, traces, starts):
    pieces = len(starts) - 1
    width = sampling.shape[-1]
    total = starts[-1]
    return pl.pallas_call(
        lambda *refs: early_kernel(starts, *refs),
        out_shape=[
            jax.ShapeDtypeStruct((width, starts[i + 1] - starts[i]), jnp.bfloat16) for i in range(pieces)
        ],
        in_specs=[pl.BlockSpec(memory_space=pltpu.HBM)] * 2,
        out_specs=[pl.BlockSpec(memory_space=pltpu.VMEM)] * pieces,
        scratch_shapes=[
            pltpu.VMEM(sampling.shape, jnp.bfloat16),
            pltpu.VMEM((total, traces.shape[1]), jnp.bfloat16),
            pltpu.SemaphoreType.DMA((pieces + 1,)),
        ],
        compiler_params=pltpu.CompilerParams(vmem_limit_bytes=KERNEL_VMEM),
        cost_estimate=pl.CostEstimate(
            flops=2 * total * width * width, bytes_accessed=4 * total * width, transcendentals=0
        ),
        name="early",
    )(sampling, traces)


def tables_kernel(
    wide, room, skeleton_hbm, compress_hbm, full_ref, small_ref, extra_ref,
    skeleton_ref, compress_ref, arrived,
):
    loads = [
        pltpu.make_async_copy(skeleton_hbm, skeleton_ref, arrived.at[0]),
        pltpu.make_async_copy(compress_hbm, compress_ref, arrived.at[1]),
    ]
    for load in loads:
        load.start()
    for load in loads:
        load.wait()
    levels, rank = skeleton_ref.shape[0], skeleton_ref.shape[-1]
    width = 2 * rank
    f32, i32 = jnp.float32, jnp.int32
    k = lax.broadcasted_iota(i32, (width, width), 1)
    twice = one_hot(lax.broadcasted_iota(i32, (width, rank), 0) % rank == lax.broadcasted_iota(i32, (width, rank), 1))
    earlier = one_hot(
        (lax.broadcasted_iota(i32, (width, width), 1) < lax.broadcasted_iota(i32, (width, width), 0) % rank)
    )
    column = lax.broadcasted_iota(i32, (2 * width, width), 0)
    is_real_entry = lax.broadcasted_iota(i32, (2 * width, width), 1) < rank
    partner_column = column >= width
    imag_column = column % width >= rank
    coefficient = column % rank + jnp.where(partner_column, rank, 0)
    slot_column = column - width
    slot_imag = slot_column >= room
    slot_of_column = jnp.where(slot_imag, slot_column - room, slot_column)
    row = lax.broadcasted_iota(i32, (width, width), 0)
    most = jnp.zeros((1, 1), f32)
    for level in range(levels):
        entry = jnp.broadcast_to(skeleton_ref[level].astype(f32), (8, rank)).astype(jnp.bfloat16)
        entry = across(entry, twice)[:1]
        picked = jnp.where(entry >= rank, 1.0, 0.0)
        slot = across(jnp.broadcast_to(picked, (8, width)).astype(jnp.bfloat16), earlier)[:1].astype(i32)
        entry = entry.astype(i32)
        from_partner_entry = entry >= rank
        matrix = compress_ref[0, level]

        def halves(match, imag):
            same = is_real_entry != imag
            real = jnp.where(match & same, jnp.where(imag, -1.0, 1.0), 0.0).astype(jnp.bfloat16)
            turned = one_hot(match & jnp.logical_not(same))
            return across(matrix, real).astype(jnp.bfloat16), across(matrix, turned).astype(jnp.bfloat16)

        match = entry == coefficient
        full_ref[level, :rank], full_ref[level, rank:] = halves(match, imag_column)
        compacted = (slot == slot_of_column) & from_partner_entry
        match = (match & jnp.logical_not(partner_column)) | (compacted & partner_column)
        imag = (imag_column & jnp.logical_not(partner_column)) | (slot_imag & partner_column)
        small_ref[level, :rank], small_ref[level, rank:] = halves(match, imag)
        once = (k < rank) & from_partner_entry
        places = across(one_hot(once & (slot == row)), one_hot(once & (entry - rank == row)))
        extra_ref[level] = places.astype(jnp.bfloat16)
        if level >= wide:
            most = jnp.maximum(most, jnp.sum(picked, axis=1, keepdims=True) * 0.5)
    for level in range(wide, levels):
        extra_ref[level] = jnp.where(k < rank, extra_ref[level].astype(f32), most).astype(jnp.bfloat16)


def tables(skeleton, compress, wide, room):
    levels, rank = skeleton.shape[1:]
    shape = (levels, 2 * rank, 4 * rank)
    return pl.pallas_call(
        lambda *refs: tables_kernel(wide, room, *refs),
        out_shape=[
            jax.ShapeDtypeStruct(shape, jnp.bfloat16),
            jax.ShapeDtypeStruct(shape, jnp.bfloat16),
            jax.ShapeDtypeStruct((levels, 2 * rank, 2 * rank), jnp.bfloat16),
        ],
        in_specs=[pl.BlockSpec(memory_space=pltpu.HBM)] * 2,
        out_specs=[pl.BlockSpec(memory_space=pltpu.VMEM)] * 3,
        scratch_shapes=[
            pltpu.VMEM((levels, 1, rank), jnp.int32),
            pltpu.VMEM(compress.shape, jnp.bfloat16),
            pltpu.SemaphoreType.DMA((2,)),
        ],
        compiler_params=pltpu.CompilerParams(vmem_limit_bytes=KERNEL_VMEM),
        cost_estimate=pl.CostEstimate(flops=50_000_000, bytes_accessed=600_000, transcendentals=0),
        name="tables",
    )(skeleton.transpose(1, 0, 2), compress)


def sampled_apart(sampling, traces):
    count, width = traces.shape
    block = count // 8

    def kernel(sampling_ref, rows_ref, coeffs_ref):
        coeffs_ref[...] = sampled_block(sampling_ref[...], rows_ref[...])

    return pl.pallas_call(
        kernel,
        grid=(count // block,),
        out_shape=jax.ShapeDtypeStruct((sampling.shape[1], count), jnp.bfloat16),
        in_specs=[
            pl.BlockSpec(sampling.shape, lambda i: (0, 0)),
            pl.BlockSpec((block, width), lambda i: (i, 0)),
        ],
        out_specs=pl.BlockSpec((sampling.shape[1], block), lambda i: (0, i)),
        compiler_params=pltpu.CompilerParams(vmem_limit_bytes=63 * 1024 * 1024),
        name="sampled_apart",
    )(sampling, traces)


def picked_columns(compress, skeleton):
    rank = skeleton.shape[-1]
    places = lax.broadcasted_iota(jnp.int32, (1, 1, 2 * rank), 2)
    chooser = (skeleton[:, :, None] == places).astype(jnp.bfloat16)
    stacked = jnp.concatenate([compress[:, :, :rank], compress[:, :, rank:]], 1)
    return jnp.einsum(
        "ljk,lki->lji", stacked, chooser, preferred_element_type=jnp.float32
    ).astype(jnp.bfloat16)


def real_form(both):
    rank = both.shape[1] // 2
    turned = jnp.concatenate([-both[:, rank:], both[:, :rank]], 1)
    return jnp.concatenate([both, turned], 2)


def compact_rows(matrix, slot):
    rank = slot.shape[1]
    parts = [
        jnp.dot(slot, half, preferred_element_type=jnp.float32)
        for half in (matrix[:rank], matrix[rank:])
    ]
    return jnp.concatenate(parts, 0).astype(jnp.bfloat16)


def times(matrix, value):
    return jnp.dot(matrix, value, preferred_element_type=jnp.float32).astype(jnp.bfloat16)


def sampled(sampling, traces):
    return jnp.einsum(
        "pc,tp->ct", sampling, traces, preferred_element_type=jnp.float32
    ).astype(jnp.bfloat16)


def evaluated(coeffs, evaluation):
    return jnp.einsum(
        "ct,cp->tp", coeffs, evaluation, preferred_element_type=jnp.float32
    ).astype(jnp.bfloat16)


def after(value, earlier):
    return value if earlier is None else lax.optimization_barrier((value, earlier))[0]


def all_hops():
    low_bits = lax.axis_size("sub").bit_length() - 1
    high_bits = lax.axis_size("bfly").bit_length() - 1
    return [("sub", bit) for bit in range(low_bits)] + [("bfly", bit) for bit in range(high_bits)]


def full_width(traces, sampling, skeleton, compress, evaluation):
    rank = skeleton.shape[-1]
    columns = picked_columns(compress, skeleton)
    full = jnp.concatenate([real_form(columns[..., :rank]), real_form(columns[..., rank:])], 2)
    coeffs = sampled_apart(sampling, traces)
    for level, hop in enumerate(all_hops()):
        partner = from_partner(coeffs, hop)
        coeffs = times(full[level], jnp.concatenate([coeffs, partner], 0))
    return evaluated(coeffs, evaluation)


def local(traces, sampling, skeleton, compress, evaluation):
    hops = all_hops()
    levels = len(hops)
    if levels != max(level for level, _ in ORDER):
        return full_width(traces, sampling[0], skeleton[0], compress[0], evaluation[0])
    wide = lax.axis_size("sub").bit_length() - 1
    rank = skeleton.shape[-1]
    room = rank * ROOM_SIXTEENTHS // 16
    unit = traces.shape[0] // sum(SHARES)
    pieces = len(SHARES)
    starts = [unit * sum(SHARES[:i]) for i in range(pieces + 1)]
    coeffs = early(sampling, traces, starts[: EARLY_PIECES + 1])
    full, small, extra = tables(after(skeleton, coeffs[0]), compress, wide, room)
    sampling, evaluation = sampling[0], evaluation[0]
    most_here = lax.broadcasted_iota(jnp.int32, extra.shape[1:], 1) >= rank

    def compact(level, piece):
        return level >= wide and piece >= FULL_PIECES[level - wide]

    inputs, partners, theirs, done = {}, {}, {}, [None] * pieces
    previous, finished, known = None, None, None
    for level, piece in ORDER:
        if (level, piece) == LOOK:
            known = after(after(partners[0], previous), partners[1])[:, starts[1] :]
            theirs[levels - 1] = known[:room, :rank]
            continue
        count = starts[piece + 1] - starts[piece]
        if level == 0:
            if piece < EARLY_PIECES:
                own = coeffs[piece]
            else:
                block = traces[starts[piece] : starts[piece + 1]]
                own = sampled(after(sampling, previous), block)
        else:
            arrived = after(partners[piece], previous)
            if level == levels:
                arrived = after(arrived, finished)
            elif piece == 0 and level - 1 >= wide:
                known = arrived[:, count:]
                theirs[level - 1] = known[:room, :rank]
            value = jnp.concatenate([inputs[piece], arrived[:, :count]], 0)
            matrix = full[level - 1]
            if compact(level - 1, piece):
                value = jnp.pad(value, ((0, full.shape[2] - value.shape[0]), (0, 0)))
                matrix = small[level - 1]
            if level < levels and compact(level, piece):
                outgoing = times(compact_rows(matrix, theirs[level]), value)
                own = times(after(matrix, outgoing), value)
            else:
                own = outgoing = times(matrix, value)
        if level == levels:
            done[piece] = finished = previous = evaluated(own, evaluation)
            if piece == COUNT_READ:
                most = jnp.maximum(most, after(counted, finished))
            continue
        if level == 0:
            outgoing = own
        if piece == 0 and level >= wide:
            block = extra[level]
            if known is not None:
                block = jnp.where(most_here, jnp.maximum(block, known), block)
            outgoing = jnp.concatenate([outgoing, block], 1)
        inputs[piece] = own
        partners[piece] = from_partner(outgoing, hops[level])
        previous = outgoing
        if (level, piece) == (levels - 1, COUNT_PIECE):
            most = after(jnp.maximum(extra[levels - 1], known)[:8, rank:], outgoing)
            for hop in hops[: wide - 1]:
                most = jnp.maximum(most, from_partner(most, hop))
            counted = from_partner(most, hops[wide - 1])
    quick = jnp.concatenate(done, 0)
    return lax.cond(
        most[0, 0] > room,
        lambda: full_width(traces, sampling, skeleton[0], compress[0], evaluation),
        lambda: quick,
    )


def solution(mesh):
    placed = (
        P(("shots", "tr"), ("bfly", "sub")),
        P(("bfly", "sub"), None, None),
        P(("bfly", "sub"), None, None),
        P(("bfly", "sub"), None, None, None),
        P(("bfly", "sub"), None, None),
    )
    return jax.shard_map(
        local,
        mesh=mesh,
        in_specs=placed,
        out_specs=P(("shots", "tr"), ("bfly", "sub")),
        check_vma=False,
    )
```

```python
import jax
import jax.numpy as jnp
from jax import lax
from jax.experimental import pallas as pl
from jax.experimental.pallas import tpu as pltpu
from jax.sharding import PartitionSpec as P

SHARES = (2, 5, 7, 9, 9)
FULL_PIECES = (2, 1)
EARLY_PIECES = 2
COUNT_PIECE = 2
COUNT_READ = 2
LOOK = (3, -1)
MAKE = (0, -1)
ORDER = (
    (0, 0), (0, 1), (0, 2), (1, 0), (1, 1), MAKE, (2, 0), (0, 3), (1, 2), LOOK, (2, 1), (0, 4), (1, 3),
    (2, 2), (3, 0), (1, 4), (2, 3), (3, 1), (2, 4), (3, 2), (3, 3), (3, 4),
)
KERNEL_VMEM = 16 * 1024 * 1024
ROOM_SIXTEENTHS = 11


def route(axis, apart):
    count = lax.axis_size(axis)
    pairs = []
    for low in range(count):
        high = low | 1 << apart
        if high != low and high < count:
            pairs += [(low, high), (high, low)]
    return pairs


def from_partner(block, hop):
    return lax.ppermute(block, hop[0], route(*hop))


def across(left, right):
    return lax.dot_general(left, right, (((1,), (1,)), ((), ())), preferred_element_type=jnp.float32)


def one_hot(condition):
    return jnp.where(condition, 1.0, 0.0).astype(jnp.bfloat16)


def sampled_block(sampling, rows):
    turned = sampling.astype(jnp.float32).T.astype(jnp.bfloat16)
    return across(turned, rows).astype(jnp.bfloat16)


def early_kernel(starts, sampling_hbm, traces_hbm, *refs):
    pieces = len(starts) - 1
    outs, (sampling_ref, rows_ref, arrived) = refs[:pieces], refs[pieces:]
    loads = [pltpu.make_async_copy(sampling_hbm, sampling_ref, arrived.at[pieces])]
    for i in range(pieces):
        span = pl.ds(starts[i], starts[i + 1] - starts[i])
        loads.append(pltpu.make_async_copy(traces_hbm.at[span], rows_ref.at[span], arrived.at[i]))
    for load in loads:
        load.start()
    loads[0].wait()
    for i in range(pieces):
        loads[i + 1].wait()
        span = pl.ds(starts[i], starts[i + 1] - starts[i])
        outs[i][...] = sampled_block(sampling_ref[0], rows_ref[span])


def early(sampling, traces, starts):
    pieces = len(starts) - 1
    width = sampling.shape[-1]
    total = starts[-1]
    return pl.pallas_call(
        lambda *refs: early_kernel(starts, *refs),
        out_shape=[
            jax.ShapeDtypeStruct((width, starts[i + 1] - starts[i]), jnp.bfloat16) for i in range(pieces)
        ],
        in_specs=[pl.BlockSpec(memory_space=pltpu.HBM)] * 2,
        out_specs=[pl.BlockSpec(memory_space=pltpu.VMEM)] * pieces,
        scratch_shapes=[
            pltpu.VMEM(sampling.shape, jnp.bfloat16),
            pltpu.VMEM((total, traces.shape[1]), jnp.bfloat16),
            pltpu.SemaphoreType.DMA((pieces + 1,)),
        ],
        compiler_params=pltpu.CompilerParams(vmem_limit_bytes=KERNEL_VMEM),
        cost_estimate=pl.CostEstimate(
            flops=2 * total * width * width, bytes_accessed=4 * total * width, transcendentals=0
        ),
        name="early",
    )(sampling, traces)


def tables_kernel(
    wide, room, skeleton_hbm, compress_hbm, full_ref, small_ref, extra_ref,
    skeleton_ref, compress_ref, arrived,
):
    loads = [
        pltpu.make_async_copy(skeleton_hbm, skeleton_ref, arrived.at[0]),
        pltpu.make_async_copy(compress_hbm, compress_ref, arrived.at[1]),
    ]
    for load in loads:
        load.start()
    for load in loads:
        load.wait()
    levels, rank = skeleton_ref.shape[0], skeleton_ref.shape[-1]
    width = 2 * rank
    f32, i32 = jnp.float32, jnp.int32
    k = lax.broadcasted_iota(i32, (width, width), 1)
    twice = one_hot(lax.broadcasted_iota(i32, (width, rank), 0) % rank == lax.broadcasted_iota(i32, (width, rank), 1))
    earlier = one_hot(
        (lax.broadcasted_iota(i32, (width, width), 1) < lax.broadcasted_iota(i32, (width, width), 0) % rank)
    )
    column = lax.broadcasted_iota(i32, (2 * width, width), 0)
    is_real_entry = lax.broadcasted_iota(i32, (2 * width, width), 1) < rank
    partner_column = column >= width
    imag_column = column % width >= rank
    coefficient = column % rank + jnp.where(partner_column, rank, 0)
    slot_column = column - width
    slot_imag = slot_column >= room
    slot_of_column = jnp.where(slot_imag, slot_column - room, slot_column)
    row = lax.broadcasted_iota(i32, (width, width), 0)
    most = jnp.zeros((1, 1), f32)
    for level in range(levels):
        entry = jnp.broadcast_to(skeleton_ref[level].astype(f32), (8, rank)).astype(jnp.bfloat16)
        entry = across(entry, twice)[:1]
        picked = jnp.where(entry >= rank, 1.0, 0.0)
        slot = across(jnp.broadcast_to(picked, (8, width)).astype(jnp.bfloat16), earlier)[:1].astype(i32)
        entry = entry.astype(i32)
        from_partner_entry = entry >= rank
        matrix = compress_ref[0, level]

        def halves(match, imag):
            same = is_real_entry != imag
            real = jnp.where(match & same, jnp.where(imag, -1.0, 1.0), 0.0).astype(jnp.bfloat16)
            turned = one_hot(match & jnp.logical_not(same))
            return across(matrix, real).astype(jnp.bfloat16), across(matrix, turned).astype(jnp.bfloat16)

        match = entry == coefficient
        full_ref[level, :rank], full_ref[level, rank:] = halves(match, imag_column)
        compacted = (slot == slot_of_column) & from_partner_entry
        match = (match & jnp.logical_not(partner_column)) | (compacted & partner_column)
        imag = (imag_column & jnp.logical_not(partner_column)) | (slot_imag & partner_column)
        small_ref[level, :rank], small_ref[level, rank:] = halves(match, imag)
        once = (k < rank) & from_partner_entry
        places = across(one_hot(once & (slot == row)), one_hot(once & (entry - rank == row)))
        extra_ref[level] = places.astype(jnp.bfloat16)
        if level >= wide:
            most = jnp.maximum(most, jnp.sum(picked, axis=1, keepdims=True) * 0.5)
    for level in range(wide, levels):
        extra_ref[level] = jnp.where(k < rank, extra_ref[level].astype(f32), most).astype(jnp.bfloat16)


def tables(skeleton, compress, wide, room):
    levels, rank = skeleton.shape[1:]
    shape = (levels, 2 * rank, 4 * rank)
    return pl.pallas_call(
        lambda *refs: tables_kernel(wide, room, *refs),
        out_shape=[
            jax.ShapeDtypeStruct(shape, jnp.bfloat16),
            jax.ShapeDtypeStruct(shape, jnp.bfloat16),
            jax.ShapeDtypeStruct((levels, 2 * rank, 2 * rank), jnp.bfloat16),
        ],
        in_specs=[pl.BlockSpec(memory_space=pltpu.HBM)] * 2,
        out_specs=[pl.BlockSpec(memory_space=pltpu.VMEM)] * 3,
        scratch_shapes=[
            pltpu.VMEM((levels, 1, rank), jnp.int32),
            pltpu.VMEM(compress.shape, jnp.bfloat16),
            pltpu.SemaphoreType.DMA((2,)),
        ],
        compiler_params=pltpu.CompilerParams(vmem_limit_bytes=KERNEL_VMEM),
        cost_estimate=pl.CostEstimate(flops=50_000_000, bytes_accessed=600_000, transcendentals=0),
        name="tables",
    )(skeleton.transpose(1, 0, 2), compress)


def sampled_apart(sampling, traces):
    count, width = traces.shape
    block = count // 8

    def kernel(sampling_ref, rows_ref, coeffs_ref):
        coeffs_ref[...] = sampled_block(sampling_ref[...], rows_ref[...])

    return pl.pallas_call(
        kernel,
        grid=(count // block,),
        out_shape=jax.ShapeDtypeStruct((sampling.shape[1], count), jnp.bfloat16),
        in_specs=[
            pl.BlockSpec(sampling.shape, lambda i: (0, 0)),
            pl.BlockSpec((block, width), lambda i: (i, 0)),
        ],
        out_specs=pl.BlockSpec((sampling.shape[1], block), lambda i: (0, i)),
        compiler_params=pltpu.CompilerParams(vmem_limit_bytes=63 * 1024 * 1024),
        name="sampled_apart",
    )(sampling, traces)


def picked_columns(compress, skeleton):
    rank = skeleton.shape[-1]
    places = lax.broadcasted_iota(jnp.int32, (1, 1, 2 * rank), 2)
    chooser = (skeleton[:, :, None] == places).astype(jnp.bfloat16)
    stacked = jnp.concatenate([compress[:, :, :rank], compress[:, :, rank:]], 1)
    return jnp.einsum(
        "ljk,lki->lji", stacked, chooser, preferred_element_type=jnp.float32
    ).astype(jnp.bfloat16)


def real_form(both):
    rank = both.shape[1] // 2
    turned = jnp.concatenate([-both[:, rank:], both[:, :rank]], 1)
    return jnp.concatenate([both, turned], 2)


def compact_rows(matrix, slot):
    rank = slot.shape[1]
    parts = [
        jnp.dot(slot, half, preferred_element_type=jnp.float32)
        for half in (matrix[:rank], matrix[rank:])
    ]
    return jnp.concatenate(parts, 0).astype(jnp.bfloat16)


def times(matrix, value):
    return jnp.dot(matrix, value, preferred_element_type=jnp.float32).astype(jnp.bfloat16)


def sampled(sampling, traces):
    return jnp.einsum(
        "pc,tp->ct", sampling, traces, preferred_element_type=jnp.float32
    ).astype(jnp.bfloat16)


def evaluated(coeffs, evaluation):
    return jnp.einsum(
        "ct,cp->tp", coeffs, evaluation, preferred_element_type=jnp.float32
    ).astype(jnp.bfloat16)


def after(value, earlier):
    return value if earlier is None else lax.optimization_barrier((value, earlier))[0]


def all_hops():
    low_bits = lax.axis_size("sub").bit_length() - 1
    high_bits = lax.axis_size("bfly").bit_length() - 1
    return [("sub", bit) for bit in range(low_bits)] + [("bfly", bit) for bit in range(high_bits)]


def full_width(traces, sampling, skeleton, compress, evaluation):
    rank = skeleton.shape[-1]
    columns = picked_columns(compress, skeleton)
    full = jnp.concatenate([real_form(columns[..., :rank]), real_form(columns[..., rank:])], 2)
    coeffs = sampled_apart(sampling, traces)
    for level, hop in enumerate(all_hops()):
        partner = from_partner(coeffs, hop)
        coeffs = times(full[level], jnp.concatenate([coeffs, partner], 0))
    return evaluated(coeffs, evaluation)


def local(traces, sampling, skeleton, compress, evaluation):
    hops = all_hops()
    levels = len(hops)
    if levels != max(level for level, _ in ORDER):
        return full_width(traces, sampling[0], skeleton[0], compress[0], evaluation[0])
    wide = lax.axis_size("sub").bit_length() - 1
    rank = skeleton.shape[-1]
    room = rank * ROOM_SIXTEENTHS // 16
    unit = traces.shape[0] // sum(SHARES)
    pieces = len(SHARES)
    starts = [unit * sum(SHARES[:i]) for i in range(pieces + 1)]
    coeffs = list(early(sampling, traces, starts[: EARLY_PIECES + 1]))
    full, small, extra = tables(after(skeleton, coeffs[0]), compress, wide, room)
    sampling, evaluation = sampling[0], evaluation[0]
    most_here = lax.broadcasted_iota(jnp.int32, extra.shape[1:], 1) >= rank

    def compact(level, piece):
        return level >= wide and piece >= FULL_PIECES[level - wide]

    inputs, partners, theirs, done = {}, {}, {}, [None] * pieces
    previous, finished, known = None, None, None
    for level, piece in ORDER:
        if (level, piece) == MAKE:
            waiting = after(sampling, previous)
            for late in range(len(coeffs), pieces):
                coeffs.append(sampled(waiting, traces[starts[late] : starts[late + 1]]))
            previous = coeffs[-1]
            continue
        if (level, piece) == LOOK:
            known = after(after(partners[0], previous), partners[1])[:, starts[1] :]
            theirs[levels - 1] = known[:room, :rank]
            continue
        count = starts[piece + 1] - starts[piece]
        if level == 0:
            if piece == len(coeffs):
                coeffs.append(sampled(after(sampling, previous), traces[starts[piece] : starts[piece + 1]]))
            own = coeffs[piece]
        else:
            arrived = after(partners[piece], previous)
            if level == levels:
                arrived = after(arrived, finished)
            elif piece == 0 and level - 1 >= wide:
                known = arrived[:, count:]
                theirs[level - 1] = known[:room, :rank]
            value = jnp.concatenate([inputs[piece], arrived[:, :count]], 0)
            matrix = full[level - 1]
            if compact(level - 1, piece):
                value = jnp.pad(value, ((0, full.shape[2] - value.shape[0]), (0, 0)))
                matrix = small[level - 1]
            if level < levels and compact(level, piece):
                outgoing = times(compact_rows(matrix, theirs[level]), value)
                own = times(after(matrix, outgoing), value)
            else:
                own = outgoing = times(matrix, value)
        if level == levels:
            done[piece] = finished = previous = evaluated(own, evaluation)
            if piece == COUNT_READ:
                most = jnp.maximum(most, after(counted, finished))
            continue
        if level == 0:
            outgoing = after(own, previous) if piece > EARLY_PIECES else own
        if piece == 0 and level >= wide:
            block = extra[level]
            if known is not None:
                block = jnp.where(most_here, jnp.maximum(block, known), block)
            outgoing = jnp.concatenate([outgoing, block], 1)
        inputs[piece] = own
        partners[piece] = from_partner(outgoing, hops[level])
        previous = outgoing
        if (level, piece) == (levels - 1, COUNT_PIECE):
            most = after(jnp.maximum(extra[levels - 1], known)[:8, rank:], outgoing)
            for hop in hops[: wide - 1]:
                most = jnp.maximum(most, from_partner(most, hop))
            counted = from_partner(most, hops[wide - 1])
    quick = jnp.concatenate(done, 0)
    return lax.cond(
        most[0, 0] > room,
        lambda: full_width(traces, sampling, skeleton[0], compress[0], evaluation),
        lambda: quick,
    )


def solution(mesh):
    placed = (
        P(("shots", "tr"), ("bfly", "sub")),
        P(("bfly", "sub"), None, None),
        P(("bfly", "sub"), None, None),
        P(("bfly", "sub"), None, None, None),
        P(("bfly", "sub"), None, None),
    )
    return jax.shard_map(
        local,
        mesh=mesh,
        in_specs=placed,
        out_specs=P(("shots", "tr"), ("bfly", "sub")),
        check_vma=False,
    )
```

```python
import jax
import jax.numpy as jnp
from jax import lax
from jax.experimental import pallas as pl
from jax.experimental.pallas import tpu as pltpu
from jax.sharding import PartitionSpec as P

SHARES = (2, 5, 9, 9, 7)
FULL_PIECES = (2, 1)
EARLY_PIECES = 2
COUNT_PIECE = 2
COUNT_READ = 2
LOOK = (3, -1)
ORDER = (
    (0, 0), (0, 1), (0, 2), (1, 0), (1, 1), (0, 3), (2, 0), (1, 2), LOOK, (2, 1), (0, 4), (1, 3),
    (2, 2), (3, 0), (1, 4), (2, 3), (3, 1), (2, 4), (3, 2), (3, 3), (3, 4),
)
KERNEL_VMEM = 16 * 1024 * 1024
ROOM_SIXTEENTHS = (11, 10)


def route(axis, apart):
    count = lax.axis_size(axis)
    pairs = []
    for low in range(count):
        high = low | 1 << apart
        if high != low and high < count:
            pairs += [(low, high), (high, low)]
    return pairs


def from_partner(block, hop):
    return lax.ppermute(block, hop[0], route(*hop))


def across(left, right):
    return lax.dot_general(left, right, (((1,), (1,)), ((), ())), preferred_element_type=jnp.float32)


def one_hot(condition):
    return jnp.where(condition, 1.0, 0.0).astype(jnp.bfloat16)


def sampled_block(sampling, rows):
    turned = sampling.astype(jnp.float32).T.astype(jnp.bfloat16)
    return across(turned, rows).astype(jnp.bfloat16)


def early_kernel(starts, sampling_hbm, traces_hbm, *refs):
    pieces = len(starts) - 1
    outs, (sampling_ref, rows_ref, arrived) = refs[:pieces], refs[pieces:]
    loads = [pltpu.make_async_copy(sampling_hbm, sampling_ref, arrived.at[pieces])]
    for i in range(pieces):
        span = pl.ds(starts[i], starts[i + 1] - starts[i])
        loads.append(pltpu.make_async_copy(traces_hbm.at[span], rows_ref.at[span], arrived.at[i]))
    for load in loads:
        load.start()
    loads[0].wait()
    for i in range(pieces):
        loads[i + 1].wait()
        span = pl.ds(starts[i], starts[i + 1] - starts[i])
        outs[i][...] = sampled_block(sampling_ref[0], rows_ref[span])


def early(sampling, traces, starts):
    pieces = len(starts) - 1
    width = sampling.shape[-1]
    total = starts[-1]
    return pl.pallas_call(
        lambda *refs: early_kernel(starts, *refs),
        out_shape=[
            jax.ShapeDtypeStruct((width, starts[i + 1] - starts[i]), jnp.bfloat16) for i in range(pieces)
        ],
        in_specs=[pl.BlockSpec(memory_space=pltpu.HBM)] * 2,
        out_specs=[pl.BlockSpec(memory_space=pltpu.VMEM)] * pieces,
        scratch_shapes=[
            pltpu.VMEM(sampling.shape, jnp.bfloat16),
            pltpu.VMEM((total, traces.shape[1]), jnp.bfloat16),
            pltpu.SemaphoreType.DMA((pieces + 1,)),
        ],
        compiler_params=pltpu.CompilerParams(vmem_limit_bytes=KERNEL_VMEM),
        cost_estimate=pl.CostEstimate(
            flops=2 * total * width * width, bytes_accessed=4 * total * width, transcendentals=0
        ),
        name="early",
    )(sampling, traces)


def tables_kernel(
    wide, rooms, skeleton_hbm, compress_hbm, full_ref, small_ref, extra_ref,
    skeleton_ref, compress_ref, arrived,
):
    loads = [
        pltpu.make_async_copy(skeleton_hbm, skeleton_ref, arrived.at[0]),
        pltpu.make_async_copy(compress_hbm, compress_ref, arrived.at[1]),
    ]
    for load in loads:
        load.start()
    for load in loads:
        load.wait()
    levels, rank = skeleton_ref.shape[0], skeleton_ref.shape[-1]
    width = 2 * rank
    f32, i32 = jnp.float32, jnp.int32
    k = lax.broadcasted_iota(i32, (width, width), 1)
    twice = one_hot(lax.broadcasted_iota(i32, (width, rank), 0) % rank == lax.broadcasted_iota(i32, (width, rank), 1))
    earlier = one_hot(
        (lax.broadcasted_iota(i32, (width, width), 1) < lax.broadcasted_iota(i32, (width, width), 0) % rank)
    )
    column = lax.broadcasted_iota(i32, (2 * width, width), 0)
    is_real_entry = lax.broadcasted_iota(i32, (2 * width, width), 1) < rank
    partner_column = column >= width
    imag_column = column % width >= rank
    coefficient = column % rank + jnp.where(partner_column, rank, 0)
    slot_column = column - width
    row = lax.broadcasted_iota(i32, (width, width), 0)
    most = jnp.full((1, 1), -float(rank), f32)
    for level in range(levels):
        entry = jnp.broadcast_to(skeleton_ref[level].astype(f32), (8, rank)).astype(jnp.bfloat16)
        entry = across(entry, twice)[:1]
        picked = jnp.where(entry >= rank, 1.0, 0.0)
        slot = across(jnp.broadcast_to(picked, (8, width)).astype(jnp.bfloat16), earlier)[:1].astype(i32)
        entry = entry.astype(i32)
        from_partner_entry = entry >= rank
        matrix = compress_ref[0, level]

        def halves(match, imag):
            same = is_real_entry != imag
            real = jnp.where(match & same, jnp.where(imag, -1.0, 1.0), 0.0).astype(jnp.bfloat16)
            turned = one_hot(match & jnp.logical_not(same))
            return across(matrix, real).astype(jnp.bfloat16), across(matrix, turned).astype(jnp.bfloat16)

        match = entry == coefficient
        full_ref[level, :rank], full_ref[level, rank:] = halves(match, imag_column)
        if level < wide:
            continue
        high = level - wide
        room = rooms[high]
        slot_imag = slot_column >= room
        slot_of_column = jnp.where(slot_imag, slot_column - room, slot_column)
        compacted = (slot == slot_of_column) & from_partner_entry
        match = (match & jnp.logical_not(partner_column)) | (compacted & partner_column)
        imag = (imag_column & jnp.logical_not(partner_column)) | (slot_imag & partner_column)
        small_ref[high, :rank], small_ref[high, rank:] = halves(match, imag)
        once = (k < rank) & from_partner_entry
        places = across(one_hot(once & (slot == row)), one_hot(once & (entry - rank == row)))
        extra_ref[high] = places.astype(jnp.bfloat16)
        most = jnp.maximum(most, jnp.sum(picked, axis=1, keepdims=True) * 0.5 - room)
    for high in range(levels - wide):
        extra_ref[high] = jnp.where(k < rank, extra_ref[high].astype(f32), most).astype(jnp.bfloat16)


def tables(skeleton, compress, wide, rooms):
    levels, rank = skeleton.shape[1:]
    shape = (levels, 2 * rank, 4 * rank)
    return pl.pallas_call(
        lambda *refs: tables_kernel(wide, rooms, *refs),
        out_shape=[
            jax.ShapeDtypeStruct(shape, jnp.bfloat16),
            jax.ShapeDtypeStruct((levels - wide,) + shape[1:], jnp.bfloat16),
            jax.ShapeDtypeStruct((levels - wide, 2 * rank, 2 * rank), jnp.bfloat16),
        ],
        in_specs=[pl.BlockSpec(memory_space=pltpu.HBM)] * 2,
        out_specs=[pl.BlockSpec(memory_space=pltpu.VMEM)] * 3,
        scratch_shapes=[
            pltpu.VMEM((levels, 1, rank), jnp.int32),
            pltpu.VMEM(compress.shape, jnp.bfloat16),
            pltpu.SemaphoreType.DMA((2,)),
        ],
        compiler_params=pltpu.CompilerParams(vmem_limit_bytes=KERNEL_VMEM),
        cost_estimate=pl.CostEstimate(flops=50_000_000, bytes_accessed=600_000, transcendentals=0),
        name="tables",
    )(skeleton.transpose(1, 0, 2), compress)


def sampled_apart(sampling, traces):
    count, width = traces.shape
    block = count // 8

    def kernel(sampling_ref, rows_ref, coeffs_ref):
        coeffs_ref[...] = sampled_block(sampling_ref[...], rows_ref[...])

    return pl.pallas_call(
        kernel,
        grid=(count // block,),
        out_shape=jax.ShapeDtypeStruct((sampling.shape[1], count), jnp.bfloat16),
        in_specs=[
            pl.BlockSpec(sampling.shape, lambda i: (0, 0)),
            pl.BlockSpec((block, width), lambda i: (i, 0)),
        ],
        out_specs=pl.BlockSpec((sampling.shape[1], block), lambda i: (0, i)),
        compiler_params=pltpu.CompilerParams(vmem_limit_bytes=63 * 1024 * 1024),
        name="sampled_apart",
    )(sampling, traces)


def picked_columns(compress, skeleton):
    rank = skeleton.shape[-1]
    places = lax.broadcasted_iota(jnp.int32, (1, 1, 2 * rank), 2)
    chooser = (skeleton[:, :, None] == places).astype(jnp.bfloat16)
    stacked = jnp.concatenate([compress[:, :, :rank], compress[:, :, rank:]], 1)
    return jnp.einsum(
        "ljk,lki->lji", stacked, chooser, preferred_element_type=jnp.float32
    ).astype(jnp.bfloat16)


def real_form(both):
    rank = both.shape[1] // 2
    turned = jnp.concatenate([-both[:, rank:], both[:, :rank]], 1)
    return jnp.concatenate([both, turned], 2)


def compact_rows(matrix, slot):
    rank = slot.shape[1]
    parts = [
        jnp.dot(slot, half, preferred_element_type=jnp.float32)
        for half in (matrix[:rank], matrix[rank:])
    ]
    return jnp.concatenate(parts, 0).astype(jnp.bfloat16)


def times(matrix, value):
    return jnp.dot(matrix, value, preferred_element_type=jnp.float32).astype(jnp.bfloat16)


def sampled(sampling, traces):
    return jnp.einsum(
        "pc,tp->ct", sampling, traces, preferred_element_type=jnp.float32
    ).astype(jnp.bfloat16)


def evaluated(coeffs, evaluation):
    return jnp.einsum(
        "ct,cp->tp", coeffs, evaluation, preferred_element_type=jnp.float32
    ).astype(jnp.bfloat16)


def after(value, earlier):
    return value if earlier is None else lax.optimization_barrier((value, earlier))[0]


def all_hops():
    low_bits = lax.axis_size("sub").bit_length() - 1
    high_bits = lax.axis_size("bfly").bit_length() - 1
    return [("sub", bit) for bit in range(low_bits)] + [("bfly", bit) for bit in range(high_bits)]


def full_width(traces, sampling, skeleton, compress, evaluation):
    rank = skeleton.shape[-1]
    columns = picked_columns(compress, skeleton)
    full = jnp.concatenate([real_form(columns[..., :rank]), real_form(columns[..., rank:])], 2)
    coeffs = sampled_apart(sampling, traces)
    for level, hop in enumerate(all_hops()):
        partner = from_partner(coeffs, hop)
        coeffs = times(full[level], jnp.concatenate([coeffs, partner], 0))
    return evaluated(coeffs, evaluation)


def local(traces, sampling, skeleton, compress, evaluation):
    hops = all_hops()
    levels = len(hops)
    if (lax.axis_size("sub"), lax.axis_size("bfly")) != (2, 4):
        return full_width(traces, sampling[0], skeleton[0], compress[0], evaluation[0])
    wide = lax.axis_size("sub").bit_length() - 1
    rank = skeleton.shape[-1]
    rooms = [rank * share // 16 for share in ROOM_SIXTEENTHS]
    unit = traces.shape[0] // sum(SHARES)
    pieces = len(SHARES)
    starts = [unit * sum(SHARES[:i]) for i in range(pieces + 1)]
    coeffs = early(sampling, traces, starts[: EARLY_PIECES + 1])
    full, small, extra = tables(after(skeleton, coeffs[0]), compress, wide, rooms)
    sampling, evaluation = sampling[0], evaluation[0]
    most_here = lax.broadcasted_iota(jnp.int32, extra.shape[1:], 1) >= rank

    def compact(level, piece):
        return level >= wide and piece >= FULL_PIECES[level - wide]

    inputs, partners, theirs, done = {}, {}, {}, [None] * pieces
    previous, finished, known = None, None, None
    for level, piece in ORDER:
        if (level, piece) == LOOK:
            known = after(after(partners[0], previous), partners[1])[:, starts[1] :]
            theirs[levels - 1] = known[: rooms[levels - 1 - wide], :rank]
            continue
        count = starts[piece + 1] - starts[piece]
        if level == 0:
            if piece < EARLY_PIECES:
                own = coeffs[piece]
            else:
                block = traces[starts[piece] : starts[piece + 1]]
                own = sampled(after(sampling, previous), block)
        else:
            arrived = after(partners[piece], previous)
            if level == levels:
                arrived = after(arrived, finished)
            elif piece == 0 and level - 1 >= wide:
                known = arrived[:, count:]
                theirs[level - 1] = known[: rooms[level - 1 - wide], :rank]
            value = jnp.concatenate([inputs[piece], arrived[:, :count]], 0)
            matrix = full[level - 1]
            if compact(level - 1, piece):
                value = jnp.pad(value, ((0, full.shape[2] - value.shape[0]), (0, 0)))
                matrix = small[level - 1 - wide]
            if level < levels and compact(level, piece):
                outgoing = times(compact_rows(matrix, theirs[level]), value)
                own = times(after(matrix, outgoing), value)
            else:
                own = outgoing = times(matrix, value)
        if level == levels:
            done[piece] = finished = previous = evaluated(own, evaluation)
            if piece == COUNT_READ:
                most = jnp.maximum(most, after(counted, finished))
            continue
        if level == 0:
            outgoing = own
        if piece == 0 and level >= wide:
            block = extra[level - wide]
            if known is not None:
                block = jnp.where(most_here, jnp.maximum(block, known), block)
            outgoing = jnp.concatenate([outgoing, block], 1)
        inputs[piece] = own
        partners[piece] = from_partner(outgoing, hops[level])
        previous = outgoing
        if (level, piece) == (levels - 1, COUNT_PIECE):
            most = after(jnp.maximum(extra[levels - 1 - wide], known)[:8, rank:], outgoing)
            for hop in hops[: wide - 1]:
                most = jnp.maximum(most, from_partner(most, hop))
            counted = from_partner(most, hops[wide - 1])
    quick = jnp.concatenate(done, 0)
    return lax.cond(
        most[0, 0] > 0,
        lambda: full_width(traces, sampling, skeleton[0], compress[0], evaluation),
        lambda: quick,
    )


def solution(mesh):
    placed = (
        P(("shots", "tr"), ("bfly", "sub")),
        P(("bfly", "sub"), None, None),
        P(("bfly", "sub"), None, None),
        P(("bfly", "sub"), None, None, None),
        P(("bfly", "sub"), None, None),
    )
    return jax.shard_map(
        local,
        mesh=mesh,
        in_specs=placed,
        out_specs=P(("shots", "tr"), ("bfly", "sub")),
        check_vma=False,
    )
```

```python
import jax
import jax.numpy as jnp
from jax import lax
from jax.experimental import pallas as pl
from jax.experimental.pallas import tpu as pltpu
from jax.sharding import PartitionSpec as P

SHARES = (2, 5, 9, 9, 7)
FULL_PIECES = (2, 1)
EARLY_PIECES = 2
COUNT_PIECE = 2
COUNT_READ = 2
LOOK = (3, -1)
ORDER = (
    (0, 0), (0, 1), (0, 2), (1, 0), (1, 1), (0, 3), (2, 0), (1, 2), LOOK, (2, 1), (1, 3), (2, 2),
    (0, 4), (3, 0), (1, 4), (2, 3), (3, 1), (2, 4), (3, 2), (3, 3), (3, 4),
)
KERNEL_VMEM = 16 * 1024 * 1024
ROOM_SIXTEENTHS = (11, 10)


def route(axis, apart):
    count = lax.axis_size(axis)
    pairs = []
    for low in range(count):
        high = low | 1 << apart
        if high != low and high < count:
            pairs += [(low, high), (high, low)]
    return pairs


def from_partner(block, hop):
    return lax.ppermute(block, hop[0], route(*hop))


def across(left, right):
    return lax.dot_general(left, right, (((1,), (1,)), ((), ())), preferred_element_type=jnp.float32)


def one_hot(condition):
    return jnp.where(condition, 1.0, 0.0).astype(jnp.bfloat16)


def sampled_block(sampling, rows):
    turned = sampling.astype(jnp.float32).T.astype(jnp.bfloat16)
    return across(turned, rows).astype(jnp.bfloat16)


def early_kernel(starts, sampling_hbm, traces_hbm, *refs):
    pieces = len(starts) - 1
    outs, (sampling_ref, rows_ref, arrived) = refs[:pieces], refs[pieces:]
    loads = [pltpu.make_async_copy(sampling_hbm, sampling_ref, arrived.at[pieces])]
    for i in range(pieces):
        span = pl.ds(starts[i], starts[i + 1] - starts[i])
        loads.append(pltpu.make_async_copy(traces_hbm.at[span], rows_ref.at[span], arrived.at[i]))
    for load in loads:
        load.start()
    loads[0].wait()
    for i in range(pieces):
        loads[i + 1].wait()
        span = pl.ds(starts[i], starts[i + 1] - starts[i])
        outs[i][...] = sampled_block(sampling_ref[0], rows_ref[span])


def early(sampling, traces, starts):
    pieces = len(starts) - 1
    width = sampling.shape[-1]
    total = starts[-1]
    return pl.pallas_call(
        lambda *refs: early_kernel(starts, *refs),
        out_shape=[
            jax.ShapeDtypeStruct((width, starts[i + 1] - starts[i]), jnp.bfloat16) for i in range(pieces)
        ],
        in_specs=[pl.BlockSpec(memory_space=pltpu.HBM)] * 2,
        out_specs=[pl.BlockSpec(memory_space=pltpu.VMEM)] * pieces,
        scratch_shapes=[
            pltpu.VMEM(sampling.shape, jnp.bfloat16),
            pltpu.VMEM((total, traces.shape[1]), jnp.bfloat16),
            pltpu.SemaphoreType.DMA((pieces + 1,)),
        ],
        compiler_params=pltpu.CompilerParams(vmem_limit_bytes=KERNEL_VMEM),
        cost_estimate=pl.CostEstimate(
            flops=2 * total * width * width, bytes_accessed=4 * total * width, transcendentals=0
        ),
        name="early",
    )(sampling, traces)


def tables_kernel(
    wide, rooms, skeleton_hbm, compress_hbm, full_ref, small_ref, extra_ref,
    skeleton_ref, compress_ref, arrived,
):
    loads = [
        pltpu.make_async_copy(skeleton_hbm, skeleton_ref, arrived.at[0]),
        pltpu.make_async_copy(compress_hbm, compress_ref, arrived.at[1]),
    ]
    for load in loads:
        load.start()
    for load in loads:
        load.wait()
    levels, rank = skeleton_ref.shape[0], skeleton_ref.shape[-1]
    width = 2 * rank
    f32, i32 = jnp.float32, jnp.int32
    k = lax.broadcasted_iota(i32, (width, width), 1)
    twice = one_hot(lax.broadcasted_iota(i32, (width, rank), 0) % rank == lax.broadcasted_iota(i32, (width, rank), 1))
    earlier = one_hot(
        (lax.broadcasted_iota(i32, (width, width), 1) < lax.broadcasted_iota(i32, (width, width), 0) % rank)
    )
    column = lax.broadcasted_iota(i32, (2 * width, width), 0)
    is_real_entry = lax.broadcasted_iota(i32, (2 * width, width), 1) < rank
    partner_column = column >= width
    imag_column = column % width >= rank
    coefficient = column % rank + jnp.where(partner_column, rank, 0)
    slot_column = column - width
    row = lax.broadcasted_iota(i32, (width, width), 0)
    most = jnp.full((1, 1), -float(rank), f32)
    for level in range(levels):
        entry = jnp.broadcast_to(skeleton_ref[level].astype(f32), (8, rank)).astype(jnp.bfloat16)
        entry = across(entry, twice)[:1]
        picked = jnp.where(entry >= rank, 1.0, 0.0)
        slot = across(jnp.broadcast_to(picked, (8, width)).astype(jnp.bfloat16), earlier)[:1].astype(i32)
        entry = entry.astype(i32)
        from_partner_entry = entry >= rank
        matrix = compress_ref[0, level]

        def halves(match, imag):
            same = is_real_entry != imag
            real = jnp.where(match & same, jnp.where(imag, -1.0, 1.0), 0.0).astype(jnp.bfloat16)
            turned = one_hot(match & jnp.logical_not(same))
            return across(matrix, real).astype(jnp.bfloat16), across(matrix, turned).astype(jnp.bfloat16)

        match = entry == coefficient
        full_ref[level, :rank], full_ref[level, rank:] = halves(match, imag_column)
        if level < wide:
            continue
        high = level - wide
        room = rooms[high]
        slot_imag = slot_column >= room
        slot_of_column = jnp.where(slot_imag, slot_column - room, slot_column)
        compacted = (slot == slot_of_column) & from_partner_entry
        match = (match & jnp.logical_not(partner_column)) | (compacted & partner_column)
        imag = (imag_column & jnp.logical_not(partner_column)) | (slot_imag & partner_column)
        small_ref[high, :rank], small_ref[high, rank:] = halves(match, imag)
        once = (k < rank) & from_partner_entry
        places = across(one_hot(once & (slot == row)), one_hot(once & (entry - rank == row)))
        extra_ref[high] = places.astype(jnp.bfloat16)
        most = jnp.maximum(most, jnp.sum(picked, axis=1, keepdims=True) * 0.5 - room)
    for high in range(levels - wide):
        extra_ref[high] = jnp.where(k < rank, extra_ref[high].astype(f32), most).astype(jnp.bfloat16)


def tables(skeleton, compress, wide, rooms):
    levels, rank = skeleton.shape[1:]
    shape = (levels, 2 * rank, 4 * rank)
    return pl.pallas_call(
        lambda *refs: tables_kernel(wide, rooms, *refs),
        out_shape=[
            jax.ShapeDtypeStruct(shape, jnp.bfloat16),
            jax.ShapeDtypeStruct((levels - wide,) + shape[1:], jnp.bfloat16),
            jax.ShapeDtypeStruct((levels - wide, 2 * rank, 2 * rank), jnp.bfloat16),
        ],
        in_specs=[pl.BlockSpec(memory_space=pltpu.HBM)] * 2,
        out_specs=[pl.BlockSpec(memory_space=pltpu.VMEM)] * 3,
        scratch_shapes=[
            pltpu.VMEM((levels, 1, rank), jnp.int32),
            pltpu.VMEM(compress.shape, jnp.bfloat16),
            pltpu.SemaphoreType.DMA((2,)),
        ],
        compiler_params=pltpu.CompilerParams(vmem_limit_bytes=KERNEL_VMEM),
        cost_estimate=pl.CostEstimate(flops=50_000_000, bytes_accessed=600_000, transcendentals=0),
        name="tables",
    )(skeleton.transpose(1, 0, 2), compress)


def sampled_apart(sampling, traces):
    count, width = traces.shape
    block = count // 8

    def kernel(sampling_ref, rows_ref, coeffs_ref):
        coeffs_ref[...] = sampled_block(sampling_ref[...], rows_ref[...])

    return pl.pallas_call(
        kernel,
        grid=(count // block,),
        out_shape=jax.ShapeDtypeStruct((sampling.shape[1], count), jnp.bfloat16),
        in_specs=[
            pl.BlockSpec(sampling.shape, lambda i: (0, 0)),
            pl.BlockSpec((block, width), lambda i: (i, 0)),
        ],
        out_specs=pl.BlockSpec((sampling.shape[1], block), lambda i: (0, i)),
        compiler_params=pltpu.CompilerParams(vmem_limit_bytes=63 * 1024 * 1024),
        name="sampled_apart",
    )(sampling, traces)


def picked_columns(compress, skeleton):
    rank = skeleton.shape[-1]
    places = lax.broadcasted_iota(jnp.int32, (1, 1, 2 * rank), 2)
    chooser = (skeleton[:, :, None] == places).astype(jnp.bfloat16)
    stacked = jnp.concatenate([compress[:, :, :rank], compress[:, :, rank:]], 1)
    return jnp.einsum(
        "ljk,lki->lji", stacked, chooser, preferred_element_type=jnp.float32
    ).astype(jnp.bfloat16)


def real_form(both):
    rank = both.shape[1] // 2
    turned = jnp.concatenate([-both[:, rank:], both[:, :rank]], 1)
    return jnp.concatenate([both, turned], 2)


def compact_rows(matrix, slot):
    rank = slot.shape[1]
    parts = [
        jnp.dot(slot, half, preferred_element_type=jnp.float32)
        for half in (matrix[:rank], matrix[rank:])
    ]
    return jnp.concatenate(parts, 0).astype(jnp.bfloat16)


def times(matrix, value):
    return jnp.dot(matrix, value, preferred_element_type=jnp.float32).astype(jnp.bfloat16)


def sampled(sampling, traces):
    return jnp.einsum(
        "pc,tp->ct", sampling, traces, preferred_element_type=jnp.float32
    ).astype(jnp.bfloat16)


def evaluated(coeffs, evaluation):
    return jnp.einsum(
        "ct,cp->tp", coeffs, evaluation, preferred_element_type=jnp.float32
    ).astype(jnp.bfloat16)


def after(value, earlier):
    return value if earlier is None else lax.optimization_barrier((value, earlier))[0]


def all_hops():
    low_bits = lax.axis_size("sub").bit_length() - 1
    high_bits = lax.axis_size("bfly").bit_length() - 1
    return [("sub", bit) for bit in range(low_bits)] + [("bfly", bit) for bit in range(high_bits)]


def full_width(traces, sampling, skeleton, compress, evaluation):
    rank = skeleton.shape[-1]
    columns = picked_columns(compress, skeleton)
    full = jnp.concatenate([real_form(columns[..., :rank]), real_form(columns[..., rank:])], 2)
    coeffs = sampled_apart(sampling, traces)
    for level, hop in enumerate(all_hops()):
        partner = from_partner(coeffs, hop)
        coeffs = times(full[level], jnp.concatenate([coeffs, partner], 0))
    return evaluated(coeffs, evaluation)


def local(traces, sampling, skeleton, compress, evaluation):
    hops = all_hops()
    levels = len(hops)
    if (lax.axis_size("sub"), lax.axis_size("bfly")) != (2, 4):
        return full_width(traces, sampling[0], skeleton[0], compress[0], evaluation[0])
    wide = lax.axis_size("sub").bit_length() - 1
    rank = skeleton.shape[-1]
    rooms = [rank * share // 16 for share in ROOM_SIXTEENTHS]
    unit = traces.shape[0] // sum(SHARES)
    pieces = len(SHARES)
    starts = [unit * sum(SHARES[:i]) for i in range(pieces + 1)]
    coeffs = list(early(sampling, traces, starts[: EARLY_PIECES + 1]))
    full, small, extra = tables(after(skeleton, coeffs[0]), compress, wide, rooms)
    sampling, evaluation = sampling[0], evaluation[0]
    most_here = lax.broadcasted_iota(jnp.int32, extra.shape[1:], 1) >= rank

    def compact(level, piece):
        return level >= wide and piece >= FULL_PIECES[level - wide]

    inputs, partners, theirs, done = {}, {}, {}, [None] * pieces
    previous, finished, known = None, None, None
    for level, piece in ORDER:
        if (level, piece) == LOOK:
            known = after(after(partners[0], previous), partners[1])[:, starts[1] :]
            theirs[levels - 1] = known[: rooms[levels - 1 - wide], :rank]
            continue
        count = starts[piece + 1] - starts[piece]
        if level == 0:
            if piece == len(coeffs):
                waiting = after(sampling, previous)
                for late in (piece, piece + 1) if piece == pieces - 2 else (piece,):
                    coeffs.append(sampled(waiting, traces[starts[late] : starts[late + 1]]))
            own = coeffs[piece]
        else:
            arrived = after(partners[piece], previous)
            if level == levels:
                arrived = after(arrived, finished)
            elif piece == 0 and level - 1 >= wide:
                known = arrived[:, count:]
                theirs[level - 1] = known[: rooms[level - 1 - wide], :rank]
            value = jnp.concatenate([inputs[piece], arrived[:, :count]], 0)
            matrix = full[level - 1]
            if compact(level - 1, piece):
                value = jnp.pad(value, ((0, full.shape[2] - value.shape[0]), (0, 0)))
                matrix = small[level - 1 - wide]
            if level < levels and compact(level, piece):
                outgoing = times(compact_rows(matrix, theirs[level]), value)
                own = times(after(matrix, outgoing), value)
            else:
                own = outgoing = times(matrix, value)
        if level == levels:
            done[piece] = finished = previous = evaluated(own, evaluation)
            if piece == COUNT_READ:
                most = jnp.maximum(most, after(counted, finished))
            continue
        if level == 0:
            outgoing = after(own, previous) if piece == pieces - 1 else own
        if piece == 0 and level >= wide:
            block = extra[level - wide]
            if known is not None:
                block = jnp.where(most_here, jnp.maximum(block, known), block)
            outgoing = jnp.concatenate([outgoing, block], 1)
        inputs[piece] = own
        partners[piece] = from_partner(outgoing, hops[level])
        previous = outgoing
        if (level, piece) == (levels - 1, COUNT_PIECE):
            most = after(jnp.maximum(extra[levels - 1 - wide], known)[:8, rank:], outgoing)
            for hop in hops[: wide - 1]:
                most = jnp.maximum(most, from_partner(most, hop))
            counted = from_partner(most, hops[wide - 1])
    quick = jnp.concatenate(done, 0)
    return lax.cond(
        most[0, 0] > 0,
        lambda: full_width(traces, sampling, skeleton[0], compress[0], evaluation),
        lambda: quick,
    )


def solution(mesh):
    placed = (
        P(("shots", "tr"), ("bfly", "sub")),
        P(("bfly", "sub"), None, None),
        P(("bfly", "sub"), None, None),
        P(("bfly", "sub"), None, None, None),
        P(("bfly", "sub"), None, None),
    )
    return jax.shard_map(
        local,
        mesh=mesh,
        in_specs=placed,
        out_specs=P(("shots", "tr"), ("bfly", "sub")),
        check_vma=False,
    )
```

```python
import jax
import jax.numpy as jnp
from jax import lax
from jax.experimental import pallas as pl
from jax.experimental.pallas import tpu as pltpu
from jax.sharding import PartitionSpec as P

SHARES = (2, 5, 9, 9, 7)
FULL_PIECES = (2, 1)
EARLY_PIECES = 2
COUNT_PIECE = 2
COUNT_READ = 2
LOOK = (3, -1)
MAKE = (0, -1)
ORDER = (
    (0, 0), (0, 1), (0, 2), (1, 0), (1, 1), MAKE, (2, 0), (0, 3), (1, 2), LOOK, (2, 1), (1, 3), (2, 2),
    (0, 4), (3, 0), (1, 4), (2, 3), (3, 1), (2, 4), (3, 2), (3, 3), (3, 4),
)
KERNEL_VMEM = 16 * 1024 * 1024
ROOM_SIXTEENTHS = (11, 10)


def route(axis, apart):
    count = lax.axis_size(axis)
    pairs = []
    for low in range(count):
        high = low | 1 << apart
        if high != low and high < count:
            pairs += [(low, high), (high, low)]
    return pairs


def from_partner(block, hop):
    return lax.ppermute(block, hop[0], route(*hop))


def across(left, right):
    return lax.dot_general(left, right, (((1,), (1,)), ((), ())), preferred_element_type=jnp.float32)


def one_hot(condition):
    return jnp.where(condition, 1.0, 0.0).astype(jnp.bfloat16)


def sampled_block(sampling, rows):
    turned = sampling.astype(jnp.float32).T.astype(jnp.bfloat16)
    return across(turned, rows).astype(jnp.bfloat16)


def early_kernel(starts, sampling_hbm, traces_hbm, *refs):
    pieces = len(starts) - 1
    outs, (sampling_ref, rows_ref, arrived) = refs[:pieces], refs[pieces:]
    loads = [pltpu.make_async_copy(sampling_hbm, sampling_ref, arrived.at[pieces])]
    for i in range(pieces):
        span = pl.ds(starts[i], starts[i + 1] - starts[i])
        loads.append(pltpu.make_async_copy(traces_hbm.at[span], rows_ref.at[span], arrived.at[i]))
    for load in loads:
        load.start()
    loads[0].wait()
    for i in range(pieces):
        loads[i + 1].wait()
        span = pl.ds(starts[i], starts[i + 1] - starts[i])
        outs[i][...] = sampled_block(sampling_ref[0], rows_ref[span])


def early(sampling, traces, starts):
    pieces = len(starts) - 1
    width = sampling.shape[-1]
    total = starts[-1]
    return pl.pallas_call(
        lambda *refs: early_kernel(starts, *refs),
        out_shape=[
            jax.ShapeDtypeStruct((width, starts[i + 1] - starts[i]), jnp.bfloat16) for i in range(pieces)
        ],
        in_specs=[pl.BlockSpec(memory_space=pltpu.HBM)] * 2,
        out_specs=[pl.BlockSpec(memory_space=pltpu.VMEM)] * pieces,
        scratch_shapes=[
            pltpu.VMEM(sampling.shape, jnp.bfloat16),
            pltpu.VMEM((total, traces.shape[1]), jnp.bfloat16),
            pltpu.SemaphoreType.DMA((pieces + 1,)),
        ],
        compiler_params=pltpu.CompilerParams(vmem_limit_bytes=KERNEL_VMEM),
        cost_estimate=pl.CostEstimate(
            flops=2 * total * width * width, bytes_accessed=4 * total * width, transcendentals=0
        ),
        name="early",
    )(sampling, traces)


def tables_kernel(
    wide, rooms, skeleton_hbm, compress_hbm, full_ref, small_ref, extra_ref,
    skeleton_ref, compress_ref, arrived,
):
    loads = [
        pltpu.make_async_copy(skeleton_hbm, skeleton_ref, arrived.at[0]),
        pltpu.make_async_copy(compress_hbm, compress_ref, arrived.at[1]),
    ]
    for load in loads:
        load.start()
    for load in loads:
        load.wait()
    levels, rank = skeleton_ref.shape[0], skeleton_ref.shape[-1]
    width = 2 * rank
    f32, i32 = jnp.float32, jnp.int32
    k = lax.broadcasted_iota(i32, (width, width), 1)
    twice = one_hot(lax.broadcasted_iota(i32, (width, rank), 0) % rank == lax.broadcasted_iota(i32, (width, rank), 1))
    earlier = one_hot(
        (lax.broadcasted_iota(i32, (width, width), 1) < lax.broadcasted_iota(i32, (width, width), 0) % rank)
    )
    column = lax.broadcasted_iota(i32, (2 * width, width), 0)
    is_real_entry = lax.broadcasted_iota(i32, (2 * width, width), 1) < rank
    partner_column = column >= width
    imag_column = column % width >= rank
    coefficient = column % rank + jnp.where(partner_column, rank, 0)
    slot_column = column - width
    row = lax.broadcasted_iota(i32, (width, width), 0)
    most = jnp.full((1, 1), -float(rank), f32)
    for level in range(levels):
        entry = jnp.broadcast_to(skeleton_ref[level].astype(f32), (8, rank)).astype(jnp.bfloat16)
        entry = across(entry, twice)[:1]
        picked = jnp.where(entry >= rank, 1.0, 0.0)
        slot = across(jnp.broadcast_to(picked, (8, width)).astype(jnp.bfloat16), earlier)[:1].astype(i32)
        entry = entry.astype(i32)
        from_partner_entry = entry >= rank
        matrix = compress_ref[0, level]

        def halves(match, imag):
            same = is_real_entry != imag
            real = jnp.where(match & same, jnp.where(imag, -1.0, 1.0), 0.0).astype(jnp.bfloat16)
            turned = one_hot(match & jnp.logical_not(same))
            return across(matrix, real).astype(jnp.bfloat16), across(matrix, turned).astype(jnp.bfloat16)

        match = entry == coefficient
        full_ref[level, :rank], full_ref[level, rank:] = halves(match, imag_column)
        if level < wide:
            continue
        high = level - wide
        room = rooms[high]
        slot_imag = slot_column >= room
        slot_of_column = jnp.where(slot_imag, slot_column - room, slot_column)
        compacted = (slot == slot_of_column) & from_partner_entry
        match = (match & jnp.logical_not(partner_column)) | (compacted & partner_column)
        imag = (imag_column & jnp.logical_not(partner_column)) | (slot_imag & partner_column)
        small_ref[high, :rank], small_ref[high, rank:] = halves(match, imag)
        once = (k < rank) & from_partner_entry
        places = across(one_hot(once & (slot == row)), one_hot(once & (entry - rank == row)))
        extra_ref[high] = places.astype(jnp.bfloat16)
        most = jnp.maximum(most, jnp.sum(picked, axis=1, keepdims=True) * 0.5 - room)
    for high in range(levels - wide):
        extra_ref[high] = jnp.where(k < rank, extra_ref[high].astype(f32), most).astype(jnp.bfloat16)


def tables(skeleton, compress, wide, rooms):
    levels, rank = skeleton.shape[1:]
    shape = (levels, 2 * rank, 4 * rank)
    return pl.pallas_call(
        lambda *refs: tables_kernel(wide, rooms, *refs),
        out_shape=[
            jax.ShapeDtypeStruct(shape, jnp.bfloat16),
            jax.ShapeDtypeStruct((levels - wide,) + shape[1:], jnp.bfloat16),
            jax.ShapeDtypeStruct((levels - wide, 2 * rank, 2 * rank), jnp.bfloat16),
        ],
        in_specs=[pl.BlockSpec(memory_space=pltpu.HBM)] * 2,
        out_specs=[pl.BlockSpec(memory_space=pltpu.VMEM)] * 3,
        scratch_shapes=[
            pltpu.VMEM((levels, 1, rank), jnp.int32),
            pltpu.VMEM(compress.shape, jnp.bfloat16),
            pltpu.SemaphoreType.DMA((2,)),
        ],
        compiler_params=pltpu.CompilerParams(vmem_limit_bytes=KERNEL_VMEM),
        cost_estimate=pl.CostEstimate(flops=50_000_000, bytes_accessed=600_000, transcendentals=0),
        name="tables",
    )(skeleton.transpose(1, 0, 2), compress)


def sampled_apart(sampling, traces):
    count, width = traces.shape
    block = count // 8

    def kernel(sampling_ref, rows_ref, coeffs_ref):
        coeffs_ref[...] = sampled_block(sampling_ref[...], rows_ref[...])

    return pl.pallas_call(
        kernel,
        grid=(count // block,),
        out_shape=jax.ShapeDtypeStruct((sampling.shape[1], count), jnp.bfloat16),
        in_specs=[
            pl.BlockSpec(sampling.shape, lambda i: (0, 0)),
            pl.BlockSpec((block, width), lambda i: (i, 0)),
        ],
        out_specs=pl.BlockSpec((sampling.shape[1], block), lambda i: (0, i)),
        compiler_params=pltpu.CompilerParams(vmem_limit_bytes=63 * 1024 * 1024),
        name="sampled_apart",
    )(sampling, traces)


def picked_columns(compress, skeleton):
    rank = skeleton.shape[-1]
    places = lax.broadcasted_iota(jnp.int32, (1, 1, 2 * rank), 2)
    chooser = (skeleton[:, :, None] == places).astype(jnp.bfloat16)
    stacked = jnp.concatenate([compress[:, :, :rank], compress[:, :, rank:]], 1)
    return jnp.einsum(
        "ljk,lki->lji", stacked, chooser, preferred_element_type=jnp.float32
    ).astype(jnp.bfloat16)


def real_form(both):
    rank = both.shape[1] // 2
    turned = jnp.concatenate([-both[:, rank:], both[:, :rank]], 1)
    return jnp.concatenate([both, turned], 2)


def compact_rows(matrix, slot):
    rank = slot.shape[1]
    parts = [
        jnp.dot(slot, half, preferred_element_type=jnp.float32)
        for half in (matrix[:rank], matrix[rank:])
    ]
    return jnp.concatenate(parts, 0).astype(jnp.bfloat16)


def times(matrix, value):
    return jnp.dot(matrix, value, preferred_element_type=jnp.float32).astype(jnp.bfloat16)


def sampled(sampling, traces):
    return jnp.einsum(
        "pc,tp->ct", sampling, traces, preferred_element_type=jnp.float32
    ).astype(jnp.bfloat16)


def evaluated(coeffs, evaluation):
    return jnp.einsum(
        "ct,cp->tp", coeffs, evaluation, preferred_element_type=jnp.float32
    ).astype(jnp.bfloat16)


def after(value, earlier):
    return value if earlier is None else lax.optimization_barrier((value, earlier))[0]


def all_hops():
    low_bits = lax.axis_size("sub").bit_length() - 1
    high_bits = lax.axis_size("bfly").bit_length() - 1
    return [("sub", bit) for bit in range(low_bits)] + [("bfly", bit) for bit in range(high_bits)]


def full_width(traces, sampling, skeleton, compress, evaluation):
    rank = skeleton.shape[-1]
    columns = picked_columns(compress, skeleton)
    full = jnp.concatenate([real_form(columns[..., :rank]), real_form(columns[..., rank:])], 2)
    coeffs = sampled_apart(sampling, traces)
    for level, hop in enumerate(all_hops()):
        partner = from_partner(coeffs, hop)
        coeffs = times(full[level], jnp.concatenate([coeffs, partner], 0))
    return evaluated(coeffs, evaluation)


def local(traces, sampling, skeleton, compress, evaluation):
    hops = all_hops()
    levels = len(hops)
    if (lax.axis_size("sub"), lax.axis_size("bfly")) != (2, 4):
        return full_width(traces, sampling[0], skeleton[0], compress[0], evaluation[0])
    wide = lax.axis_size("sub").bit_length() - 1
    rank = skeleton.shape[-1]
    rooms = [rank * share // 16 for share in ROOM_SIXTEENTHS]
    unit = traces.shape[0] // sum(SHARES)
    pieces = len(SHARES)
    starts = [unit * sum(SHARES[:i]) for i in range(pieces + 1)]
    coeffs = list(early(sampling, traces, starts[: EARLY_PIECES + 1]))
    full, small, extra = tables(after(skeleton, coeffs[0]), compress, wide, rooms)
    sampling, evaluation = sampling[0], evaluation[0]
    most_here = lax.broadcasted_iota(jnp.int32, extra.shape[1:], 1) >= rank

    def compact(level, piece):
        return level >= wide and piece >= FULL_PIECES[level - wide]

    inputs, partners, theirs, done = {}, {}, {}, [None] * pieces
    previous, finished, known = None, None, None
    for level, piece in ORDER:
        if (level, piece) == MAKE:
            waiting = after(sampling, previous)
            coeffs.append(sampled(waiting, traces[starts[pieces - 2] : starts[pieces - 1]]))
            previous = coeffs[-1]
            continue
        if (level, piece) == LOOK:
            known = after(after(partners[0], previous), partners[1])[:, starts[1] :]
            theirs[levels - 1] = known[: rooms[levels - 1 - wide], :rank]
            continue
        count = starts[piece + 1] - starts[piece]
        if level == 0:
            if piece == len(coeffs):
                waiting = after(sampling, previous)
                coeffs.append(sampled(waiting, traces[starts[piece] : starts[piece + 1]]))
            own = coeffs[piece]
            if piece == pieces - 2:
                coeffs.append(sampled(waiting, traces[starts[piece + 1] : starts[piece + 2]]))
        else:
            arrived = after(partners[piece], previous)
            if level == levels:
                arrived = after(arrived, finished)
            elif piece == 0 and level - 1 >= wide:
                known = arrived[:, count:]
                theirs[level - 1] = known[: rooms[level - 1 - wide], :rank]
            value = jnp.concatenate([inputs[piece], arrived[:, :count]], 0)
            matrix = full[level - 1]
            if compact(level - 1, piece):
                value = jnp.pad(value, ((0, full.shape[2] - value.shape[0]), (0, 0)))
                matrix = small[level - 1 - wide]
            if level < levels and compact(level, piece):
                outgoing = times(compact_rows(matrix, theirs[level]), value)
                own = times(after(matrix, outgoing), value)
            else:
                own = outgoing = times(matrix, value)
        if level == levels:
            done[piece] = finished = previous = evaluated(own, evaluation)
            if piece == COUNT_READ:
                most = jnp.maximum(most, after(counted, finished))
            continue
        if level == 0:
            outgoing = after(own, previous) if piece >= pieces - 2 else own
        if piece == 0 and level >= wide:
            block = extra[level - wide]
            if known is not None:
                block = jnp.where(most_here, jnp.maximum(block, known), block)
            outgoing = jnp.concatenate([outgoing, block], 1)
        inputs[piece] = own
        partners[piece] = from_partner(outgoing, hops[level])
        previous = outgoing
        if (level, piece) == (levels - 1, COUNT_PIECE):
            most = after(jnp.maximum(extra[levels - 1 - wide], known)[:8, rank:], outgoing)
            for hop in hops[: wide - 1]:
                most = jnp.maximum(most, from_partner(most, hop))
            counted = from_partner(most, hops[wide - 1])
    quick = jnp.concatenate(done, 0)
    return lax.cond(
        most[0, 0] > 0,
        lambda: full_width(traces, sampling, skeleton[0], compress[0], evaluation),
        lambda: quick,
    )


def solution(mesh):
    placed = (
        P(("shots", "tr"), ("bfly", "sub")),
        P(("bfly", "sub"), None, None),
        P(("bfly", "sub"), None, None),
        P(("bfly", "sub"), None, None, None),
        P(("bfly", "sub"), None, None),
    )
    return jax.shard_map(
        local,
        mesh=mesh,
        in_specs=placed,
        out_specs=P(("shots", "tr"), ("bfly", "sub")),
        check_vma=False,
    )
```

```python
import jax
import jax.numpy as jnp
from jax import lax
from jax.experimental import pallas as pl
from jax.experimental.pallas import tpu as pltpu
from jax.sharding import PartitionSpec as P

SHARES = (1, 5, 9, 10, 7)
FULL_PIECES = (2, 1)
EARLY_PIECES = 2
COUNT_PIECE = 2
COUNT_READ = 2
LOOK = (3, -1)
MAKE = (0, -1)
ORDER = (
    (0, 0), (0, 1), (1, 0), (0, 2), (1, 1), MAKE, (2, 0), (0, 3), (1, 2), LOOK, (2, 1), (1, 3), (2, 2),
    (0, 4), (3, 0), (1, 4), (2, 3), (3, 1), (2, 4), (3, 2), (3, 3), (3, 4),
)
KERNEL_VMEM = 16 * 1024 * 1024
ROOM_SIXTEENTHS = (11, 10)


def route(axis, apart):
    count = lax.axis_size(axis)
    pairs = []
    for low in range(count):
        high = low | 1 << apart
        if high != low and high < count:
            pairs += [(low, high), (high, low)]
    return pairs


def from_partner(block, hop):
    return lax.ppermute(block, hop[0], route(*hop))


def across(left, right):
    return lax.dot_general(left, right, (((1,), (1,)), ((), ())), preferred_element_type=jnp.float32)


def one_hot(condition):
    return jnp.where(condition, 1.0, 0.0).astype(jnp.bfloat16)


def sampled_block(sampling, rows):
    turned = sampling.astype(jnp.float32).T.astype(jnp.bfloat16)
    return across(turned, rows).astype(jnp.bfloat16)


def early_kernel(starts, sampling_hbm, traces_hbm, *refs):
    pieces = len(starts) - 1
    outs, (sampling_ref, rows_ref, arrived) = refs[:pieces], refs[pieces:]
    loads = [pltpu.make_async_copy(sampling_hbm, sampling_ref, arrived.at[pieces])]
    for i in range(pieces):
        span = pl.ds(starts[i], starts[i + 1] - starts[i])
        loads.append(pltpu.make_async_copy(traces_hbm.at[span], rows_ref.at[span], arrived.at[i]))
    for load in loads:
        load.start()
    loads[0].wait()
    for i in range(pieces):
        loads[i + 1].wait()
        span = pl.ds(starts[i], starts[i + 1] - starts[i])
        outs[i][...] = sampled_block(sampling_ref[0], rows_ref[span])


def early(sampling, traces, starts):
    pieces = len(starts) - 1
    width = sampling.shape[-1]
    total = starts[-1]
    return pl.pallas_call(
        lambda *refs: early_kernel(starts, *refs),
        out_shape=[
            jax.ShapeDtypeStruct((width, starts[i + 1] - starts[i]), jnp.bfloat16) for i in range(pieces)
        ],
        in_specs=[pl.BlockSpec(memory_space=pltpu.HBM)] * 2,
        out_specs=[pl.BlockSpec(memory_space=pltpu.VMEM)] * pieces,
        scratch_shapes=[
            pltpu.VMEM(sampling.shape, jnp.bfloat16),
            pltpu.VMEM((total, traces.shape[1]), jnp.bfloat16),
            pltpu.SemaphoreType.DMA((pieces + 1,)),
        ],
        compiler_params=pltpu.CompilerParams(vmem_limit_bytes=KERNEL_VMEM),
        cost_estimate=pl.CostEstimate(
            flops=2 * total * width * width, bytes_accessed=4 * total * width, transcendentals=0
        ),
        name="early",
    )(sampling, traces)


def tables_kernel(
    wide, rooms, skeleton_hbm, compress_hbm, full_ref, small_ref, extra_ref,
    skeleton_ref, compress_ref, arrived,
):
    loads = [
        pltpu.make_async_copy(skeleton_hbm, skeleton_ref, arrived.at[0]),
        pltpu.make_async_copy(compress_hbm, compress_ref, arrived.at[1]),
    ]
    for load in loads:
        load.start()
    for load in loads:
        load.wait()
    levels, rank = skeleton_ref.shape[0], skeleton_ref.shape[-1]
    width = 2 * rank
    f32, i32 = jnp.float32, jnp.int32
    k = lax.broadcasted_iota(i32, (width, width), 1)
    twice = one_hot(lax.broadcasted_iota(i32, (width, rank), 0) % rank == lax.broadcasted_iota(i32, (width, rank), 1))
    earlier = one_hot(
        (lax.broadcasted_iota(i32, (width, width), 1) < lax.broadcasted_iota(i32, (width, width), 0) % rank)
    )
    column = lax.broadcasted_iota(i32, (2 * width, width), 0)
    is_real_entry = lax.broadcasted_iota(i32, (2 * width, width), 1) < rank
    partner_column = column >= width
    imag_column = column % width >= rank
    coefficient = column % rank + jnp.where(partner_column, rank, 0)
    slot_column = column - width
    row = lax.broadcasted_iota(i32, (width, width), 0)
    most = jnp.full((1, 1), -float(rank), f32)
    for level in range(levels):
        entry = jnp.broadcast_to(skeleton_ref[level].astype(f32), (8, rank)).astype(jnp.bfloat16)
        entry = across(entry, twice)[:1]
        picked = jnp.where(entry >= rank, 1.0, 0.0)
        slot = across(jnp.broadcast_to(picked, (8, width)).astype(jnp.bfloat16), earlier)[:1].astype(i32)
        entry = entry.astype(i32)
        from_partner_entry = entry >= rank
        matrix = compress_ref[0, level]

        def halves(match, imag):
            same = is_real_entry != imag
            real = jnp.where(match & same, jnp.where(imag, -1.0, 1.0), 0.0).astype(jnp.bfloat16)
            turned = one_hot(match & jnp.logical_not(same))
            return across(matrix, real).astype(jnp.bfloat16), across(matrix, turned).astype(jnp.bfloat16)

        match = entry == coefficient
        full_ref[level, :rank], full_ref[level, rank:] = halves(match, imag_column)
        if level < wide:
            continue
        high = level - wide
        room = rooms[high]
        slot_imag = slot_column >= room
        slot_of_column = jnp.where(slot_imag, slot_column - room, slot_column)
        compacted = (slot == slot_of_column) & from_partner_entry
        match = (match & jnp.logical_not(partner_column)) | (compacted & partner_column)
        imag = (imag_column & jnp.logical_not(partner_column)) | (slot_imag & partner_column)
        small_ref[high, :rank], small_ref[high, rank:] = halves(match, imag)
        once = (k < rank) & from_partner_entry
        places = across(one_hot(once & (slot == row)), one_hot(once & (entry - rank == row)))
        extra_ref[high] = places.astype(jnp.bfloat16)
        most = jnp.maximum(most, jnp.sum(picked, axis=1, keepdims=True) * 0.5 - room)
    for high in range(levels - wide):
        extra_ref[high] = jnp.where(k < rank, extra_ref[high].astype(f32), most).astype(jnp.bfloat16)


def tables(skeleton, compress, wide, rooms):
    levels, rank = skeleton.shape[1:]
    shape = (levels, 2 * rank, 4 * rank)
    return pl.pallas_call(
        lambda *refs: tables_kernel(wide, rooms, *refs),
        out_shape=[
            jax.ShapeDtypeStruct(shape, jnp.bfloat16),
            jax.ShapeDtypeStruct((levels - wide,) + shape[1:], jnp.bfloat16),
            jax.ShapeDtypeStruct((levels - wide, 2 * rank, 2 * rank), jnp.bfloat16),
        ],
        in_specs=[pl.BlockSpec(memory_space=pltpu.HBM)] * 2,
        out_specs=[pl.BlockSpec(memory_space=pltpu.VMEM)] * 3,
        scratch_shapes=[
            pltpu.VMEM((levels, 1, rank), jnp.int32),
            pltpu.VMEM(compress.shape, jnp.bfloat16),
            pltpu.SemaphoreType.DMA((2,)),
        ],
        compiler_params=pltpu.CompilerParams(vmem_limit_bytes=KERNEL_VMEM),
        cost_estimate=pl.CostEstimate(flops=50_000_000, bytes_accessed=600_000, transcendentals=0),
        name="tables",
    )(skeleton.transpose(1, 0, 2), compress)


def sampled_apart(sampling, traces):
    count, width = traces.shape
    block = count // 8

    def kernel(sampling_ref, rows_ref, coeffs_ref):
        coeffs_ref[...] = sampled_block(sampling_ref[...], rows_ref[...])

    return pl.pallas_call(
        kernel,
        grid=(count // block,),
        out_shape=jax.ShapeDtypeStruct((sampling.shape[1], count), jnp.bfloat16),
        in_specs=[
            pl.BlockSpec(sampling.shape, lambda i: (0, 0)),
            pl.BlockSpec((block, width), lambda i: (i, 0)),
        ],
        out_specs=pl.BlockSpec((sampling.shape[1], block), lambda i: (0, i)),
        compiler_params=pltpu.CompilerParams(vmem_limit_bytes=63 * 1024 * 1024),
        name="sampled_apart",
    )(sampling, traces)


def picked_columns(compress, skeleton):
    rank = skeleton.shape[-1]
    places = lax.broadcasted_iota(jnp.int32, (1, 1, 2 * rank), 2)
    chooser = (skeleton[:, :, None] == places).astype(jnp.bfloat16)
    stacked = jnp.concatenate([compress[:, :, :rank], compress[:, :, rank:]], 1)
    return jnp.einsum(
        "ljk,lki->lji", stacked, chooser, preferred_element_type=jnp.float32
    ).astype(jnp.bfloat16)


def real_form(both):
    rank = both.shape[1] // 2
    turned = jnp.concatenate([-both[:, rank:], both[:, :rank]], 1)
    return jnp.concatenate([both, turned], 2)


def compact_rows(matrix, slot):
    rank = slot.shape[1]
    parts = [
        jnp.dot(slot, half, preferred_element_type=jnp.float32)
        for half in (matrix[:rank], matrix[rank:])
    ]
    return jnp.concatenate(parts, 0).astype(jnp.bfloat16)


def times(matrix, value):
    return jnp.dot(matrix, value, preferred_element_type=jnp.float32).astype(jnp.bfloat16)


def sampled(sampling, traces):
    return jnp.einsum(
        "pc,tp->ct", sampling, traces, preferred_element_type=jnp.float32
    ).astype(jnp.bfloat16)


def evaluated(coeffs, evaluation):
    return jnp.einsum(
        "ct,cp->tp", coeffs, evaluation, preferred_element_type=jnp.float32
    ).astype(jnp.bfloat16)


def after(value, earlier):
    return value if earlier is None else lax.optimization_barrier((value, earlier))[0]


def all_hops():
    low_bits = lax.axis_size("sub").bit_length() - 1
    high_bits = lax.axis_size("bfly").bit_length() - 1
    return [("sub", bit) for bit in range(low_bits)] + [("bfly", bit) for bit in range(high_bits)]


def full_width(traces, sampling, skeleton, compress, evaluation):
    rank = skeleton.shape[-1]
    columns = picked_columns(compress, skeleton)
    full = jnp.concatenate([real_form(columns[..., :rank]), real_form(columns[..., rank:])], 2)
    coeffs = sampled_apart(sampling, traces)
    for level, hop in enumerate(all_hops()):
        partner = from_partner(coeffs, hop)
        coeffs = times(full[level], jnp.concatenate([coeffs, partner], 0))
    return evaluated(coeffs, evaluation)


def local(traces, sampling, skeleton, compress, evaluation):
    hops = all_hops()
    levels = len(hops)
    if (lax.axis_size("sub"), lax.axis_size("bfly")) != (2, 4):
        return full_width(traces, sampling[0], skeleton[0], compress[0], evaluation[0])
    wide = lax.axis_size("sub").bit_length() - 1
    rank = skeleton.shape[-1]
    rooms = [rank * share // 16 for share in ROOM_SIXTEENTHS]
    unit = traces.shape[0] // sum(SHARES)
    pieces = len(SHARES)
    starts = [unit * sum(SHARES[:i]) for i in range(pieces + 1)]
    coeffs = list(early(sampling, traces, starts[: EARLY_PIECES + 1]))
    full, small, extra = tables(after(skeleton, coeffs[0]), compress, wide, rooms)
    sampling, evaluation = sampling[0], evaluation[0]
    most_here = lax.broadcasted_iota(jnp.int32, extra.shape[1:], 1) >= rank

    def compact(level, piece):
        return level >= wide and piece >= FULL_PIECES[level - wide]

    inputs, partners, theirs, done = {}, {}, {}, [None] * pieces
    previous, finished, known = None, None, None
    for level, piece in ORDER:
        if (level, piece) == MAKE:
            waiting = after(sampling, previous)
            coeffs.append(sampled(waiting, traces[starts[pieces - 2] : starts[pieces - 1]]))
            previous = coeffs[-1]
            continue
        if (level, piece) == LOOK:
            known = after(partners[0], previous)[:, starts[1] :]
            theirs[levels - 1] = known[: rooms[levels - 1 - wide], :rank]
            continue
        count = starts[piece + 1] - starts[piece]
        if level == 0:
            if piece == len(coeffs):
                waiting = after(sampling, previous)
                coeffs.append(sampled(waiting, traces[starts[piece] : starts[piece + 1]]))
            own = coeffs[piece]
            if piece == pieces - 2:
                coeffs.append(sampled(waiting, traces[starts[piece + 1] : starts[piece + 2]]))
        else:
            arrived = after(partners[piece], previous)
            if level == levels:
                arrived = after(arrived, finished)
            elif piece == 0 and level - 1 >= wide:
                known = arrived[:, count:]
                theirs[level - 1] = known[: rooms[level - 1 - wide], :rank]
            value = jnp.concatenate([inputs[piece], arrived[:, :count]], 0)
            matrix = full[level - 1]
            if compact(level - 1, piece):
                value = jnp.pad(value, ((0, full.shape[2] - value.shape[0]), (0, 0)))
                matrix = small[level - 1 - wide]
            if level < levels and compact(level, piece):
                outgoing = times(compact_rows(matrix, theirs[level]), value)
                own = times(after(matrix, outgoing), value)
            else:
                own = outgoing = times(matrix, value)
        if level == levels:
            done[piece] = finished = previous = evaluated(own, evaluation)
            if piece == COUNT_READ:
                most = jnp.maximum(most, after(counted, finished))
            continue
        if level == 0:
            outgoing = after(own, previous) if piece >= pieces - 2 else own
        if piece == 0 and level >= wide:
            block = extra[level - wide]
            if known is not None:
                block = jnp.where(most_here, jnp.maximum(block, known), block)
            outgoing = jnp.concatenate([outgoing, block], 1)
        inputs[piece] = own
        partners[piece] = from_partner(outgoing, hops[level])
        previous = outgoing
        if (level, piece) == (levels - 1, COUNT_PIECE):
            most = after(jnp.maximum(extra[levels - 1 - wide], known)[:8, rank:], outgoing)
            for hop in hops[: wide - 1]:
                most = jnp.maximum(most, from_partner(most, hop))
            counted = from_partner(most, hops[wide - 1])
    quick = jnp.concatenate(done, 0)
    return lax.cond(
        most[0, 0] > 0,
        lambda: full_width(traces, sampling, skeleton[0], compress[0], evaluation),
        lambda: quick,
    )


def solution(mesh):
    placed = (
        P(("shots", "tr"), ("bfly", "sub")),
        P(("bfly", "sub"), None, None),
        P(("bfly", "sub"), None, None),
        P(("bfly", "sub"), None, None, None),
        P(("bfly", "sub"), None, None),
    )
    return jax.shard_map(
        local,
        mesh=mesh,
        in_specs=placed,
        out_specs=P(("shots", "tr"), ("bfly", "sub")),
        check_vma=False,
    )
```

```python
import jax
import jax.numpy as jnp
from jax import lax
from jax.experimental import pallas as pl
from jax.experimental.pallas import tpu as pltpu
from jax.sharding import PartitionSpec as P

SHARES = (2, 5, 7, 10, 8)
FULL_PIECES = (2, 1)
EARLY_PIECES = 2
COUNT_PIECE = 2
COUNT_READ = 2
LOOK = (3, -1)
MAKE = (0, -1)
ORDER = (
    (0, 0), (0, 1), (0, 2), (1, 0), (1, 1), MAKE, (2, 0), (0, 3), (1, 2), LOOK, (2, 1), (1, 3), (2, 2),
    (0, 4), (3, 0), (1, 4), (2, 3), (3, 1), (2, 4), (3, 2), (3, 3), (3, 4),
)
KERNEL_VMEM = 16 * 1024 * 1024
ROOM_SIXTEENTHS = (11, 10)


def route(axis, apart):
    count = lax.axis_size(axis)
    pairs = []
    for low in range(count):
        high = low | 1 << apart
        if high != low and high < count:
            pairs += [(low, high), (high, low)]
    return pairs


def from_partner(block, hop):
    return lax.ppermute(block, hop[0], route(*hop))


def across(left, right):
    return lax.dot_general(left, right, (((1,), (1,)), ((), ())), preferred_element_type=jnp.float32)


def one_hot(condition):
    return jnp.where(condition, 1.0, 0.0).astype(jnp.bfloat16)


def sampled_block(sampling, rows):
    turned = sampling.astype(jnp.float32).T.astype(jnp.bfloat16)
    return across(turned, rows).astype(jnp.bfloat16)


def early_kernel(starts, sampling_hbm, traces_hbm, *refs):
    pieces = len(starts) - 1
    outs, (sampling_ref, rows_ref, arrived) = refs[:pieces], refs[pieces:]
    loads = [pltpu.make_async_copy(sampling_hbm, sampling_ref, arrived.at[pieces])]
    for i in range(pieces):
        span = pl.ds(starts[i], starts[i + 1] - starts[i])
        loads.append(pltpu.make_async_copy(traces_hbm.at[span], rows_ref.at[span], arrived.at[i]))
    for load in loads:
        load.start()
    loads[0].wait()
    for i in range(pieces):
        loads[i + 1].wait()
        span = pl.ds(starts[i], starts[i + 1] - starts[i])
        outs[i][...] = sampled_block(sampling_ref[0], rows_ref[span])


def early(sampling, traces, starts):
    pieces = len(starts) - 1
    width = sampling.shape[-1]
    total = starts[-1]
    return pl.pallas_call(
        lambda *refs: early_kernel(starts, *refs),
        out_shape=[
            jax.ShapeDtypeStruct((width, starts[i + 1] - starts[i]), jnp.bfloat16) for i in range(pieces)
        ],
        in_specs=[pl.BlockSpec(memory_space=pltpu.HBM)] * 2,
        out_specs=[pl.BlockSpec(memory_space=pltpu.VMEM)] * pieces,
        scratch_shapes=[
            pltpu.VMEM(sampling.shape, jnp.bfloat16),
            pltpu.VMEM((total, traces.shape[1]), jnp.bfloat16),
            pltpu.SemaphoreType.DMA((pieces + 1,)),
        ],
        compiler_params=pltpu.CompilerParams(vmem_limit_bytes=KERNEL_VMEM),
        cost_estimate=pl.CostEstimate(
            flops=2 * total * width * width, bytes_accessed=4 * total * width, transcendentals=0
        ),
        name="early",
    )(sampling, traces)


def tables_kernel(
    wide, rooms, skeleton_hbm, compress_hbm, full_ref, small_ref, extra_ref,
    skeleton_ref, compress_ref, arrived,
):
    loads = [
        pltpu.make_async_copy(skeleton_hbm, skeleton_ref, arrived.at[0]),
        pltpu.make_async_copy(compress_hbm, compress_ref, arrived.at[1]),
    ]
    for load in loads:
        load.start()
    for load in loads:
        load.wait()
    levels, rank = skeleton_ref.shape[0], skeleton_ref.shape[-1]
    width = 2 * rank
    f32, i32 = jnp.float32, jnp.int32
    k = lax.broadcasted_iota(i32, (width, width), 1)
    twice = one_hot(lax.broadcasted_iota(i32, (width, rank), 0) % rank == lax.broadcasted_iota(i32, (width, rank), 1))
    earlier = one_hot(
        (lax.broadcasted_iota(i32, (width, width), 1) < lax.broadcasted_iota(i32, (width, width), 0) % rank)
    )
    column = lax.broadcasted_iota(i32, (2 * width, width), 0)
    is_real_entry = lax.broadcasted_iota(i32, (2 * width, width), 1) < rank
    partner_column = column >= width
    imag_column = column % width >= rank
    coefficient = column % rank + jnp.where(partner_column, rank, 0)
    slot_column = column - width
    row = lax.broadcasted_iota(i32, (width, width), 0)
    most = jnp.full((1, 1), -float(rank), f32)
    for level in range(levels):
        entry = jnp.broadcast_to(skeleton_ref[level].astype(f32), (8, rank)).astype(jnp.bfloat16)
        entry = across(entry, twice)[:1]
        picked = jnp.where(entry >= rank, 1.0, 0.0)
        slot = across(jnp.broadcast_to(picked, (8, width)).astype(jnp.bfloat16), earlier)[:1].astype(i32)
        entry = entry.astype(i32)
        from_partner_entry = entry >= rank
        matrix = compress_ref[0, level]

        def halves(match, imag):
            same = is_real_entry != imag
            real = jnp.where(match & same, jnp.where(imag, -1.0, 1.0), 0.0).astype(jnp.bfloat16)
            turned = one_hot(match & jnp.logical_not(same))
            return across(matrix, real).astype(jnp.bfloat16), across(matrix, turned).astype(jnp.bfloat16)

        match = entry == coefficient
        full_ref[level, :rank], full_ref[level, rank:] = halves(match, imag_column)
        if level < wide:
            continue
        high = level - wide
        room = rooms[high]
        slot_imag = slot_column >= room
        slot_of_column = jnp.where(slot_imag, slot_column - room, slot_column)
        compacted = (slot == slot_of_column) & from_partner_entry
        match = (match & jnp.logical_not(partner_column)) | (compacted & partner_column)
        imag = (imag_column & jnp.logical_not(partner_column)) | (slot_imag & partner_column)
        small_ref[high, :rank], small_ref[high, rank:] = halves(match, imag)
        once = (k < rank) & from_partner_entry
        places = across(one_hot(once & (slot == row)), one_hot(once & (entry - rank == row)))
        extra_ref[high] = places.astype(jnp.bfloat16)
        most = jnp.maximum(most, jnp.sum(picked, axis=1, keepdims=True) * 0.5 - room)
    for high in range(levels - wide):
        extra_ref[high] = jnp.where(k < rank, extra_ref[high].astype(f32), most).astype(jnp.bfloat16)


def tables(skeleton, compress, wide, rooms):
    levels, rank = skeleton.shape[1:]
    shape = (levels, 2 * rank, 4 * rank)
    return pl.pallas_call(
        lambda *refs: tables_kernel(wide, rooms, *refs),
        out_shape=[
            jax.ShapeDtypeStruct(shape, jnp.bfloat16),
            jax.ShapeDtypeStruct((levels - wide,) + shape[1:], jnp.bfloat16),
            jax.ShapeDtypeStruct((levels - wide, 2 * rank, 2 * rank), jnp.bfloat16),
        ],
        in_specs=[pl.BlockSpec(memory_space=pltpu.HBM)] * 2,
        out_specs=[pl.BlockSpec(memory_space=pltpu.VMEM)] * 3,
        scratch_shapes=[
            pltpu.VMEM((levels, 1, rank), jnp.int32),
            pltpu.VMEM(compress.shape, jnp.bfloat16),
            pltpu.SemaphoreType.DMA((2,)),
        ],
        compiler_params=pltpu.CompilerParams(vmem_limit_bytes=KERNEL_VMEM),
        cost_estimate=pl.CostEstimate(flops=50_000_000, bytes_accessed=600_000, transcendentals=0),
        name="tables",
    )(skeleton.transpose(1, 0, 2), compress)


def sampled_apart(sampling, traces):
    count, width = traces.shape
    block = count // 8

    def kernel(sampling_ref, rows_ref, coeffs_ref):
        coeffs_ref[...] = sampled_block(sampling_ref[...], rows_ref[...])

    return pl.pallas_call(
        kernel,
        grid=(count // block,),
        out_shape=jax.ShapeDtypeStruct((sampling.shape[1], count), jnp.bfloat16),
        in_specs=[
            pl.BlockSpec(sampling.shape, lambda i: (0, 0)),
            pl.BlockSpec((block, width), lambda i: (i, 0)),
        ],
        out_specs=pl.BlockSpec((sampling.shape[1], block), lambda i: (0, i)),
        compiler_params=pltpu.CompilerParams(vmem_limit_bytes=63 * 1024 * 1024),
        name="sampled_apart",
    )(sampling, traces)


def picked_columns(compress, skeleton):
    rank = skeleton.shape[-1]
    places = lax.broadcasted_iota(jnp.int32, (1, 1, 2 * rank), 2)
    chooser = (skeleton[:, :, None] == places).astype(jnp.bfloat16)
    stacked = jnp.concatenate([compress[:, :, :rank], compress[:, :, rank:]], 1)
    return jnp.einsum(
        "ljk,lki->lji", stacked, chooser, preferred_element_type=jnp.float32
    ).astype(jnp.bfloat16)


def real_form(both):
    rank = both.shape[1] // 2
    turned = jnp.concatenate([-both[:, rank:], both[:, :rank]], 1)
    return jnp.concatenate([both, turned], 2)


def compact_rows(matrix, slot):
    rank = slot.shape[1]
    parts = [
        jnp.dot(slot, half, preferred_element_type=jnp.float32)
        for half in (matrix[:rank], matrix[rank:])
    ]
    return jnp.concatenate(parts, 0).astype(jnp.bfloat16)


def times(matrix, value):
    return jnp.dot(matrix, value, preferred_element_type=jnp.float32).astype(jnp.bfloat16)


def sampled(sampling, traces):
    return jnp.einsum(
        "pc,tp->ct", sampling, traces, preferred_element_type=jnp.float32
    ).astype(jnp.bfloat16)


def evaluated(coeffs, evaluation):
    return jnp.einsum(
        "ct,cp->tp", coeffs, evaluation, preferred_element_type=jnp.float32
    ).astype(jnp.bfloat16)


def after(value, earlier):
    return value if earlier is None else lax.optimization_barrier((value, earlier))[0]


def all_hops():
    low_bits = lax.axis_size("sub").bit_length() - 1
    high_bits = lax.axis_size("bfly").bit_length() - 1
    return [("sub", bit) for bit in range(low_bits)] + [("bfly", bit) for bit in range(high_bits)]


def full_width(traces, sampling, skeleton, compress, evaluation):
    rank = skeleton.shape[-1]
    columns = picked_columns(compress, skeleton)
    full = jnp.concatenate([real_form(columns[..., :rank]), real_form(columns[..., rank:])], 2)
    coeffs = sampled_apart(sampling, traces)
    for level, hop in enumerate(all_hops()):
        partner = from_partner(coeffs, hop)
        coeffs = times(full[level], jnp.concatenate([coeffs, partner], 0))
    return evaluated(coeffs, evaluation)


def local(traces, sampling, skeleton, compress, evaluation):
    hops = all_hops()
    levels = len(hops)
    if (lax.axis_size("sub"), lax.axis_size("bfly")) != (2, 4):
        return full_width(traces, sampling[0], skeleton[0], compress[0], evaluation[0])
    wide = lax.axis_size("sub").bit_length() - 1
    rank = skeleton.shape[-1]
    rooms = [rank * share // 16 for share in ROOM_SIXTEENTHS]
    unit = traces.shape[0] // sum(SHARES)
    pieces = len(SHARES)
    starts = [unit * sum(SHARES[:i]) for i in range(pieces + 1)]
    coeffs = list(early(sampling, traces, starts[: EARLY_PIECES + 1]))
    full, small, extra = tables(after(skeleton, coeffs[0]), compress, wide, rooms)
    sampling, evaluation = sampling[0], evaluation[0]
    most_here = lax.broadcasted_iota(jnp.int32, extra.shape[1:], 1) >= rank

    def compact(level, piece):
        return level >= wide and piece >= FULL_PIECES[level - wide]

    inputs, partners, theirs, done = {}, {}, {}, [None] * pieces
    previous, finished, known = None, None, None
    for level, piece in ORDER:
        if (level, piece) == MAKE:
            waiting = after(sampling, previous)
            coeffs.append(sampled(waiting, traces[starts[pieces - 2] : starts[pieces - 1]]))
            previous = coeffs[-1]
            continue
        if (level, piece) == LOOK:
            known = after(after(partners[0], previous), partners[1])[:, starts[1] :]
            theirs[levels - 1] = known[: rooms[levels - 1 - wide], :rank]
            continue
        count = starts[piece + 1] - starts[piece]
        if level == 0:
            if piece == len(coeffs):
                waiting = after(sampling, previous)
                coeffs.append(sampled(waiting, traces[starts[piece] : starts[piece + 1]]))
            own = coeffs[piece]
            if piece == pieces - 2:
                coeffs.append(sampled(waiting, traces[starts[piece + 1] : starts[piece + 2]]))
        else:
            arrived = after(partners[piece], previous)
            if level == levels:
                arrived = after(arrived, finished)
            elif piece == 0 and level - 1 >= wide:
                known = arrived[:, count:]
                theirs[level - 1] = known[: rooms[level - 1 - wide], :rank]
            value = jnp.concatenate([inputs[piece], arrived[:, :count]], 0)
            matrix = full[level - 1]
            if compact(level - 1, piece):
                value = jnp.pad(value, ((0, full.shape[2] - value.shape[0]), (0, 0)))
                matrix = small[level - 1 - wide]
            if level < levels and compact(level, piece):
                outgoing = times(compact_rows(matrix, theirs[level]), value)
                own = times(after(matrix, outgoing), value)
            else:
                own = outgoing = times(matrix, value)
        if level == levels:
            done[piece] = finished = previous = evaluated(own, evaluation)
            if piece == COUNT_READ:
                most = jnp.maximum(most, after(counted, finished))
            continue
        if level == 0:
            outgoing = after(own, previous) if piece >= pieces - 2 else own
        if piece == 0 and level >= wide:
            block = extra[level - wide]
            if known is not None:
                block = jnp.where(most_here, jnp.maximum(block, known), block)
            outgoing = jnp.concatenate([outgoing, block], 1)
        inputs[piece] = own
        partners[piece] = from_partner(outgoing, hops[level])
        previous = outgoing
        if (level, piece) == (levels - 1, COUNT_PIECE):
            most = after(jnp.maximum(extra[levels - 1 - wide], known)[:8, rank:], outgoing)
            for hop in hops[: wide - 1]:
                most = jnp.maximum(most, from_partner(most, hop))
            counted = from_partner(most, hops[wide - 1])
    quick = jnp.concatenate(done, 0)
    return lax.cond(
        most[0, 0] > 0,
        lambda: full_width(traces, sampling, skeleton[0], compress[0], evaluation),
        lambda: quick,
    )


def solution(mesh):
    placed = (
        P(("shots", "tr"), ("bfly", "sub")),
        P(("bfly", "sub"), None, None),
        P(("bfly", "sub"), None, None),
        P(("bfly", "sub"), None, None, None),
        P(("bfly", "sub"), None, None),
    )
    return jax.shard_map(
        local,
        mesh=mesh,
        in_specs=placed,
        out_specs=P(("shots", "tr"), ("bfly", "sub")),
        check_vma=False,
    )
```

```python
import jax
import jax.numpy as jnp
from jax import lax
from jax.experimental import pallas as pl
from jax.experimental.pallas import tpu as pltpu
from jax.sharding import PartitionSpec as P

SHARES = (1, 5, 8, 10, 8)
FULL_PIECES = (2, 1)
EARLY_PIECES = 2
COUNT_PIECE = 2
COUNT_READ = 2
LOOK = (3, -1)
MAKE = (0, -1)
ORDER = (
    (0, 0), (0, 1), (0, 2), (1, 0), (1, 1), MAKE, (2, 0), (0, 3), (1, 2), LOOK, (2, 1), (1, 3), (2, 2),
    (0, 4), (3, 0), (1, 4), (2, 3), (3, 1), (2, 4), (3, 2), (3, 3), (3, 4),
)
KERNEL_VMEM = 16 * 1024 * 1024
ROOM_SIXTEENTHS = (11, 10)


def route(axis, apart):
    count = lax.axis_size(axis)
    pairs = []
    for low in range(count):
        high = low | 1 << apart
        if high != low and high < count:
            pairs += [(low, high), (high, low)]
    return pairs


def from_partner(block, hop):
    return lax.ppermute(block, hop[0], route(*hop))


def across(left, right):
    return lax.dot_general(left, right, (((1,), (1,)), ((), ())), preferred_element_type=jnp.float32)


def one_hot(condition):
    return jnp.where(condition, 1.0, 0.0).astype(jnp.bfloat16)


def sampled_block(sampling, rows):
    turned = sampling.astype(jnp.float32).T.astype(jnp.bfloat16)
    return across(turned, rows).astype(jnp.bfloat16)


def early_kernel(starts, sampling_hbm, traces_hbm, *refs):
    pieces = len(starts) - 1
    outs, (sampling_ref, rows_ref, arrived) = refs[:pieces], refs[pieces:]
    loads = [pltpu.make_async_copy(sampling_hbm, sampling_ref, arrived.at[pieces])]
    for i in range(pieces):
        span = pl.ds(starts[i], starts[i + 1] - starts[i])
        loads.append(pltpu.make_async_copy(traces_hbm.at[span], rows_ref.at[span], arrived.at[i]))
    for load in loads:
        load.start()
    loads[0].wait()
    for i in range(pieces):
        loads[i + 1].wait()
        span = pl.ds(starts[i], starts[i + 1] - starts[i])
        outs[i][...] = sampled_block(sampling_ref[0], rows_ref[span])


def early(sampling, traces, starts):
    pieces = len(starts) - 1
    width = sampling.shape[-1]
    total = starts[-1]
    return pl.pallas_call(
        lambda *refs: early_kernel(starts, *refs),
        out_shape=[
            jax.ShapeDtypeStruct((width, starts[i + 1] - starts[i]), jnp.bfloat16) for i in range(pieces)
        ],
        in_specs=[pl.BlockSpec(memory_space=pltpu.HBM)] * 2,
        out_specs=[pl.BlockSpec(memory_space=pltpu.VMEM)] * pieces,
        scratch_shapes=[
            pltpu.VMEM(sampling.shape, jnp.bfloat16),
            pltpu.VMEM((total, traces.shape[1]), jnp.bfloat16),
            pltpu.SemaphoreType.DMA((pieces + 1,)),
        ],
        compiler_params=pltpu.CompilerParams(vmem_limit_bytes=KERNEL_VMEM),
        cost_estimate=pl.CostEstimate(
            flops=2 * total * width * width, bytes_accessed=4 * total * width, transcendentals=0
        ),
        name="early",
    )(sampling, traces)


def tables_kernel(
    wide, rooms, skeleton_hbm, compress_hbm, full_ref, small_ref, extra_ref,
    skeleton_ref, compress_ref, arrived,
):
    loads = [
        pltpu.make_async_copy(skeleton_hbm, skeleton_ref, arrived.at[0]),
        pltpu.make_async_copy(compress_hbm, compress_ref, arrived.at[1]),
    ]
    for load in loads:
        load.start()
    for load in loads:
        load.wait()
    levels, rank = skeleton_ref.shape[0], skeleton_ref.shape[-1]
    width = 2 * rank
    f32, i32 = jnp.float32, jnp.int32
    k = lax.broadcasted_iota(i32, (width, width), 1)
    twice = one_hot(lax.broadcasted_iota(i32, (width, rank), 0) % rank == lax.broadcasted_iota(i32, (width, rank), 1))
    earlier = one_hot(
        (lax.broadcasted_iota(i32, (width, width), 1) < lax.broadcasted_iota(i32, (width, width), 0) % rank)
    )
    column = lax.broadcasted_iota(i32, (2 * width, width), 0)
    is_real_entry = lax.broadcasted_iota(i32, (2 * width, width), 1) < rank
    partner_column = column >= width
    imag_column = column % width >= rank
    coefficient = column % rank + jnp.where(partner_column, rank, 0)
    slot_column = column - width
    row = lax.broadcasted_iota(i32, (width, width), 0)
    most = jnp.full((1, 1), -float(rank), f32)
    for level in range(levels):
        entry = jnp.broadcast_to(skeleton_ref[level].astype(f32), (8, rank)).astype(jnp.bfloat16)
        entry = across(entry, twice)[:1]
        picked = jnp.where(entry >= rank, 1.0, 0.0)
        slot = across(jnp.broadcast_to(picked, (8, width)).astype(jnp.bfloat16), earlier)[:1].astype(i32)
        entry = entry.astype(i32)
        from_partner_entry = entry >= rank
        matrix = compress_ref[0, level]

        def halves(match, imag):
            same = is_real_entry != imag
            real = jnp.where(match & same, jnp.where(imag, -1.0, 1.0), 0.0).astype(jnp.bfloat16)
            turned = one_hot(match & jnp.logical_not(same))
            return across(matrix, real).astype(jnp.bfloat16), across(matrix, turned).astype(jnp.bfloat16)

        match = entry == coefficient
        full_ref[level, :rank], full_ref[level, rank:] = halves(match, imag_column)
        if level < wide:
            continue
        high = level - wide
        room = rooms[high]
        slot_imag = slot_column >= room
        slot_of_column = jnp.where(slot_imag, slot_column - room, slot_column)
        compacted = (slot == slot_of_column) & from_partner_entry
        match = (match & jnp.logical_not(partner_column)) | (compacted & partner_column)
        imag = (imag_column & jnp.logical_not(partner_column)) | (slot_imag & partner_column)
        small_ref[high, :rank], small_ref[high, rank:] = halves(match, imag)
        once = (k < rank) & from_partner_entry
        places = across(one_hot(once & (slot == row)), one_hot(once & (entry - rank == row)))
        extra_ref[high] = places.astype(jnp.bfloat16)
        most = jnp.maximum(most, jnp.sum(picked, axis=1, keepdims=True) * 0.5 - room)
    for high in range(levels - wide):
        extra_ref[high] = jnp.where(k < rank, extra_ref[high].astype(f32), most).astype(jnp.bfloat16)


def tables(skeleton, compress, wide, rooms):
    levels, rank = skeleton.shape[1:]
    shape = (levels, 2 * rank, 4 * rank)
    return pl.pallas_call(
        lambda *refs: tables_kernel(wide, rooms, *refs),
        out_shape=[
            jax.ShapeDtypeStruct(shape, jnp.bfloat16),
            jax.ShapeDtypeStruct((levels - wide,) + shape[1:], jnp.bfloat16),
            jax.ShapeDtypeStruct((levels - wide, 2 * rank, 2 * rank), jnp.bfloat16),
        ],
        in_specs=[pl.BlockSpec(memory_space=pltpu.HBM)] * 2,
        out_specs=[pl.BlockSpec(memory_space=pltpu.VMEM)] * 3,
        scratch_shapes=[
            pltpu.VMEM((levels, 1, rank), jnp.int32),
            pltpu.VMEM(compress.shape, jnp.bfloat16),
            pltpu.SemaphoreType.DMA((2,)),
        ],
        compiler_params=pltpu.CompilerParams(vmem_limit_bytes=KERNEL_VMEM),
        cost_estimate=pl.CostEstimate(flops=50_000_000, bytes_accessed=600_000, transcendentals=0),
        name="tables",
    )(skeleton.transpose(1, 0, 2), compress)


def sampled_apart(sampling, traces):
    count, width = traces.shape
    block = count // 8

    def kernel(sampling_ref, rows_ref, coeffs_ref):
        coeffs_ref[...] = sampled_block(sampling_ref[...], rows_ref[...])

    return pl.pallas_call(
        kernel,
        grid=(count // block,),
        out_shape=jax.ShapeDtypeStruct((sampling.shape[1], count), jnp.bfloat16),
        in_specs=[
            pl.BlockSpec(sampling.shape, lambda i: (0, 0)),
            pl.BlockSpec((block, width), lambda i: (i, 0)),
        ],
        out_specs=pl.BlockSpec((sampling.shape[1], block), lambda i: (0, i)),
        compiler_params=pltpu.CompilerParams(vmem_limit_bytes=63 * 1024 * 1024),
        name="sampled_apart",
    )(sampling, traces)


def picked_columns(compress, skeleton):
    rank = skeleton.shape[-1]
    places = lax.broadcasted_iota(jnp.int32, (1, 1, 2 * rank), 2)
    chooser = (skeleton[:, :, None] == places).astype(jnp.bfloat16)
    stacked = jnp.concatenate([compress[:, :, :rank], compress[:, :, rank:]], 1)
    return jnp.einsum(
        "ljk,lki->lji", stacked, chooser, preferred_element_type=jnp.float32
    ).astype(jnp.bfloat16)


def real_form(both):
    rank = both.shape[1] // 2
    turned = jnp.concatenate([-both[:, rank:], both[:, :rank]], 1)
    return jnp.concatenate([both, turned], 2)


def compact_rows(matrix, slot):
    rank = slot.shape[1]
    parts = [
        jnp.dot(slot, half, preferred_element_type=jnp.float32)
        for half in (matrix[:rank], matrix[rank:])
    ]
    return jnp.concatenate(parts, 0).astype(jnp.bfloat16)


def times(matrix, value):
    return jnp.dot(matrix, value, preferred_element_type=jnp.float32).astype(jnp.bfloat16)


def sampled(sampling, traces):
    return jnp.einsum(
        "pc,tp->ct", sampling, traces, preferred_element_type=jnp.float32
    ).astype(jnp.bfloat16)


def evaluated(coeffs, evaluation):
    return jnp.einsum(
        "ct,cp->tp", coeffs, evaluation, preferred_element_type=jnp.float32
    ).astype(jnp.bfloat16)


def after(value, earlier):
    return value if earlier is None else lax.optimization_barrier((value, earlier))[0]


def all_hops():
    low_bits = lax.axis_size("sub").bit_length() - 1
    high_bits = lax.axis_size("bfly").bit_length() - 1
    return [("sub", bit) for bit in range(low_bits)] + [("bfly", bit) for bit in range(high_bits)]


def full_width(traces, sampling, skeleton, compress, evaluation):
    rank = skeleton.shape[-1]
    columns = picked_columns(compress, skeleton)
    full = jnp.concatenate([real_form(columns[..., :rank]), real_form(columns[..., rank:])], 2)
    coeffs = sampled_apart(sampling, traces)
    for level, hop in enumerate(all_hops()):
        partner = from_partner(coeffs, hop)
        coeffs = times(full[level], jnp.concatenate([coeffs, partner], 0))
    return evaluated(coeffs, evaluation)


def local(traces, sampling, skeleton, compress, evaluation):
    hops = all_hops()
    levels = len(hops)
    if (lax.axis_size("sub"), lax.axis_size("bfly")) != (2, 4):
        return full_width(traces, sampling[0], skeleton[0], compress[0], evaluation[0])
    wide = lax.axis_size("sub").bit_length() - 1
    rank = skeleton.shape[-1]
    rooms = [rank * share // 16 for share in ROOM_SIXTEENTHS]
    unit = traces.shape[0] // sum(SHARES)
    pieces = len(SHARES)
    starts = [unit * sum(SHARES[:i]) for i in range(pieces + 1)]
    coeffs = list(early(sampling, traces, starts[: EARLY_PIECES + 1]))
    full, small, extra = tables(after(skeleton, coeffs[0]), compress, wide, rooms)
    sampling, evaluation = sampling[0], evaluation[0]
    most_here = lax.broadcasted_iota(jnp.int32, extra.shape[1:], 1) >= rank

    def compact(level, piece):
        return level >= wide and piece >= FULL_PIECES[level - wide]

    inputs, partners, theirs, done = {}, {}, {}, [None] * pieces
    previous, finished, known = None, None, None
    for level, piece in ORDER:
        if (level, piece) == MAKE:
            waiting = after(sampling, previous)
            coeffs.append(sampled(waiting, traces[starts[pieces - 2] : starts[pieces - 1]]))
            previous = coeffs[-1]
            continue
        if (level, piece) == LOOK:
            known = after(after(partners[0], previous), partners[1])[:, starts[1] :]
            theirs[levels - 1] = known[: rooms[levels - 1 - wide], :rank]
            continue
        count = starts[piece + 1] - starts[piece]
        if level == 0:
            if piece == len(coeffs):
                waiting = after(sampling, previous)
                coeffs.append(sampled(waiting, traces[starts[piece] : starts[piece + 1]]))
            own = coeffs[piece]
            if piece == pieces - 2:
                coeffs.append(sampled(waiting, traces[starts[piece + 1] : starts[piece + 2]]))
        else:
            arrived = after(partners[piece], previous)
            if level == levels:
                arrived = after(arrived, finished)
            elif piece == 0 and level - 1 >= wide:
                known = arrived[:, count:]
                theirs[level - 1] = known[: rooms[level - 1 - wide], :rank]
            value = jnp.concatenate([inputs[piece], arrived[:, :count]], 0)
            matrix = full[level - 1]
            if compact(level - 1, piece):
                value = jnp.pad(value, ((0, full.shape[2] - value.shape[0]), (0, 0)))
                matrix = small[level - 1 - wide]
            if level < levels and compact(level, piece):
                outgoing = times(compact_rows(matrix, theirs[level]), value)
                own = times(after(matrix, outgoing), value)
            else:
                own = outgoing = times(matrix, value)
        if level == levels:
            done[piece] = finished = previous = evaluated(own, evaluation)
            if piece == COUNT_READ:
                most = jnp.maximum(most, after(counted, finished))
            continue
        if level == 0:
            outgoing = after(own, previous) if piece >= pieces - 2 else own
        if piece == 0 and level >= wide:
            block = extra[level - wide]
            if known is not None:
                block = jnp.where(most_here, jnp.maximum(block, known), block)
            outgoing = jnp.concatenate([outgoing, block], 1)
        inputs[piece] = own
        partners[piece] = from_partner(outgoing, hops[level])
        previous = outgoing
        if (level, piece) == (levels - 1, COUNT_PIECE):
            most = after(jnp.maximum(extra[levels - 1 - wide], known)[:8, rank:], outgoing)
            for hop in hops[: wide - 1]:
                most = jnp.maximum(most, from_partner(most, hop))
            counted = from_partner(most, hops[wide - 1])
    quick = jnp.concatenate(done, 0)
    return lax.cond(
        most[0, 0] > 0,
        lambda: full_width(traces, sampling, skeleton[0], compress[0], evaluation),
        lambda: quick,
    )


def solution(mesh):
    placed = (
        P(("shots", "tr"), ("bfly", "sub")),
        P(("bfly", "sub"), None, None),
        P(("bfly", "sub"), None, None),
        P(("bfly", "sub"), None, None, None),
        P(("bfly", "sub"), None, None),
    )
    return jax.shard_map(
        local,
        mesh=mesh,
        in_specs=placed,
        out_specs=P(("shots", "tr"), ("bfly", "sub")),
        check_vma=False,
    )
```

```python
import jax
import jax.numpy as jnp
from jax import lax
from jax.experimental import pallas as pl
from jax.experimental.pallas import tpu as pltpu
from jax.sharding import PartitionSpec as P

SHARES = (1, 6, 7, 9, 9)
FULL_PIECES = (2, 1)
EARLY_PIECES = 2
COUNT_PIECE = 2
COUNT_READ = 2
LOOK = (3, -1)
MAKE = (0, -1)
ORDER = (
    (0, 0), (0, 1), (0, 2), (1, 0), (1, 1), MAKE, (2, 0), (0, 3), (1, 2), LOOK, (2, 1), (1, 3), (2, 2),
    (0, 4), (3, 0), (1, 4), (2, 3), (3, 1), (2, 4), (3, 2), (3, 3), (3, 4),
)
KERNEL_VMEM = 16 * 1024 * 1024
ROOM_SIXTEENTHS = (11, 10)


def route(axis, apart):
    count = lax.axis_size(axis)
    pairs = []
    for low in range(count):
        high = low | 1 << apart
        if high != low and high < count:
            pairs += [(low, high), (high, low)]
    return pairs


def from_partner(block, hop):
    return lax.ppermute(block, hop[0], route(*hop))


def across(left, right):
    return lax.dot_general(left, right, (((1,), (1,)), ((), ())), preferred_element_type=jnp.float32)


def one_hot(condition):
    return jnp.where(condition, 1.0, 0.0).astype(jnp.bfloat16)


def sampled_block(sampling, rows):
    turned = sampling.astype(jnp.float32).T.astype(jnp.bfloat16)
    return across(turned, rows).astype(jnp.bfloat16)


def early_kernel(starts, sampling_hbm, traces_hbm, *refs):
    pieces = len(starts) - 1
    outs, (sampling_ref, rows_ref, arrived) = refs[:pieces], refs[pieces:]
    loads = [pltpu.make_async_copy(sampling_hbm, sampling_ref, arrived.at[pieces])]
    for i in range(pieces):
        span = pl.ds(starts[i], starts[i + 1] - starts[i])
        loads.append(pltpu.make_async_copy(traces_hbm.at[span], rows_ref.at[span], arrived.at[i]))
    for load in loads:
        load.start()
    loads[0].wait()
    for i in range(pieces):
        loads[i + 1].wait()
        span = pl.ds(starts[i], starts[i + 1] - starts[i])
        outs[i][...] = sampled_block(sampling_ref[0], rows_ref[span])


def early(sampling, traces, starts):
    pieces = len(starts) - 1
    width = sampling.shape[-1]
    total = starts[-1]
    return pl.pallas_call(
        lambda *refs: early_kernel(starts, *refs),
        out_shape=[
            jax.ShapeDtypeStruct((width, starts[i + 1] - starts[i]), jnp.bfloat16) for i in range(pieces)
        ],
        in_specs=[pl.BlockSpec(memory_space=pltpu.HBM)] * 2,
        out_specs=[pl.BlockSpec(memory_space=pltpu.VMEM)] * pieces,
        scratch_shapes=[
            pltpu.VMEM(sampling.shape, jnp.bfloat16),
            pltpu.VMEM((total, traces.shape[1]), jnp.bfloat16),
            pltpu.SemaphoreType.DMA((pieces + 1,)),
        ],
        compiler_params=pltpu.CompilerParams(vmem_limit_bytes=KERNEL_VMEM),
        cost_estimate=pl.CostEstimate(
            flops=2 * total * width * width, bytes_accessed=4 * total * width, transcendentals=0
        ),
        name="early",
    )(sampling, traces)


def tables_kernel(
    wide, rooms, skeleton_hbm, compress_hbm, full_ref, small_ref, extra_ref,
    skeleton_ref, compress_ref, arrived,
):
    loads = [
        pltpu.make_async_copy(skeleton_hbm, skeleton_ref, arrived.at[0]),
        pltpu.make_async_copy(compress_hbm, compress_ref, arrived.at[1]),
    ]
    for load in loads:
        load.start()
    for load in loads:
        load.wait()
    levels, rank = skeleton_ref.shape[0], skeleton_ref.shape[-1]
    width = 2 * rank
    f32, i32 = jnp.float32, jnp.int32
    k = lax.broadcasted_iota(i32, (width, width), 1)
    twice = one_hot(lax.broadcasted_iota(i32, (width, rank), 0) % rank == lax.broadcasted_iota(i32, (width, rank), 1))
    earlier = one_hot(
        (lax.broadcasted_iota(i32, (width, width), 1) < lax.broadcasted_iota(i32, (width, width), 0) % rank)
    )
    column = lax.broadcasted_iota(i32, (2 * width, width), 0)
    is_real_entry = lax.broadcasted_iota(i32, (2 * width, width), 1) < rank
    partner_column = column >= width
    imag_column = column % width >= rank
    coefficient = column % rank + jnp.where(partner_column, rank, 0)
    slot_column = column - width
    row = lax.broadcasted_iota(i32, (width, width), 0)
    most = jnp.full((1, 1), -float(rank), f32)
    for level in range(levels):
        entry = jnp.broadcast_to(skeleton_ref[level].astype(f32), (8, rank)).astype(jnp.bfloat16)
        entry = across(entry, twice)[:1]
        picked = jnp.where(entry >= rank, 1.0, 0.0)
        slot = across(jnp.broadcast_to(picked, (8, width)).astype(jnp.bfloat16), earlier)[:1].astype(i32)
        entry = entry.astype(i32)
        from_partner_entry = entry >= rank
        matrix = compress_ref[0, level]

        def halves(match, imag):
            same = is_real_entry != imag
            real = jnp.where(match & same, jnp.where(imag, -1.0, 1.0), 0.0).astype(jnp.bfloat16)
            turned = one_hot(match & jnp.logical_not(same))
            return across(matrix, real).astype(jnp.bfloat16), across(matrix, turned).astype(jnp.bfloat16)

        match = entry == coefficient
        full_ref[level, :rank], full_ref[level, rank:] = halves(match, imag_column)
        if level < wide:
            continue
        high = level - wide
        room = rooms[high]
        slot_imag = slot_column >= room
        slot_of_column = jnp.where(slot_imag, slot_column - room, slot_column)
        compacted = (slot == slot_of_column) & from_partner_entry
        match = (match & jnp.logical_not(partner_column)) | (compacted & partner_column)
        imag = (imag_column & jnp.logical_not(partner_column)) | (slot_imag & partner_column)
        small_ref[high, :rank], small_ref[high, rank:] = halves(match, imag)
        once = (k < rank) & from_partner_entry
        places = across(one_hot(once & (slot == row)), one_hot(once & (entry - rank == row)))
        extra_ref[high] = places.astype(jnp.bfloat16)
        most = jnp.maximum(most, jnp.sum(picked, axis=1, keepdims=True) * 0.5 - room)
    for high in range(levels - wide):
        extra_ref[high] = jnp.where(k < rank, extra_ref[high].astype(f32), most).astype(jnp.bfloat16)


def tables(skeleton, compress, wide, rooms):
    levels, rank = skeleton.shape[1:]
    shape = (levels, 2 * rank, 4 * rank)
    return pl.pallas_call(
        lambda *refs: tables_kernel(wide, rooms, *refs),
        out_shape=[
            jax.ShapeDtypeStruct(shape, jnp.bfloat16),
            jax.ShapeDtypeStruct((levels - wide,) + shape[1:], jnp.bfloat16),
            jax.ShapeDtypeStruct((levels - wide, 2 * rank, 2 * rank), jnp.bfloat16),
        ],
        in_specs=[pl.BlockSpec(memory_space=pltpu.HBM)] * 2,
        out_specs=[pl.BlockSpec(memory_space=pltpu.VMEM)] * 3,
        scratch_shapes=[
            pltpu.VMEM((levels, 1, rank), jnp.int32),
            pltpu.VMEM(compress.shape, jnp.bfloat16),
            pltpu.SemaphoreType.DMA((2,)),
        ],
        compiler_params=pltpu.CompilerParams(vmem_limit_bytes=KERNEL_VMEM),
        cost_estimate=pl.CostEstimate(flops=50_000_000, bytes_accessed=600_000, transcendentals=0),
        name="tables",
    )(skeleton.transpose(1, 0, 2), compress)


def sampled_apart(sampling, traces):
    count, width = traces.shape
    block = count // 8

    def kernel(sampling_ref, rows_ref, coeffs_ref):
        coeffs_ref[...] = sampled_block(sampling_ref[...], rows_ref[...])

    return pl.pallas_call(
        kernel,
        grid=(count // block,),
        out_shape=jax.ShapeDtypeStruct((sampling.shape[1], count), jnp.bfloat16),
        in_specs=[
            pl.BlockSpec(sampling.shape, lambda i: (0, 0)),
            pl.BlockSpec((block, width), lambda i: (i, 0)),
        ],
        out_specs=pl.BlockSpec((sampling.shape[1], block), lambda i: (0, i)),
        compiler_params=pltpu.CompilerParams(vmem_limit_bytes=63 * 1024 * 1024),
        name="sampled_apart",
    )(sampling, traces)


def picked_columns(compress, skeleton):
    rank = skeleton.shape[-1]
    places = lax.broadcasted_iota(jnp.int32, (1, 1, 2 * rank), 2)
    chooser = (skeleton[:, :, None] == places).astype(jnp.bfloat16)
    stacked = jnp.concatenate([compress[:, :, :rank], compress[:, :, rank:]], 1)
    return jnp.einsum(
        "ljk,lki->lji", stacked, chooser, preferred_element_type=jnp.float32
    ).astype(jnp.bfloat16)


def real_form(both):
    rank = both.shape[1] // 2
    turned = jnp.concatenate([-both[:, rank:], both[:, :rank]], 1)
    return jnp.concatenate([both, turned], 2)


def compact_rows(matrix, slot):
    rank = slot.shape[1]
    parts = [
        jnp.dot(slot, half, preferred_element_type=jnp.float32)
        for half in (matrix[:rank], matrix[rank:])
    ]
    return jnp.concatenate(parts, 0).astype(jnp.bfloat16)


def times(matrix, value):
    return jnp.dot(matrix, value, preferred_element_type=jnp.float32).astype(jnp.bfloat16)


def sampled(sampling, traces):
    return jnp.einsum(
        "pc,tp->ct", sampling, traces, preferred_element_type=jnp.float32
    ).astype(jnp.bfloat16)


def evaluated(coeffs, evaluation):
    return jnp.einsum(
        "ct,cp->tp", coeffs, evaluation, preferred_element_type=jnp.float32
    ).astype(jnp.bfloat16)


def after(value, earlier):
    return value if earlier is None else lax.optimization_barrier((value, earlier))[0]


def all_hops():
    low_bits = lax.axis_size("sub").bit_length() - 1
    high_bits = lax.axis_size("bfly").bit_length() - 1
    return [("sub", bit) for bit in range(low_bits)] + [("bfly", bit) for bit in range(high_bits)]


def full_width(traces, sampling, skeleton, compress, evaluation):
    rank = skeleton.shape[-1]
    columns = picked_columns(compress, skeleton)
    full = jnp.concatenate([real_form(columns[..., :rank]), real_form(columns[..., rank:])], 2)
    coeffs = sampled_apart(sampling, traces)
    for level, hop in enumerate(all_hops()):
        partner = from_partner(coeffs, hop)
        coeffs = times(full[level], jnp.concatenate([coeffs, partner], 0))
    return evaluated(coeffs, evaluation)


def local(traces, sampling, skeleton, compress, evaluation):
    hops = all_hops()
    levels = len(hops)
    if (lax.axis_size("sub"), lax.axis_size("bfly")) != (2, 4):
        return full_width(traces, sampling[0], skeleton[0], compress[0], evaluation[0])
    wide = lax.axis_size("sub").bit_length() - 1
    rank = skeleton.shape[-1]
    rooms = [rank * share // 16 for share in ROOM_SIXTEENTHS]
    unit = traces.shape[0] // sum(SHARES)
    pieces = len(SHARES)
    starts = [unit * sum(SHARES[:i]) for i in range(pieces + 1)]
    coeffs = list(early(sampling, traces, starts[: EARLY_PIECES + 1]))
    full, small, extra = tables(after(skeleton, coeffs[0]), compress, wide, rooms)
    sampling, evaluation = sampling[0], evaluation[0]
    most_here = lax.broadcasted_iota(jnp.int32, extra.shape[1:], 1) >= rank

    def compact(level, piece):
        return level >= wide and piece >= FULL_PIECES[level - wide]

    inputs, partners, theirs, done = {}, {}, {}, [None] * pieces
    previous, finished, known = None, None, None
    for level, piece in ORDER:
        if (level, piece) == MAKE:
            waiting = after(sampling, previous)
            coeffs.append(sampled(waiting, traces[starts[pieces - 2] : starts[pieces - 1]]))
            previous = coeffs[-1]
            continue
        if (level, piece) == LOOK:
            known = after(after(partners[0], previous), partners[1])[:, starts[1] :]
            theirs[levels - 1] = known[: rooms[levels - 1 - wide], :rank]
            continue
        count = starts[piece + 1] - starts[piece]
        if level == 0:
            if piece == len(coeffs):
                waiting = after(sampling, previous)
                coeffs.append(sampled(waiting, traces[starts[piece] : starts[piece + 1]]))
            own = coeffs[piece]
            if piece == pieces - 2:
                coeffs.append(sampled(waiting, traces[starts[piece + 1] : starts[piece + 2]]))
        else:
            arrived = after(partners[piece], previous)
            if level == levels:
                arrived = after(arrived, finished)
            elif piece == 0 and level - 1 >= wide:
                known = arrived[:, count:]
                theirs[level - 1] = known[: rooms[level - 1 - wide], :rank]
            value = jnp.concatenate([inputs[piece], arrived[:, :count]], 0)
            matrix = full[level - 1]
            if compact(level - 1, piece):
                value = jnp.pad(value, ((0, full.shape[2] - value.shape[0]), (0, 0)))
                matrix = small[level - 1 - wide]
            if level < levels and compact(level, piece):
                outgoing = times(compact_rows(matrix, theirs[level]), value)
                own = times(after(matrix, outgoing), value)
            else:
                own = outgoing = times(matrix, value)
        if level == levels:
            done[piece] = finished = previous = evaluated(own, evaluation)
            if piece == COUNT_READ:
                most = jnp.maximum(most, after(counted, finished))
            continue
        if level == 0:
            outgoing = after(own, previous) if piece >= pieces - 2 else own
        if piece == 0 and level >= wide:
            block = extra[level - wide]
            if known is not None:
                block = jnp.where(most_here, jnp.maximum(block, known), block)
            outgoing = jnp.concatenate([outgoing, block], 1)
        inputs[piece] = own
        partners[piece] = from_partner(outgoing, hops[level])
        previous = outgoing
        if (level, piece) == (levels - 1, COUNT_PIECE):
            most = after(jnp.maximum(extra[levels - 1 - wide], known)[:8, rank:], outgoing)
            for hop in hops[: wide - 1]:
                most = jnp.maximum(most, from_partner(most, hop))
            counted = from_partner(most, hops[wide - 1])
    quick = jnp.concatenate(done, 0)
    return lax.cond(
        most[0, 0] > 0,
        lambda: full_width(traces, sampling, skeleton[0], compress[0], evaluation),
        lambda: quick,
    )


def solution(mesh):
    placed = (
        P(("shots", "tr"), ("bfly", "sub")),
        P(("bfly", "sub"), None, None),
        P(("bfly", "sub"), None, None),
        P(("bfly", "sub"), None, None, None),
        P(("bfly", "sub"), None, None),
    )
    return jax.shard_map(
        local,
        mesh=mesh,
        in_specs=placed,
        out_specs=P(("shots", "tr"), ("bfly", "sub")),
        check_vma=False,
    )
```

```python
import jax
import jax.numpy as jnp
from jax import lax
from jax.experimental import pallas as pl
from jax.experimental.pallas import tpu as pltpu
from jax.sharding import PartitionSpec as P

SHARES = (1, 5, 8, 10, 8)
FULL_PIECES = (2, 1)
EARLY_PIECES = 2
COUNT_PIECE = 2
COUNT_READ = 2
LOOK = (3, -1)
MAKE = (0, -1)
ORDER = (
    (0, 0), (0, 1), (0, 2), (1, 0), (1, 1), MAKE, (2, 0), (0, 3), (1, 2), LOOK, (2, 1), (1, 3), (2, 2),
    (0, 4), (3, 0), (1, 4), (2, 3), (3, 1), (2, 4), (3, 2), (3, 3), (3, 4),
)
KERNEL_VMEM = 16 * 1024 * 1024
ROOM_SIXTEENTHS = (11, 10)
MOST_ROW = 96


def route(axis, apart):
    count = lax.axis_size(axis)
    pairs = []
    for low in range(count):
        high = low | 1 << apart
        if high != low and high < count:
            pairs += [(low, high), (high, low)]
    return pairs


def from_partner(block, hop):
    return lax.ppermute(block, hop[0], route(*hop))


def across(left, right):
    return lax.dot_general(left, right, (((1,), (1,)), ((), ())), preferred_element_type=jnp.float32)


def one_hot(condition):
    return jnp.where(condition, 1.0, 0.0).astype(jnp.bfloat16)


def sampled_block(sampling, rows):
    turned = sampling.astype(jnp.float32).T.astype(jnp.bfloat16)
    return across(turned, rows).astype(jnp.bfloat16)


def early_kernel(starts, sampling_hbm, traces_hbm, *refs):
    pieces = len(starts) - 1
    outs, (sampling_ref, rows_ref, arrived) = refs[:pieces], refs[pieces:]
    loads = [pltpu.make_async_copy(sampling_hbm, sampling_ref, arrived.at[pieces])]
    for i in range(pieces):
        span = pl.ds(starts[i], starts[i + 1] - starts[i])
        loads.append(pltpu.make_async_copy(traces_hbm.at[span], rows_ref.at[span], arrived.at[i]))
    for load in loads:
        load.start()
    loads[0].wait()
    for i in range(pieces):
        loads[i + 1].wait()
        span = pl.ds(starts[i], starts[i + 1] - starts[i])
        outs[i][...] = sampled_block(sampling_ref[0], rows_ref[span])


def early(sampling, traces, starts):
    pieces = len(starts) - 1
    width = sampling.shape[-1]
    total = starts[-1]
    return pl.pallas_call(
        lambda *refs: early_kernel(starts, *refs),
        out_shape=[
            jax.ShapeDtypeStruct((width, starts[i + 1] - starts[i]), jnp.bfloat16) for i in range(pieces)
        ],
        in_specs=[pl.BlockSpec(memory_space=pltpu.HBM)] * 2,
        out_specs=[pl.BlockSpec(memory_space=pltpu.VMEM)] * pieces,
        scratch_shapes=[
            pltpu.VMEM(sampling.shape, jnp.bfloat16),
            pltpu.VMEM((total, traces.shape[1]), jnp.bfloat16),
            pltpu.SemaphoreType.DMA((pieces + 1,)),
        ],
        compiler_params=pltpu.CompilerParams(vmem_limit_bytes=KERNEL_VMEM),
        cost_estimate=pl.CostEstimate(
            flops=2 * total * width * width, bytes_accessed=4 * total * width, transcendentals=0
        ),
        name="early",
    )(sampling, traces)


def tables_kernel(
    wide, rooms, skeleton_hbm, compress_hbm, full_ref, small_ref, extra_ref,
    skeleton_ref, compress_ref, arrived,
):
    loads = [
        pltpu.make_async_copy(skeleton_hbm, skeleton_ref, arrived.at[0]),
        pltpu.make_async_copy(compress_hbm, compress_ref, arrived.at[1]),
    ]
    for load in loads:
        load.start()
    for load in loads:
        load.wait()
    levels, rank = skeleton_ref.shape[0], skeleton_ref.shape[-1]
    width = 2 * rank
    f32, i32 = jnp.float32, jnp.int32
    k = lax.broadcasted_iota(i32, (width, width), 1)
    twice = one_hot(lax.broadcasted_iota(i32, (width, rank), 0) % rank == lax.broadcasted_iota(i32, (width, rank), 1))
    earlier = one_hot(
        (lax.broadcasted_iota(i32, (width, width), 1) < lax.broadcasted_iota(i32, (width, width), 0) % rank)
    )
    column = lax.broadcasted_iota(i32, (2 * width, width), 0)
    is_real_entry = lax.broadcasted_iota(i32, (2 * width, width), 1) < rank
    partner_column = column >= width
    imag_column = column % width >= rank
    coefficient = column % rank + jnp.where(partner_column, rank, 0)
    slot_column = column - width
    row = lax.broadcasted_iota(i32, (width, width), 0)
    most = jnp.full((1, 1), -float(rank), f32)
    for level in range(levels):
        entry = jnp.broadcast_to(skeleton_ref[level].astype(f32), (8, rank)).astype(jnp.bfloat16)
        entry = across(entry, twice)[:1]
        picked = jnp.where(entry >= rank, 1.0, 0.0)
        slot = across(jnp.broadcast_to(picked, (8, width)).astype(jnp.bfloat16), earlier)[:1].astype(i32)
        entry = entry.astype(i32)
        from_partner_entry = entry >= rank
        matrix = compress_ref[0, level]

        def halves(match, imag):
            same = is_real_entry != imag
            real = jnp.where(match & same, jnp.where(imag, -1.0, 1.0), 0.0).astype(jnp.bfloat16)
            turned = one_hot(match & jnp.logical_not(same))
            return across(matrix, real).astype(jnp.bfloat16), across(matrix, turned).astype(jnp.bfloat16)

        match = entry == coefficient
        full_ref[level, :rank], full_ref[level, rank:] = halves(match, imag_column)
        if level < wide:
            continue
        high = level - wide
        room = rooms[high]
        slot_imag = slot_column >= room
        slot_of_column = jnp.where(slot_imag, slot_column - room, slot_column)
        compacted = (slot == slot_of_column) & from_partner_entry
        match = (match & jnp.logical_not(partner_column)) | (compacted & partner_column)
        imag = (imag_column & jnp.logical_not(partner_column)) | (slot_imag & partner_column)
        small_ref[high, :rank], small_ref[high, rank:] = halves(match, imag)
        imag_entry = jnp.where(k < rank, 0, 1)
        used = from_partner_entry & (slot < room)
        to_slot = one_hot(used & (slot + room * imag_entry == row))
        from_coefficient = one_hot(used & (entry - rank + rank * imag_entry == row))
        extra_ref[high] = across(to_slot, from_coefficient).astype(jnp.bfloat16)
        most = jnp.maximum(most, jnp.sum(picked, axis=1, keepdims=True) * 0.5 - room)
    for high in range(levels - wide):
        extra_ref[high] = jnp.where(row < MOST_ROW, extra_ref[high].astype(f32), most).astype(jnp.bfloat16)


def tables(skeleton, compress, wide, rooms):
    levels, rank = skeleton.shape[1:]
    shape = (levels, 2 * rank, 4 * rank)
    return pl.pallas_call(
        lambda *refs: tables_kernel(wide, rooms, *refs),
        out_shape=[
            jax.ShapeDtypeStruct(shape, jnp.bfloat16),
            jax.ShapeDtypeStruct((levels - wide,) + shape[1:], jnp.bfloat16),
            jax.ShapeDtypeStruct((levels - wide, 2 * rank, 2 * rank), jnp.bfloat16),
        ],
        in_specs=[pl.BlockSpec(memory_space=pltpu.HBM)] * 2,
        out_specs=[pl.BlockSpec(memory_space=pltpu.VMEM)] * 3,
        scratch_shapes=[
            pltpu.VMEM((levels, 1, rank), jnp.int32),
            pltpu.VMEM(compress.shape, jnp.bfloat16),
            pltpu.SemaphoreType.DMA((2,)),
        ],
        compiler_params=pltpu.CompilerParams(vmem_limit_bytes=KERNEL_VMEM),
        cost_estimate=pl.CostEstimate(flops=50_000_000, bytes_accessed=600_000, transcendentals=0),
        name="tables",
    )(skeleton.transpose(1, 0, 2), compress)


def sampled_apart(sampling, traces):
    count, width = traces.shape
    block = count // 8

    def kernel(sampling_ref, rows_ref, coeffs_ref):
        coeffs_ref[...] = sampled_block(sampling_ref[...], rows_ref[...])

    return pl.pallas_call(
        kernel,
        grid=(count // block,),
        out_shape=jax.ShapeDtypeStruct((sampling.shape[1], count), jnp.bfloat16),
        in_specs=[
            pl.BlockSpec(sampling.shape, lambda i: (0, 0)),
            pl.BlockSpec((block, width), lambda i: (i, 0)),
        ],
        out_specs=pl.BlockSpec((sampling.shape[1], block), lambda i: (0, i)),
        compiler_params=pltpu.CompilerParams(vmem_limit_bytes=63 * 1024 * 1024),
        name="sampled_apart",
    )(sampling, traces)


def picked_columns(compress, skeleton):
    rank = skeleton.shape[-1]
    places = lax.broadcasted_iota(jnp.int32, (1, 1, 2 * rank), 2)
    chooser = (skeleton[:, :, None] == places).astype(jnp.bfloat16)
    stacked = jnp.concatenate([compress[:, :, :rank], compress[:, :, rank:]], 1)
    return jnp.einsum(
        "ljk,lki->lji", stacked, chooser, preferred_element_type=jnp.float32
    ).astype(jnp.bfloat16)


def real_form(both):
    rank = both.shape[1] // 2
    turned = jnp.concatenate([-both[:, rank:], both[:, :rank]], 1)
    return jnp.concatenate([both, turned], 2)


def times(matrix, value):
    return jnp.dot(matrix, value, preferred_element_type=jnp.float32).astype(jnp.bfloat16)


def sampled(sampling, traces):
    return jnp.einsum(
        "pc,tp->ct", sampling, traces, preferred_element_type=jnp.float32
    ).astype(jnp.bfloat16)


def evaluated(coeffs, evaluation):
    return jnp.einsum(
        "ct,cp->tp", coeffs, evaluation, preferred_element_type=jnp.float32
    ).astype(jnp.bfloat16)


def after(value, earlier):
    return value if earlier is None else lax.optimization_barrier((value, earlier))[0]


def all_hops():
    low_bits = lax.axis_size("sub").bit_length() - 1
    high_bits = lax.axis_size("bfly").bit_length() - 1
    return [("sub", bit) for bit in range(low_bits)] + [("bfly", bit) for bit in range(high_bits)]


def full_width(traces, sampling, skeleton, compress, evaluation):
    rank = skeleton.shape[-1]
    columns = picked_columns(compress, skeleton)
    full = jnp.concatenate([real_form(columns[..., :rank]), real_form(columns[..., rank:])], 2)
    coeffs = sampled_apart(sampling, traces)
    for level, hop in enumerate(all_hops()):
        partner = from_partner(coeffs, hop)
        coeffs = times(full[level], jnp.concatenate([coeffs, partner], 0))
    return evaluated(coeffs, evaluation)


def local(traces, sampling, skeleton, compress, evaluation):
    hops = all_hops()
    levels = len(hops)
    if (lax.axis_size("sub"), lax.axis_size("bfly")) != (2, 4):
        return full_width(traces, sampling[0], skeleton[0], compress[0], evaluation[0])
    wide = lax.axis_size("sub").bit_length() - 1
    rank = skeleton.shape[-1]
    rooms = [rank * share // 16 for share in ROOM_SIXTEENTHS]
    unit = traces.shape[0] // sum(SHARES)
    pieces = len(SHARES)
    starts = [unit * sum(SHARES[:i]) for i in range(pieces + 1)]
    coeffs = list(early(sampling, traces, starts[: EARLY_PIECES + 1]))
    full, small, extra = tables(after(skeleton, coeffs[0]), compress, wide, rooms)
    sampling, evaluation = sampling[0], evaluation[0]
    most_here = lax.broadcasted_iota(jnp.int32, extra.shape[1:], 0) >= MOST_ROW

    def compact(level, piece):
        return level >= wide and piece >= FULL_PIECES[level - wide]

    inputs, partners, theirs, done = {}, {}, {}, [None] * pieces
    previous, finished, known = None, None, None
    for level, piece in ORDER:
        if (level, piece) == MAKE:
            waiting = after(sampling, previous)
            coeffs.append(sampled(waiting, traces[starts[pieces - 2] : starts[pieces - 1]]))
            previous = coeffs[-1]
            continue
        if (level, piece) == LOOK:
            known = after(after(partners[0], previous), partners[1])[:, starts[1] :]
            theirs[levels - 1] = known[: 2 * rooms[levels - 1 - wide]]
            continue
        count = starts[piece + 1] - starts[piece]
        if level == 0:
            if piece == len(coeffs):
                waiting = after(sampling, previous)
                coeffs.append(sampled(waiting, traces[starts[piece] : starts[piece + 1]]))
            own = coeffs[piece]
            if piece == pieces - 2:
                coeffs.append(sampled(waiting, traces[starts[piece + 1] : starts[piece + 2]]))
        else:
            arrived = after(partners[piece], previous)
            if level == levels:
                arrived = after(arrived, finished)
            elif piece == 0 and level - 1 >= wide:
                known = arrived[:, count:]
                theirs[level - 1] = known[: 2 * rooms[level - 1 - wide]]
            value = jnp.concatenate([inputs[piece], arrived[:, :count]], 0)
            matrix = full[level - 1]
            if compact(level - 1, piece):
                value = jnp.pad(value, ((0, full.shape[2] - value.shape[0]), (0, 0)))
                matrix = small[level - 1 - wide]
            if level < levels and compact(level, piece):
                outgoing = times(times(theirs[level], matrix), value)
                own = times(after(matrix, outgoing), value)
            else:
                own = outgoing = times(matrix, value)
        if level == levels:
            done[piece] = finished = previous = evaluated(own, evaluation)
            if piece == COUNT_READ:
                most = jnp.maximum(most, after(counted, finished))
            continue
        if level == 0:
            outgoing = after(own, previous) if piece >= pieces - 2 else own
        if piece == 0 and level >= wide:
            block = extra[level - wide]
            if known is not None:
                block = jnp.where(most_here, jnp.maximum(block, known), block)
            outgoing = jnp.concatenate([outgoing, block], 1)
        inputs[piece] = own
        partners[piece] = from_partner(outgoing, hops[level])
        previous = outgoing
        if (level, piece) == (levels - 1, COUNT_PIECE):
            most = after(jnp.maximum(extra[levels - 1 - wide], known)[MOST_ROW : MOST_ROW + 8], outgoing)
            for hop in hops[: wide - 1]:
                most = jnp.maximum(most, from_partner(most, hop))
            counted = from_partner(most, hops[wide - 1])
    quick = jnp.concatenate(done, 0)
    return lax.cond(
        most[0, 0] > 0,
        lambda: full_width(traces, sampling, skeleton[0], compress[0], evaluation),
        lambda: quick,
    )


def solution(mesh):
    placed = (
        P(("shots", "tr"), ("bfly", "sub")),
        P(("bfly", "sub"), None, None),
        P(("bfly", "sub"), None, None),
        P(("bfly", "sub"), None, None, None),
        P(("bfly", "sub"), None, None),
    )
    return jax.shard_map(
        local,
        mesh=mesh,
        in_specs=placed,
        out_specs=P(("shots", "tr"), ("bfly", "sub")),
        check_vma=False,
    )
```

```python
import jax
import jax.numpy as jnp
from jax import lax
from jax.experimental import pallas as pl
from jax.experimental.pallas import tpu as pltpu
from jax.sharding import PartitionSpec as P

SHARES = (1, 5, 8, 10, 8)
FULL_PIECES = (2, 1)
EARLY_PIECES = 2
COUNT_PIECE = 2
COUNT_READ = 2
TELL = (1, -1)
LOOK = (3, -1)
MAKE = (0, -1)
ORDER = (
    (0, 0), (0, 1), (0, 2), (1, 0), TELL, (1, 1), MAKE, (2, 0), (0, 3), (1, 2), LOOK, (2, 1), (1, 3), (2, 2),
    (0, 4), (3, 0), (1, 4), (2, 3), (3, 1), (2, 4), (3, 2), (3, 3), (3, 4),
)
KERNEL_VMEM = 16 * 1024 * 1024
ROOM_SIXTEENTHS = (11, 10)
MOST_ROW = 96


def route(axis, apart):
    count = lax.axis_size(axis)
    pairs = []
    for low in range(count):
        high = low | 1 << apart
        if high != low and high < count:
            pairs += [(low, high), (high, low)]
    return pairs


def from_partner(block, hop):
    return lax.ppermute(block, hop[0], route(*hop))


def across(left, right):
    return lax.dot_general(left, right, (((1,), (1,)), ((), ())), preferred_element_type=jnp.float32)


def one_hot(condition):
    return jnp.where(condition, 1.0, 0.0).astype(jnp.bfloat16)


def sampled_block(sampling, rows):
    turned = sampling.astype(jnp.float32).T.astype(jnp.bfloat16)
    return across(turned, rows).astype(jnp.bfloat16)


def early_kernel(starts, sampling_hbm, traces_hbm, *refs):
    pieces = len(starts) - 1
    outs, (sampling_ref, rows_ref, arrived) = refs[:pieces], refs[pieces:]
    loads = [pltpu.make_async_copy(sampling_hbm, sampling_ref, arrived.at[pieces])]
    for i in range(pieces):
        span = pl.ds(starts[i], starts[i + 1] - starts[i])
        loads.append(pltpu.make_async_copy(traces_hbm.at[span], rows_ref.at[span], arrived.at[i]))
    for load in loads:
        load.start()
    loads[0].wait()
    for i in range(pieces):
        loads[i + 1].wait()
        span = pl.ds(starts[i], starts[i + 1] - starts[i])
        outs[i][...] = sampled_block(sampling_ref[0], rows_ref[span])


def early(sampling, traces, starts):
    pieces = len(starts) - 1
    width = sampling.shape[-1]
    total = starts[-1]
    return pl.pallas_call(
        lambda *refs: early_kernel(starts, *refs),
        out_shape=[
            jax.ShapeDtypeStruct((width, starts[i + 1] - starts[i]), jnp.bfloat16) for i in range(pieces)
        ],
        in_specs=[pl.BlockSpec(memory_space=pltpu.HBM)] * 2,
        out_specs=[pl.BlockSpec(memory_space=pltpu.VMEM)] * pieces,
        scratch_shapes=[
            pltpu.VMEM(sampling.shape, jnp.bfloat16),
            pltpu.VMEM((total, traces.shape[1]), jnp.bfloat16),
            pltpu.SemaphoreType.DMA((pieces + 1,)),
        ],
        compiler_params=pltpu.CompilerParams(vmem_limit_bytes=KERNEL_VMEM),
        cost_estimate=pl.CostEstimate(
            flops=2 * total * width * width, bytes_accessed=4 * total * width, transcendentals=0
        ),
        name="early",
    )(sampling, traces)


def tables_kernel(
    wide, rooms, skeleton_hbm, compress_hbm, full_ref, small_ref, extra_ref,
    skeleton_ref, compress_ref, arrived,
):
    loads = [
        pltpu.make_async_copy(skeleton_hbm, skeleton_ref, arrived.at[0]),
        pltpu.make_async_copy(compress_hbm, compress_ref, arrived.at[1]),
    ]
    for load in loads:
        load.start()
    for load in loads:
        load.wait()
    levels, rank = skeleton_ref.shape[0], skeleton_ref.shape[-1]
    width = 2 * rank
    f32, i32 = jnp.float32, jnp.int32
    k = lax.broadcasted_iota(i32, (width, width), 1)
    twice = one_hot(lax.broadcasted_iota(i32, (width, rank), 0) % rank == lax.broadcasted_iota(i32, (width, rank), 1))
    earlier = one_hot(
        (lax.broadcasted_iota(i32, (width, width), 1) < lax.broadcasted_iota(i32, (width, width), 0) % rank)
    )
    column = lax.broadcasted_iota(i32, (2 * width, width), 0)
    is_real_entry = lax.broadcasted_iota(i32, (2 * width, width), 1) < rank
    partner_column = column >= width
    imag_column = column % width >= rank
    coefficient = column % rank + jnp.where(partner_column, rank, 0)
    slot_column = column - width
    row = lax.broadcasted_iota(i32, (width, width), 0)
    most = jnp.full((1, 1), -float(rank), f32)
    for level in range(levels):
        entry = jnp.broadcast_to(skeleton_ref[level].astype(f32), (8, rank)).astype(jnp.bfloat16)
        entry = across(entry, twice)[:1]
        picked = jnp.where(entry >= rank, 1.0, 0.0)
        slot = across(jnp.broadcast_to(picked, (8, width)).astype(jnp.bfloat16), earlier)[:1].astype(i32)
        entry = entry.astype(i32)
        from_partner_entry = entry >= rank
        matrix = compress_ref[0, level]

        def halves(match, imag):
            same = is_real_entry != imag
            real = jnp.where(match & same, jnp.where(imag, -1.0, 1.0), 0.0).astype(jnp.bfloat16)
            turned = one_hot(match & jnp.logical_not(same))
            return across(matrix, real).astype(jnp.bfloat16), across(matrix, turned).astype(jnp.bfloat16)

        match = entry == coefficient
        full_ref[level, :rank], full_ref[level, rank:] = halves(match, imag_column)
        if level < wide:
            continue
        high = level - wide
        room = rooms[high]
        slot_imag = slot_column >= room
        slot_of_column = jnp.where(slot_imag, slot_column - room, slot_column)
        compacted = (slot == slot_of_column) & from_partner_entry
        match = (match & jnp.logical_not(partner_column)) | (compacted & partner_column)
        imag = (imag_column & jnp.logical_not(partner_column)) | (slot_imag & partner_column)
        small_ref[high, :rank], small_ref[high, rank:] = halves(match, imag)
        imag_entry = jnp.where(k < rank, 0, 1)
        used = from_partner_entry & (slot < room)
        to_slot = one_hot(used & (slot + room * imag_entry == row))
        from_coefficient = one_hot(used & (entry - rank + rank * imag_entry == row))
        extra_ref[high] = across(to_slot, from_coefficient).astype(jnp.bfloat16)
        most = jnp.maximum(most, jnp.sum(picked, axis=1, keepdims=True) * 0.5 - room)
    for high in range(levels - wide):
        extra_ref[high] = jnp.where(row < MOST_ROW, extra_ref[high].astype(f32), most).astype(jnp.bfloat16)


def tables(skeleton, compress, wide, rooms):
    levels, rank = skeleton.shape[1:]
    shape = (levels, 2 * rank, 4 * rank)
    return pl.pallas_call(
        lambda *refs: tables_kernel(wide, rooms, *refs),
        out_shape=[
            jax.ShapeDtypeStruct(shape, jnp.bfloat16),
            jax.ShapeDtypeStruct((levels - wide,) + shape[1:], jnp.bfloat16),
            jax.ShapeDtypeStruct((levels - wide, 2 * rank, 2 * rank), jnp.bfloat16),
        ],
        in_specs=[pl.BlockSpec(memory_space=pltpu.HBM)] * 2,
        out_specs=[pl.BlockSpec(memory_space=pltpu.VMEM)] * 3,
        scratch_shapes=[
            pltpu.VMEM((levels, 1, rank), jnp.int32),
            pltpu.VMEM(compress.shape, jnp.bfloat16),
            pltpu.SemaphoreType.DMA((2,)),
        ],
        compiler_params=pltpu.CompilerParams(vmem_limit_bytes=KERNEL_VMEM),
        cost_estimate=pl.CostEstimate(flops=50_000_000, bytes_accessed=600_000, transcendentals=0),
        name="tables",
    )(skeleton.transpose(1, 0, 2), compress)


def sampled_apart(sampling, traces):
    count, width = traces.shape
    block = count // 8

    def kernel(sampling_ref, rows_ref, coeffs_ref):
        coeffs_ref[...] = sampled_block(sampling_ref[...], rows_ref[...])

    return pl.pallas_call(
        kernel,
        grid=(count // block,),
        out_shape=jax.ShapeDtypeStruct((sampling.shape[1], count), jnp.bfloat16),
        in_specs=[
            pl.BlockSpec(sampling.shape, lambda i: (0, 0)),
            pl.BlockSpec((block, width), lambda i: (i, 0)),
        ],
        out_specs=pl.BlockSpec((sampling.shape[1], block), lambda i: (0, i)),
        compiler_params=pltpu.CompilerParams(vmem_limit_bytes=63 * 1024 * 1024),
        name="sampled_apart",
    )(sampling, traces)


def picked_columns(compress, skeleton):
    rank = skeleton.shape[-1]
    places = lax.broadcasted_iota(jnp.int32, (1, 1, 2 * rank), 2)
    chooser = (skeleton[:, :, None] == places).astype(jnp.bfloat16)
    stacked = jnp.concatenate([compress[:, :, :rank], compress[:, :, rank:]], 1)
    return jnp.einsum(
        "ljk,lki->lji", stacked, chooser, preferred_element_type=jnp.float32
    ).astype(jnp.bfloat16)


def real_form(both):
    rank = both.shape[1] // 2
    turned = jnp.concatenate([-both[:, rank:], both[:, :rank]], 1)
    return jnp.concatenate([both, turned], 2)


def times(matrix, value):
    return jnp.dot(matrix, value, preferred_element_type=jnp.float32).astype(jnp.bfloat16)


def sampled(sampling, traces):
    return jnp.einsum(
        "pc,tp->ct", sampling, traces, preferred_element_type=jnp.float32
    ).astype(jnp.bfloat16)


def evaluated(coeffs, evaluation):
    return jnp.einsum(
        "ct,cp->tp", coeffs, evaluation, preferred_element_type=jnp.float32
    ).astype(jnp.bfloat16)


def after(value, earlier):
    return value if earlier is None else lax.optimization_barrier((value, earlier))[0]


def all_hops():
    low_bits = lax.axis_size("sub").bit_length() - 1
    high_bits = lax.axis_size("bfly").bit_length() - 1
    return [("sub", bit) for bit in range(low_bits)] + [("bfly", bit) for bit in range(high_bits)]


def full_width(traces, sampling, skeleton, compress, evaluation):
    rank = skeleton.shape[-1]
    columns = picked_columns(compress, skeleton)
    full = jnp.concatenate([real_form(columns[..., :rank]), real_form(columns[..., rank:])], 2)
    coeffs = sampled_apart(sampling, traces)
    for level, hop in enumerate(all_hops()):
        partner = from_partner(coeffs, hop)
        coeffs = times(full[level], jnp.concatenate([coeffs, partner], 0))
    return evaluated(coeffs, evaluation)


def local(traces, sampling, skeleton, compress, evaluation):
    hops = all_hops()
    levels = len(hops)
    if (lax.axis_size("sub"), lax.axis_size("bfly")) != (2, 4):
        return full_width(traces, sampling[0], skeleton[0], compress[0], evaluation[0])
    wide = lax.axis_size("sub").bit_length() - 1
    rank = skeleton.shape[-1]
    rooms = [rank * share // 16 for share in ROOM_SIXTEENTHS]
    unit = traces.shape[0] // sum(SHARES)
    pieces = len(SHARES)
    starts = [unit * sum(SHARES[:i]) for i in range(pieces + 1)]
    coeffs = list(early(sampling, traces, starts[: EARLY_PIECES + 1]))
    full, small, extra = tables(after(skeleton, coeffs[0]), compress, wide, rooms)
    sampling, evaluation = sampling[0], evaluation[0]

    def compact(level, piece):
        return level >= wide and piece >= FULL_PIECES[level - wide]

    inputs, partners, theirs, done = {}, {}, {}, [None] * pieces
    previous, finished = None, None
    for level, piece in ORDER:
        if (level, piece) == TELL:
            told = from_partner(after(extra[levels - 1 - wide], previous), hops[levels - 1])
            continue
        if (level, piece) == LOOK:
            told = after(told, (previous, partners[1]))
            theirs[levels - 1] = told[: 2 * rooms[levels - 1 - wide]]
            continue
        if (level, piece) == MAKE:
            waiting = after(sampling, previous)
            coeffs.append(sampled(waiting, traces[starts[pieces - 2] : starts[pieces - 1]]))
            previous = coeffs[-1]
            continue
        count = starts[piece + 1] - starts[piece]
        if level == 0:
            if piece == len(coeffs):
                waiting = after(sampling, previous)
                coeffs.append(sampled(waiting, traces[starts[piece] : starts[piece + 1]]))
            own = coeffs[piece]
            if piece == pieces - 2:
                coeffs.append(sampled(waiting, traces[starts[piece + 1] : starts[piece + 2]]))
        else:
            arrived = after(partners[piece], previous)
            if level == levels:
                arrived = after(arrived, finished)
            elif piece == 0 and level - 1 >= wide:
                theirs[level - 1] = arrived[: 2 * rooms[level - 1 - wide], count:]
            value = jnp.concatenate([inputs[piece], arrived[:, :count]], 0)
            matrix = full[level - 1]
            if compact(level - 1, piece):
                value = jnp.pad(value, ((0, full.shape[2] - value.shape[0]), (0, 0)))
                matrix = small[level - 1 - wide]
            if level < levels and compact(level, piece):
                outgoing = times(times(theirs[level], matrix), value)
                own = times(after(matrix, outgoing), value)
            else:
                own = outgoing = times(matrix, value)
        if level == levels:
            done[piece] = finished = previous = evaluated(own, evaluation)
            if piece == COUNT_READ:
                most = jnp.maximum(most, after(counted, finished))
            continue
        if level == 0:
            outgoing = after(own, previous) if piece >= pieces - 2 else own
        if piece == 0 and wide <= level < levels - 1:
            outgoing = jnp.concatenate([outgoing, extra[level - wide]], 1)
        inputs[piece] = own
        partners[piece] = from_partner(outgoing, hops[level])
        previous = outgoing
        if level == levels - 1 and 0 <= piece - COUNT_PIECE < levels - 1:
            if piece == COUNT_PIECE:
                most = after(jnp.maximum(extra[levels - 1 - wide], told)[MOST_ROW : MOST_ROW + 8], outgoing)
            else:
                most = jnp.maximum(most, after(counted, outgoing))
            counted = from_partner(most, hops[piece - COUNT_PIECE])
    quick = jnp.concatenate(done, 0)
    return lax.cond(
        most[0, 0] > 0,
        lambda: full_width(traces, sampling, skeleton[0], compress[0], evaluation),
        lambda: quick,
    )


def solution(mesh):
    placed = (
        P(("shots", "tr"), ("bfly", "sub")),
        P(("bfly", "sub"), None, None),
        P(("bfly", "sub"), None, None),
        P(("bfly", "sub"), None, None, None),
        P(("bfly", "sub"), None, None),
    )
    return jax.shard_map(
        local,
        mesh=mesh,
        in_specs=placed,
        out_specs=P(("shots", "tr"), ("bfly", "sub")),
        check_vma=False,
    )
```

```python
import jax
import jax.numpy as jnp
from jax import lax
from jax.experimental import pallas as pl
from jax.experimental.pallas import tpu as pltpu
from jax.sharding import PartitionSpec as P

SHARES = (2, 5, 9, 9, 7)
FULL_PIECES = (2, 1)
EARLY_PIECES = 2
COUNT_PIECE = 2
COUNT_READ = 2
LOOK = (3, -1)
MAKE = (0, -1)
ORDER = (
    (0, 0), (0, 1), (0, 2), (1, 0), (1, 1), MAKE, (2, 0), (0, 3), (1, 2), LOOK, (2, 1), (1, 3), (2, 2),
    (0, 4), (3, 0), (1, 4), (2, 3), (3, 1), (2, 4), (3, 2), (3, 3), (3, 4),
)
KERNEL_VMEM = 16 * 1024 * 1024
ROOM_SIXTEENTHS = (11, 10)


def route(axis, apart):
    count = lax.axis_size(axis)
    pairs = []
    for low in range(count):
        high = low | 1 << apart
        if high != low and high < count:
            pairs += [(low, high), (high, low)]
    return pairs


def from_partner(block, hop):
    return lax.ppermute(block, hop[0], route(*hop))


def across(left, right):
    return lax.dot_general(left, right, (((1,), (1,)), ((), ())), preferred_element_type=jnp.float32)


def one_hot(condition):
    return jnp.where(condition, 1.0, 0.0).astype(jnp.bfloat16)


def sampled_block(sampling, rows):
    turned = sampling.astype(jnp.float32).T.astype(jnp.bfloat16)
    return across(turned, rows).astype(jnp.bfloat16)


def early_kernel(starts, sampling_hbm, traces_hbm, *refs):
    pieces = len(starts) - 1
    outs, (sampling_ref, rows_ref, arrived) = refs[:pieces], refs[pieces:]
    loads = [pltpu.make_async_copy(sampling_hbm, sampling_ref, arrived.at[pieces])]
    for i in range(pieces):
        span = pl.ds(starts[i], starts[i + 1] - starts[i])
        loads.append(pltpu.make_async_copy(traces_hbm.at[span], rows_ref.at[span], arrived.at[i]))
    for load in loads:
        load.start()
    loads[0].wait()
    for i in range(pieces):
        loads[i + 1].wait()
        span = pl.ds(starts[i], starts[i + 1] - starts[i])
        outs[i][...] = sampled_block(sampling_ref[0], rows_ref[span])


def early(sampling, traces, starts):
    pieces = len(starts) - 1
    width = sampling.shape[-1]
    total = starts[-1]
    return pl.pallas_call(
        lambda *refs: early_kernel(starts, *refs),
        out_shape=[
            jax.ShapeDtypeStruct((width, starts[i + 1] - starts[i]), jnp.bfloat16) for i in range(pieces)
        ],
        in_specs=[pl.BlockSpec(memory_space=pltpu.HBM)] * 2,
        out_specs=[pl.BlockSpec(memory_space=pltpu.VMEM)] * pieces,
        scratch_shapes=[
            pltpu.VMEM(sampling.shape, jnp.bfloat16),
            pltpu.VMEM((total, traces.shape[1]), jnp.bfloat16),
            pltpu.SemaphoreType.DMA((pieces + 1,)),
        ],
        compiler_params=pltpu.CompilerParams(vmem_limit_bytes=KERNEL_VMEM),
        cost_estimate=pl.CostEstimate(
            flops=2 * total * width * width, bytes_accessed=4 * total * width, transcendentals=0
        ),
        name="early",
    )(sampling, traces)


def tables_kernel(
    wide, rooms, skeleton_hbm, compress_hbm, full_ref, small_ref, extra_ref,
    skeleton_ref, compress_ref, arrived,
):
    loads = [
        pltpu.make_async_copy(skeleton_hbm, skeleton_ref, arrived.at[0]),
        pltpu.make_async_copy(compress_hbm, compress_ref, arrived.at[1]),
    ]
    for load in loads:
        load.start()
    for load in loads:
        load.wait()
    levels, rank = skeleton_ref.shape[0], skeleton_ref.shape[-1]
    width = 2 * rank
    f32, i32 = jnp.float32, jnp.int32
    k = lax.broadcasted_iota(i32, (width, width), 1)
    twice = one_hot(lax.broadcasted_iota(i32, (width, rank), 0) % rank == lax.broadcasted_iota(i32, (width, rank), 1))
    earlier = one_hot(
        (lax.broadcasted_iota(i32, (width, width), 1) < lax.broadcasted_iota(i32, (width, width), 0) % rank)
    )
    column = lax.broadcasted_iota(i32, (2 * width, width), 0)
    is_real_entry = lax.broadcasted_iota(i32, (2 * width, width), 1) < rank
    partner_column = column >= width
    imag_column = column % width >= rank
    coefficient = column % rank + jnp.where(partner_column, rank, 0)
    slot_column = column - width
    row = lax.broadcasted_iota(i32, (width, width), 0)
    most = jnp.full((1, 1), -float(rank), f32)
    for level in range(levels):
        entry = jnp.broadcast_to(skeleton_ref[level].astype(f32), (8, rank)).astype(jnp.bfloat16)
        entry = across(entry, twice)[:1]
        picked = jnp.where(entry >= rank, 1.0, 0.0)
        slot = across(jnp.broadcast_to(picked, (8, width)).astype(jnp.bfloat16), earlier)[:1].astype(i32)
        entry = entry.astype(i32)
        from_partner_entry = entry >= rank
        matrix = compress_ref[0, level]

        def halves(match, imag):
            same = is_real_entry != imag
            real = jnp.where(match & same, jnp.where(imag, -1.0, 1.0), 0.0).astype(jnp.bfloat16)
            turned = one_hot(match & jnp.logical_not(same))
            return across(matrix, real).astype(jnp.bfloat16), across(matrix, turned).astype(jnp.bfloat16)

        match = entry == coefficient
        full_ref[level, :rank], full_ref[level, rank:] = halves(match, imag_column)
        if level < wide:
            continue
        high = level - wide
        room = rooms[high]
        slot_imag = slot_column >= room
        slot_of_column = jnp.where(slot_imag, slot_column - room, slot_column)
        compacted = (slot == slot_of_column) & from_partner_entry
        match = (match & jnp.logical_not(partner_column)) | (compacted & partner_column)
        imag = (imag_column & jnp.logical_not(partner_column)) | (slot_imag & partner_column)
        small_ref[high, :rank], small_ref[high, rank:] = halves(match, imag)
        once = (k < rank) & from_partner_entry
        places = across(one_hot(once & (slot == row)), one_hot(once & (entry - rank == row)))
        extra_ref[high] = places.astype(jnp.bfloat16)
        most = jnp.maximum(most, jnp.sum(picked, axis=1, keepdims=True) * 0.5 - room)
    for high in range(levels - wide):
        extra_ref[high] = jnp.where(k < rank, extra_ref[high].astype(f32), most).astype(jnp.bfloat16)


def tables(skeleton, compress, wide, rooms):
    levels, rank = skeleton.shape[1:]
    shape = (levels, 2 * rank, 4 * rank)
    return pl.pallas_call(
        lambda *refs: tables_kernel(wide, rooms, *refs),
        out_shape=[
            jax.ShapeDtypeStruct(shape, jnp.bfloat16),
            jax.ShapeDtypeStruct((levels - wide,) + shape[1:], jnp.bfloat16),
            jax.ShapeDtypeStruct((levels - wide, 2 * rank, 2 * rank), jnp.bfloat16),
        ],
        in_specs=[pl.BlockSpec(memory_space=pltpu.HBM)] * 2,
        out_specs=[pl.BlockSpec(memory_space=pltpu.VMEM)] * 3,
        scratch_shapes=[
            pltpu.VMEM((levels, 1, rank), jnp.int32),
            pltpu.VMEM(compress.shape, jnp.bfloat16),
            pltpu.SemaphoreType.DMA((2,)),
        ],
        compiler_params=pltpu.CompilerParams(vmem_limit_bytes=KERNEL_VMEM),
        cost_estimate=pl.CostEstimate(flops=50_000_000, bytes_accessed=600_000, transcendentals=0),
        name="tables",
    )(skeleton.transpose(1, 0, 2), compress)


def sampled_apart(sampling, traces):
    count, width = traces.shape
    block = count // 8

    def kernel(sampling_ref, rows_ref, coeffs_ref):
        coeffs_ref[...] = sampled_block(sampling_ref[...], rows_ref[...])

    return pl.pallas_call(
        kernel,
        grid=(count // block,),
        out_shape=jax.ShapeDtypeStruct((sampling.shape[1], count), jnp.bfloat16),
        in_specs=[
            pl.BlockSpec(sampling.shape, lambda i: (0, 0)),
            pl.BlockSpec((block, width), lambda i: (i, 0)),
        ],
        out_specs=pl.BlockSpec((sampling.shape[1], block), lambda i: (0, i)),
        compiler_params=pltpu.CompilerParams(vmem_limit_bytes=63 * 1024 * 1024),
        name="sampled_apart",
    )(sampling, traces)


def picked_columns(compress, skeleton):
    rank = skeleton.shape[-1]
    places = lax.broadcasted_iota(jnp.int32, (1, 1, 2 * rank), 2)
    chooser = (skeleton[:, :, None] == places).astype(jnp.bfloat16)
    stacked = jnp.concatenate([compress[:, :, :rank], compress[:, :, rank:]], 1)
    return jnp.einsum(
        "ljk,lki->lji", stacked, chooser, preferred_element_type=jnp.float32
    ).astype(jnp.bfloat16)


def real_form(both):
    rank = both.shape[1] // 2
    turned = jnp.concatenate([-both[:, rank:], both[:, :rank]], 1)
    return jnp.concatenate([both, turned], 2)


def compact_rows(matrix, slot):
    rank = slot.shape[1]
    parts = [
        jnp.dot(slot, half, preferred_element_type=jnp.float32)
        for half in (matrix[:rank], matrix[rank:])
    ]
    return jnp.concatenate(parts, 0).astype(jnp.bfloat16)


def times(matrix, value):
    return jnp.dot(matrix, value, preferred_element_type=jnp.float32).astype(jnp.bfloat16)


def sampled(sampling, traces):
    return jnp.einsum(
        "pc,tp->ct", sampling, traces, preferred_element_type=jnp.float32
    ).astype(jnp.bfloat16)


def evaluated(coeffs, evaluation):
    return jnp.einsum(
        "ct,cp->tp", coeffs, evaluation, preferred_element_type=jnp.float32
    ).astype(jnp.bfloat16)


def after(value, earlier):
    return value if earlier is None else lax.optimization_barrier((value, earlier))[0]


def all_hops():
    low_bits = lax.axis_size("sub").bit_length() - 1
    high_bits = lax.axis_size("bfly").bit_length() - 1
    return [("sub", bit) for bit in range(low_bits)] + [("bfly", bit) for bit in range(high_bits)]


def full_width(traces, sampling, skeleton, compress, evaluation):
    rank = skeleton.shape[-1]
    columns = picked_columns(compress, skeleton)
    full = jnp.concatenate([real_form(columns[..., :rank]), real_form(columns[..., rank:])], 2)
    coeffs = sampled_apart(sampling, traces)
    for level, hop in enumerate(all_hops()):
        partner = from_partner(coeffs, hop)
        coeffs = times(full[level], jnp.concatenate([coeffs, partner], 0))
    return evaluated(coeffs, evaluation)


def local(traces, sampling, skeleton, compress, evaluation):
    hops = all_hops()
    levels = len(hops)
    if (lax.axis_size("sub"), lax.axis_size("bfly")) != (2, 4):
        return full_width(traces, sampling[0], skeleton[0], compress[0], evaluation[0])
    wide = lax.axis_size("sub").bit_length() - 1
    rank = skeleton.shape[-1]
    rooms = [rank * share // 16 for share in ROOM_SIXTEENTHS]
    unit = traces.shape[0] // sum(SHARES)
    pieces = len(SHARES)
    starts = [unit * sum(SHARES[:i]) for i in range(pieces + 1)]
    coeffs = list(early(sampling, traces, starts[: EARLY_PIECES + 1]))
    full, small, extra = tables(after(skeleton, coeffs[0]), compress, wide, rooms)
    sampling, evaluation = sampling[0], evaluation[0]
    most_here = lax.broadcasted_iota(jnp.int32, extra.shape[1:], 1) >= rank

    def compact(level, piece):
        return level >= wide and piece >= FULL_PIECES[level - wide]

    inputs, partners, theirs, done = {}, {}, {}, [None] * pieces
    previous, finished, known = None, None, None
    for level, piece in ORDER:
        if (level, piece) == MAKE:
            waiting = after(sampling, previous)
            coeffs.append(sampled(waiting, traces[starts[pieces - 2] : starts[pieces - 1]]))
            previous = coeffs[-1]
            continue
        if (level, piece) == LOOK:
            known = after(after(partners[0], previous), partners[1])[:, starts[1] :]
            theirs[levels - 1] = known[: rooms[levels - 1 - wide], :rank]
            continue
        count = starts[piece + 1] - starts[piece]
        if level == 0:
            if piece == len(coeffs):
                waiting = after(sampling, previous)
                coeffs.append(sampled(waiting, traces[starts[piece] : starts[piece + 1]]))
            own = coeffs[piece]
            if piece == pieces - 2:
                coeffs.append(sampled(waiting, traces[starts[piece + 1] : starts[piece + 2]]))
        else:
            arrived = after(partners[piece], previous)
            if level == levels:
                arrived = after(arrived, finished)
            elif piece == 0 and level - 1 >= wide:
                known = arrived[:, count:]
                theirs[level - 1] = known[: rooms[level - 1 - wide], :rank]
            value = jnp.concatenate([inputs[piece], arrived[:, :count]], 0)
            matrix = full[level - 1]
            if compact(level - 1, piece):
                value = jnp.pad(value, ((0, full.shape[2] - value.shape[0]), (0, 0)))
                matrix = small[level - 1 - wide]
            if level < levels and compact(level, piece):
                outgoing = times(compact_rows(matrix, theirs[level]), value)
                own = times(after(matrix, outgoing), value)
            else:
                own = outgoing = times(matrix, value)
        if level == levels:
            done[piece] = finished = previous = evaluated(own, evaluation)
            if piece == COUNT_READ:
                most = jnp.maximum(most, after(counted, finished))
            continue
        if level == 0:
            outgoing = after(own, previous) if piece >= pieces - 2 else own
        if piece == 0 and level >= wide:
            block = extra[level - wide]
            if known is not None:
                block = jnp.where(most_here, jnp.maximum(block, known), block)
            so_far = block
            outgoing = jnp.concatenate([outgoing, block], 1)
        inputs[piece] = own
        partners[piece] = from_partner(outgoing, hops[level])
        previous = outgoing
        if (level, piece) == (levels - 1, COUNT_PIECE):
            most = after(jnp.maximum(so_far, known)[:8, rank:], outgoing)
            for hop in hops[: wide - 1]:
                most = jnp.maximum(most, from_partner(most, hop))
            counted = from_partner(most, hops[wide - 1])
    quick = jnp.concatenate(done, 0)
    return lax.cond(
        most[0, 0] > 0,
        lambda: full_width(traces, sampling, skeleton[0], compress[0], evaluation),
        lambda: quick,
    )


def solution(mesh):
    placed = (
        P(("shots", "tr"), ("bfly", "sub")),
        P(("bfly", "sub"), None, None),
        P(("bfly", "sub"), None, None),
        P(("bfly", "sub"), None, None, None),
        P(("bfly", "sub"), None, None),
    )
    return jax.shard_map(
        local,
        mesh=mesh,
        in_specs=placed,
        out_specs=P(("shots", "tr"), ("bfly", "sub")),
        check_vma=False,
    )
```

```python
import jax
import jax.numpy as jnp
from jax import lax
from jax.experimental import pallas as pl
from jax.experimental.pallas import tpu as pltpu
from jax.sharding import PartitionSpec as P

SHARES = (2, 5, 9, 9, 7)
FULL_PIECES = (2, 1)
EARLY_PIECES = 2
COUNT_PIECE = 2
COUNT_READ = 2
LOOK = (3, -1)
MAKE = (0, -1)
LATE = (1, 2)
ORDER = (
    (0, 0), (0, 1), (0, 2), (1, 0), (1, 1), MAKE, (2, 0), (0, 3), (1, 2), LOOK, (2, 1), (1, 3), (2, 2),
    (0, 4), (3, 0), (1, 4), (2, 3), (3, 1), (2, 4), (3, 2), (3, 3), (3, 4),
)
KERNEL_VMEM = 16 * 1024 * 1024
ROOM_SIXTEENTHS = (11, 10)


def route(axis, apart):
    count = lax.axis_size(axis)
    pairs = []
    for low in range(count):
        high = low | 1 << apart
        if high != low and high < count:
            pairs += [(low, high), (high, low)]
    return pairs


def from_partner(block, hop):
    return lax.ppermute(block, hop[0], route(*hop))


def across(left, right):
    return lax.dot_general(left, right, (((1,), (1,)), ((), ())), preferred_element_type=jnp.float32)


def one_hot(condition):
    return jnp.where(condition, 1.0, 0.0).astype(jnp.bfloat16)


def sampled_block(sampling, rows):
    turned = sampling.astype(jnp.float32).T.astype(jnp.bfloat16)
    return across(turned, rows).astype(jnp.bfloat16)


def early_kernel(starts, sampling_hbm, traces_hbm, *refs):
    pieces = len(starts) - 1
    outs, (sampling_ref, rows_ref, arrived) = refs[:pieces], refs[pieces:]
    loads = [pltpu.make_async_copy(sampling_hbm, sampling_ref, arrived.at[pieces])]
    for i in range(pieces):
        span = pl.ds(starts[i], starts[i + 1] - starts[i])
        loads.append(pltpu.make_async_copy(traces_hbm.at[span], rows_ref.at[span], arrived.at[i]))
    for load in loads:
        load.start()
    loads[0].wait()
    for i in range(pieces):
        loads[i + 1].wait()
        span = pl.ds(starts[i], starts[i + 1] - starts[i])
        outs[i][...] = sampled_block(sampling_ref[0], rows_ref[span])


def early(sampling, traces, starts):
    pieces = len(starts) - 1
    width = sampling.shape[-1]
    total = starts[-1]
    return pl.pallas_call(
        lambda *refs: early_kernel(starts, *refs),
        out_shape=[
            jax.ShapeDtypeStruct((width, starts[i + 1] - starts[i]), jnp.bfloat16) for i in range(pieces)
        ],
        in_specs=[pl.BlockSpec(memory_space=pltpu.HBM)] * 2,
        out_specs=[pl.BlockSpec(memory_space=pltpu.VMEM)] * pieces,
        scratch_shapes=[
            pltpu.VMEM(sampling.shape, jnp.bfloat16),
            pltpu.VMEM((total, traces.shape[1]), jnp.bfloat16),
            pltpu.SemaphoreType.DMA((pieces + 1,)),
        ],
        compiler_params=pltpu.CompilerParams(vmem_limit_bytes=KERNEL_VMEM),
        cost_estimate=pl.CostEstimate(
            flops=2 * total * width * width, bytes_accessed=4 * total * width, transcendentals=0
        ),
        name="early",
    )(sampling, traces)


def tables_kernel(
    wide, rooms, skeleton_hbm, compress_hbm, full_ref, small_ref, extra_ref,
    skeleton_ref, compress_ref, arrived,
):
    loads = [
        pltpu.make_async_copy(skeleton_hbm, skeleton_ref, arrived.at[0]),
        pltpu.make_async_copy(compress_hbm, compress_ref, arrived.at[1]),
    ]
    for load in loads:
        load.start()
    for load in loads:
        load.wait()
    levels, rank = skeleton_ref.shape[0], skeleton_ref.shape[-1]
    width = 2 * rank
    f32, i32 = jnp.float32, jnp.int32
    k = lax.broadcasted_iota(i32, (width, width), 1)
    twice = one_hot(lax.broadcasted_iota(i32, (width, rank), 0) % rank == lax.broadcasted_iota(i32, (width, rank), 1))
    earlier = one_hot(
        (lax.broadcasted_iota(i32, (width, width), 1) < lax.broadcasted_iota(i32, (width, width), 0) % rank)
    )
    column = lax.broadcasted_iota(i32, (2 * width, width), 0)
    is_real_entry = lax.broadcasted_iota(i32, (2 * width, width), 1) < rank
    partner_column = column >= width
    imag_column = column % width >= rank
    coefficient = column % rank + jnp.where(partner_column, rank, 0)
    slot_column = column - width
    row = lax.broadcasted_iota(i32, (width, width), 0)
    most = jnp.full((1, 1), -float(rank), f32)
    for level in range(levels):
        entry = jnp.broadcast_to(skeleton_ref[level].astype(f32), (8, rank)).astype(jnp.bfloat16)
        entry = across(entry, twice)[:1]
        picked = jnp.where(entry >= rank, 1.0, 0.0)
        slot = across(jnp.broadcast_to(picked, (8, width)).astype(jnp.bfloat16), earlier)[:1].astype(i32)
        entry = entry.astype(i32)
        from_partner_entry = entry >= rank
        matrix = compress_ref[0, level]

        def halves(match, imag):
            same = is_real_entry != imag
            real = jnp.where(match & same, jnp.where(imag, -1.0, 1.0), 0.0).astype(jnp.bfloat16)
            turned = one_hot(match & jnp.logical_not(same))
            return across(matrix, real).astype(jnp.bfloat16), across(matrix, turned).astype(jnp.bfloat16)

        match = entry == coefficient
        full_ref[level, :rank], full_ref[level, rank:] = halves(match, imag_column)
        if level < wide:
            continue
        high = level - wide
        room = rooms[high]
        slot_imag = slot_column >= room
        slot_of_column = jnp.where(slot_imag, slot_column - room, slot_column)
        compacted = (slot == slot_of_column) & from_partner_entry
        match = (match & jnp.logical_not(partner_column)) | (compacted & partner_column)
        imag = (imag_column & jnp.logical_not(partner_column)) | (slot_imag & partner_column)
        small_ref[high, :rank], small_ref[high, rank:] = halves(match, imag)
        once = (k < rank) & from_partner_entry
        places = across(one_hot(once & (slot == row)), one_hot(once & (entry - rank == row)))
        extra_ref[high] = places.astype(jnp.bfloat16)
        most = jnp.maximum(most, jnp.sum(picked, axis=1, keepdims=True) * 0.5 - room)
    for high in range(levels - wide):
        extra_ref[high] = jnp.where(k < rank, extra_ref[high].astype(f32), most).astype(jnp.bfloat16)


def tables(skeleton, compress, wide, rooms):
    levels, rank = skeleton.shape[1:]
    shape = (levels, 2 * rank, 4 * rank)
    return pl.pallas_call(
        lambda *refs: tables_kernel(wide, rooms, *refs),
        out_shape=[
            jax.ShapeDtypeStruct(shape, jnp.bfloat16),
            jax.ShapeDtypeStruct((levels - wide,) + shape[1:], jnp.bfloat16),
            jax.ShapeDtypeStruct((levels - wide, 2 * rank, 2 * rank), jnp.bfloat16),
        ],
        in_specs=[pl.BlockSpec(memory_space=pltpu.HBM)] * 2,
        out_specs=[pl.BlockSpec(memory_space=pltpu.VMEM)] * 3,
        scratch_shapes=[
            pltpu.VMEM((levels, 1, rank), jnp.int32),
            pltpu.VMEM(compress.shape, jnp.bfloat16),
            pltpu.SemaphoreType.DMA((2,)),
        ],
        compiler_params=pltpu.CompilerParams(vmem_limit_bytes=KERNEL_VMEM),
        cost_estimate=pl.CostEstimate(flops=50_000_000, bytes_accessed=600_000, transcendentals=0),
        name="tables",
    )(skeleton.transpose(1, 0, 2), compress)


def sampled_apart(sampling, traces):
    count, width = traces.shape
    block = count // 8

    def kernel(sampling_ref, rows_ref, coeffs_ref):
        coeffs_ref[...] = sampled_block(sampling_ref[...], rows_ref[...])

    return pl.pallas_call(
        kernel,
        grid=(count // block,),
        out_shape=jax.ShapeDtypeStruct((sampling.shape[1], count), jnp.bfloat16),
        in_specs=[
            pl.BlockSpec(sampling.shape, lambda i: (0, 0)),
            pl.BlockSpec((block, width), lambda i: (i, 0)),
        ],
        out_specs=pl.BlockSpec((sampling.shape[1], block), lambda i: (0, i)),
        compiler_params=pltpu.CompilerParams(vmem_limit_bytes=63 * 1024 * 1024),
        name="sampled_apart",
    )(sampling, traces)


def picked_columns(compress, skeleton):
    rank = skeleton.shape[-1]
    places = lax.broadcasted_iota(jnp.int32, (1, 1, 2 * rank), 2)
    chooser = (skeleton[:, :, None] == places).astype(jnp.bfloat16)
    stacked = jnp.concatenate([compress[:, :, :rank], compress[:, :, rank:]], 1)
    return jnp.einsum(
        "ljk,lki->lji", stacked, chooser, preferred_element_type=jnp.float32
    ).astype(jnp.bfloat16)


def real_form(both):
    rank = both.shape[1] // 2
    turned = jnp.concatenate([-both[:, rank:], both[:, :rank]], 1)
    return jnp.concatenate([both, turned], 2)


def compact_rows(matrix, slot):
    rank = slot.shape[1]
    parts = [
        jnp.dot(slot, half, preferred_element_type=jnp.float32)
        for half in (matrix[:rank], matrix[rank:])
    ]
    return jnp.concatenate(parts, 0).astype(jnp.bfloat16)


def times(matrix, value):
    return jnp.dot(matrix, value, preferred_element_type=jnp.float32).astype(jnp.bfloat16)


def sampled(sampling, traces):
    return jnp.einsum(
        "pc,tp->ct", sampling, traces, preferred_element_type=jnp.float32
    ).astype(jnp.bfloat16)


def evaluated(coeffs, evaluation):
    return jnp.einsum(
        "ct,cp->tp", coeffs, evaluation, preferred_element_type=jnp.float32
    ).astype(jnp.bfloat16)


def after(value, earlier):
    return value if earlier is None else lax.optimization_barrier((value, earlier))[0]


def all_hops():
    low_bits = lax.axis_size("sub").bit_length() - 1
    high_bits = lax.axis_size("bfly").bit_length() - 1
    return [("sub", bit) for bit in range(low_bits)] + [("bfly", bit) for bit in range(high_bits)]


def full_width(traces, sampling, skeleton, compress, evaluation):
    rank = skeleton.shape[-1]
    columns = picked_columns(compress, skeleton)
    full = jnp.concatenate([real_form(columns[..., :rank]), real_form(columns[..., rank:])], 2)
    coeffs = sampled_apart(sampling, traces)
    for level, hop in enumerate(all_hops()):
        partner = from_partner(coeffs, hop)
        coeffs = times(full[level], jnp.concatenate([coeffs, partner], 0))
    return evaluated(coeffs, evaluation)


def local(traces, sampling, skeleton, compress, evaluation):
    hops = all_hops()
    levels = len(hops)
    if (lax.axis_size("sub"), lax.axis_size("bfly")) != (2, 4):
        return full_width(traces, sampling[0], skeleton[0], compress[0], evaluation[0])
    wide = lax.axis_size("sub").bit_length() - 1
    rank = skeleton.shape[-1]
    rooms = [rank * share // 16 for share in ROOM_SIXTEENTHS]
    unit = traces.shape[0] // sum(SHARES)
    pieces = len(SHARES)
    starts = [unit * sum(SHARES[:i]) for i in range(pieces + 1)]
    coeffs = list(early(sampling, traces, starts[: EARLY_PIECES + 1]))
    full, small, extra = tables(after(skeleton, coeffs[0]), compress, wide, rooms)
    sampling, evaluation = sampling[0], evaluation[0]
    most_here = lax.broadcasted_iota(jnp.int32, extra.shape[1:], 1) >= rank

    def compact(level, piece):
        return level >= wide and piece >= FULL_PIECES[level - wide]

    inputs, partners, theirs, done = {}, {}, {}, [None] * pieces
    previous, finished, known, kept = None, None, None, None
    for level, piece in ORDER:
        if (level, piece) == MAKE:
            waiting = after(sampling, previous)
            coeffs.append(sampled(waiting, traces[starts[pieces - 2] : starts[pieces - 1]]))
            previous = coeffs[-1]
            continue
        if (level, piece) == LOOK:
            known = after(after(partners[0], previous), partners[1])[:, starts[1] :]
            theirs[levels - 1] = known[: rooms[levels - 1 - wide], :rank]
            continue
        count = starts[piece + 1] - starts[piece]
        if level == 0:
            if piece == len(coeffs):
                waiting = after(sampling, previous)
                coeffs.append(sampled(waiting, traces[starts[piece] : starts[piece + 1]]))
            own = coeffs[piece]
            if piece == pieces - 2:
                coeffs.append(sampled(waiting, traces[starts[piece + 1] : starts[piece + 2]]))
        else:
            arrived = after(partners[piece], previous)
            if level == levels:
                arrived = after(arrived, finished)
            elif piece == 0 and level - 1 >= wide:
                known = arrived[:, count:]
                theirs[level - 1] = known[: rooms[level - 1 - wide], :rank]
            value = jnp.concatenate([inputs[piece], arrived[:, :count]], 0)
            matrix = full[level - 1]
            if compact(level - 1, piece):
                value = jnp.pad(value, ((0, full.shape[2] - value.shape[0]), (0, 0)))
                matrix = small[level - 1 - wide]
            if level < levels and compact(level, piece):
                outgoing = times(compact_rows(matrix, theirs[level]), value)
                if (level, piece) == LATE:
                    own, kept = None, (matrix, value)
                else:
                    own = times(after(matrix, outgoing), value)
            else:
                own = outgoing = times(matrix, value)
        if level == levels:
            done[piece] = finished = previous = evaluated(own, evaluation)
            if piece == COUNT_READ:
                most = jnp.maximum(most, after(counted, finished))
            continue
        if level == 0:
            outgoing = after(own, previous) if piece >= pieces - 2 else own
        if piece == 0 and level >= wide:
            block = extra[level - wide]
            if known is not None:
                block = jnp.where(most_here, jnp.maximum(block, known), block)
            so_far = block
            outgoing = jnp.concatenate([outgoing, block], 1)
        if kept is not None and own is not None:
            inputs[LATE[1]], kept = times(after(kept[0], outgoing), kept[1]), None
        inputs[piece] = own
        partners[piece] = from_partner(outgoing, hops[level])
        previous = outgoing
        if (level, piece) == (levels - 1, COUNT_PIECE):
            most = after(jnp.maximum(so_far, known)[:8, rank:], outgoing)
            for hop in hops[: wide - 1]:
                most = jnp.maximum(most, from_partner(most, hop))
            counted = from_partner(most, hops[wide - 1])
    quick = jnp.concatenate(done, 0)
    return lax.cond(
        most[0, 0] > 0,
        lambda: full_width(traces, sampling, skeleton[0], compress[0], evaluation),
        lambda: quick,
    )


def solution(mesh):
    placed = (
        P(("shots", "tr"), ("bfly", "sub")),
        P(("bfly", "sub"), None, None),
        P(("bfly", "sub"), None, None),
        P(("bfly", "sub"), None, None, None),
        P(("bfly", "sub"), None, None),
    )
    return jax.shard_map(
        local,
        mesh=mesh,
        in_specs=placed,
        out_specs=P(("shots", "tr"), ("bfly", "sub")),
        check_vma=False,
    )
```

```python
import jax
import jax.numpy as jnp
from jax import lax
from jax.experimental import pallas as pl
from jax.experimental.pallas import tpu as pltpu
from jax.sharding import PartitionSpec as P

SHARES = (2, 5, 8, 10, 7)
FULL_PIECES = (2, 1)
EARLY_PIECES = 2
COUNT_PIECE = 2
COUNT_READ = 2
LOOK = (3, -1)
MAKE = (0, -1)
ORDER = (
    (0, 0), (0, 1), (0, 2), (1, 0), (1, 1), MAKE, (2, 0), (0, 3), (1, 2), LOOK, (2, 1), (1, 3), (2, 2),
    (0, 4), (3, 0), (1, 4), (2, 3), (3, 1), (2, 4), (3, 2), (3, 3), (3, 4),
)
KERNEL_VMEM = 16 * 1024 * 1024
ROOM_SIXTEENTHS = (11, 10)


def route(axis, apart):
    count = lax.axis_size(axis)
    pairs = []
    for low in range(count):
        high = low | 1 << apart
        if high != low and high < count:
            pairs += [(low, high), (high, low)]
    return pairs


def from_partner(block, hop):
    return lax.ppermute(block, hop[0], route(*hop))


def across(left, right):
    return lax.dot_general(left, right, (((1,), (1,)), ((), ())), preferred_element_type=jnp.float32)


def one_hot(condition):
    return jnp.where(condition, 1.0, 0.0).astype(jnp.bfloat16)


def sampled_block(sampling, rows):
    turned = sampling.astype(jnp.float32).T.astype(jnp.bfloat16)
    return across(turned, rows).astype(jnp.bfloat16)


def early_kernel(starts, sampling_hbm, traces_hbm, *refs):
    pieces = len(starts) - 1
    outs, (sampling_ref, rows_ref, arrived) = refs[:pieces], refs[pieces:]
    loads = [pltpu.make_async_copy(sampling_hbm, sampling_ref, arrived.at[pieces])]
    for i in range(pieces):
        span = pl.ds(starts[i], starts[i + 1] - starts[i])
        loads.append(pltpu.make_async_copy(traces_hbm.at[span], rows_ref.at[span], arrived.at[i]))
    for load in loads:
        load.start()
    loads[0].wait()
    for i in range(pieces):
        loads[i + 1].wait()
        span = pl.ds(starts[i], starts[i + 1] - starts[i])
        outs[i][...] = sampled_block(sampling_ref[0], rows_ref[span])


def early(sampling, traces, starts):
    pieces = len(starts) - 1
    width = sampling.shape[-1]
    total = starts[-1]
    return pl.pallas_call(
        lambda *refs: early_kernel(starts, *refs),
        out_shape=[
            jax.ShapeDtypeStruct((width, starts[i + 1] - starts[i]), jnp.bfloat16) for i in range(pieces)
        ],
        in_specs=[pl.BlockSpec(memory_space=pltpu.HBM)] * 2,
        out_specs=[pl.BlockSpec(memory_space=pltpu.VMEM)] * pieces,
        scratch_shapes=[
            pltpu.VMEM(sampling.shape, jnp.bfloat16),
            pltpu.VMEM((total, traces.shape[1]), jnp.bfloat16),
            pltpu.SemaphoreType.DMA((pieces + 1,)),
        ],
        compiler_params=pltpu.CompilerParams(vmem_limit_bytes=KERNEL_VMEM),
        cost_estimate=pl.CostEstimate(
            flops=2 * total * width * width, bytes_accessed=4 * total * width, transcendentals=0
        ),
        name="early",
    )(sampling, traces)


def tables_kernel(
    wide, rooms, skeleton_hbm, compress_hbm, full_ref, small_ref, extra_ref,
    skeleton_ref, compress_ref, arrived,
):
    loads = [
        pltpu.make_async_copy(skeleton_hbm, skeleton_ref, arrived.at[0]),
        pltpu.make_async_copy(compress_hbm, compress_ref, arrived.at[1]),
    ]
    for load in loads:
        load.start()
    for load in loads:
        load.wait()
    levels, rank = skeleton_ref.shape[0], skeleton_ref.shape[-1]
    width = 2 * rank
    f32, i32 = jnp.float32, jnp.int32
    k = lax.broadcasted_iota(i32, (width, width), 1)
    twice = one_hot(lax.broadcasted_iota(i32, (width, rank), 0) % rank == lax.broadcasted_iota(i32, (width, rank), 1))
    earlier = one_hot(
        (lax.broadcasted_iota(i32, (width, width), 1) < lax.broadcasted_iota(i32, (width, width), 0) % rank)
    )
    column = lax.broadcasted_iota(i32, (2 * width, width), 0)
    is_real_entry = lax.broadcasted_iota(i32, (2 * width, width), 1) < rank
    partner_column = column >= width
    imag_column = column % width >= rank
    coefficient = column % rank + jnp.where(partner_column, rank, 0)
    slot_column = column - width
    row = lax.broadcasted_iota(i32, (width, width), 0)
    most = jnp.full((1, 1), -float(rank), f32)
    for level in range(levels):
        entry = jnp.broadcast_to(skeleton_ref[level].astype(f32), (8, rank)).astype(jnp.bfloat16)
        entry = across(entry, twice)[:1]
        picked = jnp.where(entry >= rank, 1.0, 0.0)
        slot = across(jnp.broadcast_to(picked, (8, width)).astype(jnp.bfloat16), earlier)[:1].astype(i32)
        entry = entry.astype(i32)
        from_partner_entry = entry >= rank
        matrix = compress_ref[0, level]

        def halves(match, imag):
            same = is_real_entry != imag
            real = jnp.where(match & same, jnp.where(imag, -1.0, 1.0), 0.0).astype(jnp.bfloat16)
            turned = one_hot(match & jnp.logical_not(same))
            return across(matrix, real).astype(jnp.bfloat16), across(matrix, turned).astype(jnp.bfloat16)

        match = entry == coefficient
        full_ref[level, :rank], full_ref[level, rank:] = halves(match, imag_column)
        if level < wide:
            continue
        high = level - wide
        room = rooms[high]
        slot_imag = slot_column >= room
        slot_of_column = jnp.where(slot_imag, slot_column - room, slot_column)
        compacted = (slot == slot_of_column) & from_partner_entry
        match = (match & jnp.logical_not(partner_column)) | (compacted & partner_column)
        imag = (imag_column & jnp.logical_not(partner_column)) | (slot_imag & partner_column)
        small_ref[high, :rank], small_ref[high, rank:] = halves(match, imag)
        once = (k < rank) & from_partner_entry
        places = across(one_hot(once & (slot == row)), one_hot(once & (entry - rank == row)))
        extra_ref[high] = places.astype(jnp.bfloat16)
        most = jnp.maximum(most, jnp.sum(picked, axis=1, keepdims=True) * 0.5 - room)
    for high in range(levels - wide):
        extra_ref[high] = jnp.where(k < rank, extra_ref[high].astype(f32), most).astype(jnp.bfloat16)


def tables(skeleton, compress, wide, rooms):
    levels, rank = skeleton.shape[1:]
    shape = (levels, 2 * rank, 4 * rank)
    return pl.pallas_call(
        lambda *refs: tables_kernel(wide, rooms, *refs),
        out_shape=[
            jax.ShapeDtypeStruct(shape, jnp.bfloat16),
            jax.ShapeDtypeStruct((levels - wide,) + shape[1:], jnp.bfloat16),
            jax.ShapeDtypeStruct((levels - wide, 2 * rank, 2 * rank), jnp.bfloat16),
        ],
        in_specs=[pl.BlockSpec(memory_space=pltpu.HBM)] * 2,
        out_specs=[pl.BlockSpec(memory_space=pltpu.VMEM)] * 3,
        scratch_shapes=[
            pltpu.VMEM((levels, 1, rank), jnp.int32),
            pltpu.VMEM(compress.shape, jnp.bfloat16),
            pltpu.SemaphoreType.DMA((2,)),
        ],
        compiler_params=pltpu.CompilerParams(vmem_limit_bytes=KERNEL_VMEM),
        cost_estimate=pl.CostEstimate(flops=50_000_000, bytes_accessed=600_000, transcendentals=0),
        name="tables",
    )(skeleton.transpose(1, 0, 2), compress)


def sampled_apart(sampling, traces):
    count, width = traces.shape
    block = count // 8

    def kernel(sampling_ref, rows_ref, coeffs_ref):
        coeffs_ref[...] = sampled_block(sampling_ref[...], rows_ref[...])

    return pl.pallas_call(
        kernel,
        grid=(count // block,),
        out_shape=jax.ShapeDtypeStruct((sampling.shape[1], count), jnp.bfloat16),
        in_specs=[
            pl.BlockSpec(sampling.shape, lambda i: (0, 0)),
            pl.BlockSpec((block, width), lambda i: (i, 0)),
        ],
        out_specs=pl.BlockSpec((sampling.shape[1], block), lambda i: (0, i)),
        compiler_params=pltpu.CompilerParams(vmem_limit_bytes=63 * 1024 * 1024),
        name="sampled_apart",
    )(sampling, traces)


def picked_columns(compress, skeleton):
    rank = skeleton.shape[-1]
    places = lax.broadcasted_iota(jnp.int32, (1, 1, 2 * rank), 2)
    chooser = (skeleton[:, :, None] == places).astype(jnp.bfloat16)
    stacked = jnp.concatenate([compress[:, :, :rank], compress[:, :, rank:]], 1)
    return jnp.einsum(
        "ljk,lki->lji", stacked, chooser, preferred_element_type=jnp.float32
    ).astype(jnp.bfloat16)


def real_form(both):
    rank = both.shape[1] // 2
    turned = jnp.concatenate([-both[:, rank:], both[:, :rank]], 1)
    return jnp.concatenate([both, turned], 2)


def compact_rows(matrix, slot):
    rank = slot.shape[1]
    parts = [
        jnp.dot(slot, half, preferred_element_type=jnp.float32)
        for half in (matrix[:rank], matrix[rank:])
    ]
    return jnp.concatenate(parts, 0).astype(jnp.bfloat16)


def times(matrix, value):
    return jnp.dot(matrix, value, preferred_element_type=jnp.float32).astype(jnp.bfloat16)


def sampled(sampling, traces):
    return jnp.einsum(
        "pc,tp->ct", sampling, traces, preferred_element_type=jnp.float32
    ).astype(jnp.bfloat16)


def evaluated(coeffs, evaluation):
    return jnp.einsum(
        "ct,cp->tp", coeffs, evaluation, preferred_element_type=jnp.float32
    ).astype(jnp.bfloat16)


def after(value, earlier):
    return value if earlier is None else lax.optimization_barrier((value, earlier))[0]


def all_hops():
    low_bits = lax.axis_size("sub").bit_length() - 1
    high_bits = lax.axis_size("bfly").bit_length() - 1
    return [("sub", bit) for bit in range(low_bits)] + [("bfly", bit) for bit in range(high_bits)]


def full_width(traces, sampling, skeleton, compress, evaluation):
    rank = skeleton.shape[-1]
    columns = picked_columns(compress, skeleton)
    full = jnp.concatenate([real_form(columns[..., :rank]), real_form(columns[..., rank:])], 2)
    coeffs = sampled_apart(sampling, traces)
    for level, hop in enumerate(all_hops()):
        partner = from_partner(coeffs, hop)
        coeffs = times(full[level], jnp.concatenate([coeffs, partner], 0))
    return evaluated(coeffs, evaluation)


def local(traces, sampling, skeleton, compress, evaluation):
    hops = all_hops()
    levels = len(hops)
    if (lax.axis_size("sub"), lax.axis_size("bfly")) != (2, 4):
        return full_width(traces, sampling[0], skeleton[0], compress[0], evaluation[0])
    wide = lax.axis_size("sub").bit_length() - 1
    rank = skeleton.shape[-1]
    rooms = [rank * share // 16 for share in ROOM_SIXTEENTHS]
    unit = traces.shape[0] // sum(SHARES)
    pieces = len(SHARES)
    starts = [unit * sum(SHARES[:i]) for i in range(pieces + 1)]
    coeffs = list(early(sampling, traces, starts[: EARLY_PIECES + 1]))
    full, small, extra = tables(after(skeleton, coeffs[0]), compress, wide, rooms)
    sampling, evaluation = sampling[0], evaluation[0]
    most_here = lax.broadcasted_iota(jnp.int32, extra.shape[1:], 1) >= rank

    def compact(level, piece):
        return level >= wide and piece >= FULL_PIECES[level - wide]

    inputs, partners, theirs, done = {}, {}, {}, [None] * pieces
    previous, finished, known = None, None, None
    for level, piece in ORDER:
        if (level, piece) == MAKE:
            waiting = after(sampling, previous)
            coeffs.append(sampled(waiting, traces[starts[pieces - 2] : starts[pieces - 1]]))
            previous = coeffs[-1]
            continue
        if (level, piece) == LOOK:
            known = after(after(partners[0], previous), partners[1])[:, starts[1] :]
            theirs[levels - 1] = known[: rooms[levels - 1 - wide], :rank]
            continue
        count = starts[piece + 1] - starts[piece]
        if level == 0:
            if piece == len(coeffs):
                waiting = after(sampling, previous)
                coeffs.append(sampled(waiting, traces[starts[piece] : starts[piece + 1]]))
            own = coeffs[piece]
            if piece == pieces - 2:
                coeffs.append(sampled(waiting, traces[starts[piece + 1] : starts[piece + 2]]))
        else:
            arrived = after(partners[piece], previous)
            if level == levels:
                arrived = after(arrived, finished)
            elif piece == 0 and level - 1 >= wide:
                known = arrived[:, count:]
                theirs[level - 1] = known[: rooms[level - 1 - wide], :rank]
            value = jnp.concatenate([inputs[piece], arrived[:, :count]], 0)
            matrix = full[level - 1]
            if compact(level - 1, piece):
                value = jnp.pad(value, ((0, full.shape[2] - value.shape[0]), (0, 0)))
                matrix = small[level - 1 - wide]
            if level < levels and compact(level, piece):
                outgoing = times(compact_rows(matrix, theirs[level]), value)
                own = times(after(matrix, outgoing), value)
            else:
                own = outgoing = times(matrix, value)
        if level == levels:
            done[piece] = finished = previous = evaluated(own, evaluation)
            if piece == COUNT_READ:
                most = jnp.maximum(most, after(counted, finished))
            continue
        if level == 0:
            outgoing = after(own, previous) if piece >= pieces - 2 else own
        if piece == 0 and level >= wide:
            block = extra[level - wide]
            if known is not None:
                block = jnp.where(most_here, jnp.maximum(block, known), block)
            so_far = block
            outgoing = jnp.concatenate([outgoing, block], 1)
        inputs[piece] = own
        partners[piece] = from_partner(outgoing, hops[level])
        previous = outgoing
        if (level, piece) == (levels - 1, COUNT_PIECE):
            most = after(jnp.maximum(so_far, known)[:8, rank:], outgoing)
            for hop in hops[: wide - 1]:
                most = jnp.maximum(most, from_partner(most, hop))
            counted = from_partner(most, hops[wide - 1])
    quick = jnp.concatenate(done, 0)
    return lax.cond(
        most[0, 0] > 0,
        lambda: full_width(traces, sampling, skeleton[0], compress[0], evaluation),
        lambda: quick,
    )


def solution(mesh):
    placed = (
        P(("shots", "tr"), ("bfly", "sub")),
        P(("bfly", "sub"), None, None),
        P(("bfly", "sub"), None, None),
        P(("bfly", "sub"), None, None, None),
        P(("bfly", "sub"), None, None),
    )
    return jax.shard_map(
        local,
        mesh=mesh,
        in_specs=placed,
        out_specs=P(("shots", "tr"), ("bfly", "sub")),
        check_vma=False,
    )
```
